32 devices in a mesh: ctx: 16 (over z, y, x), tp: 2 (over core).
Axes of the slice: x: 2, y: 2, z: 4, core: 2. Of those that a mesh axis runs over, the one named last changes fastest.
Arguments:
- tokens: bfloat16 [2048, 1536], P('ctx'), may hold values from -6 to 6
- w_query: bfloat16 [1536, 1536], P(None, 'tp'), may hold values from -0.15625 to 0.15625
- w_key: bfloat16 [1536, 512], P(None, 'tp'), may hold values from -0.15625 to 0.15625
- w_value: bfloat16 [1536, 512], P(None, 'tp'), may hold values from -0.15625 to 0.15625
- w_output: bfloat16 [1536, 1536], P(None, 'tp'), may hold values from -0.625 to 0.625
- w_gate: bfloat16 [1536, 6912], P(None, 'tp'), may hold values from -0.15625 to 0.15625
- w_up: bfloat16 [1536, 6912], P(None, 'tp'), may hold values from -0.15625 to 0.15625
- w_down: bfloat16 [1536, 6912], P(None, 'tp'), may hold values from -0.078125 to 0.078125
- attn_gain: float32 [1536], replicated, may hold values from 0.1 to 1.9
- mlp_gain: float32 [1536], replicated, may hold values from 0.1 to 1.9
- query_gain: float32 [64], replicated, may hold values from 0.1 to 1.9
- key_gain: float32 [64], replicated, may hold values from 0.1 to 1.9
- segments: int32 [2048], replicated, may hold values from 0 to 20, as said below
- positions: int32 [2048], P('ctx'), may hold values from 0 to 511, as said below
- cotangent: bfloat16 [2048, 1536], P('ctx'), may hold values from -6 to 6
Outputs:
- output: bfloat16 [2048, 1536], P('ctx')
- grad_tokens: bfloat16 [2048, 1536], P('ctx')
- grad_w_query: float32 [1536, 1536], P('ctx', 'tp')
- grad_w_key: float32 [1536, 512], P('ctx', 'tp')
- grad_w_value: float32 [1536, 512], P('ctx', 'tp')
- grad_w_output: float32 [1536, 1536], P('ctx', 'tp')
- grad_w_gate: float32 [1536, 6912], P('ctx', 'tp')
- grad_w_up: float32 [1536, 6912], P('ctx', 'tp')
- grad_w_down: float32 [1536, 6912], P('ctx', 'tp')
- grad_attn_gain: float32 [1536], replicated
- grad_mlp_gain: float32 [1536], replicated
- grad_query_gain: float32 [64], replicated
- grad_key_gain: float32 [64], replicated
The draws below stay inside these ranges and needn't reach their ends.
Inputs may be any that keep to these rules, and one draw needn't show every extreme that they name: `segments`: within each sequence (in place order) documents follow one another and fill it; each has at most 512 tokens, all but the last of a sequence 51 or more; segment numbers count a sequence's documents from 0 in place order. In every draw one sequence begins with a document of exactly 512 tokens, and another holds documents numbered up to the stated most. `positions`: each token's place within its document, counted from 0, consistent with segments.
All inputs are finite; a program needn't handle non-finite values.
Results may differ from the reference program's by a relative error of at most 0.02.
Values may be sent and summed in bfloat16 or wider, within the bound.
No kernel may reach another device: no remote copies, remote signals or barrier semaphores. Data moves between devices by JAX's collectives and lax.ppermute only.
A program may use at most 448 MiB of HBM per device.

```python
import math
import jax
import jax.numpy as jnp
from jax import lax

D = 1536
HEADS = 24
KV_HEADS = 8
HD = 64
FF = 6912
BLK = 32
SEQS = 2
PAIRS = 16
SEQ_LEN = 1024
TOKENS = 2048
DOC_MAX = 512
DOC_MIN = 51


def device_order(values):
    pair_count = SEQ_LEN // (2 * BLK)
    blocks = values.reshape(SEQS, 2 * pair_count, BLK)
    lower = blocks[:, :pair_count]
    upper = jnp.flip(blocks[:, pair_count:], axis=1)
    paired = jnp.stack([lower, upper], axis=2)
    return jnp.transpose(paired, (1, 0, 2, 3)).reshape(-1)


def document_tables(key):
    candidates = SEQ_LEN // DOC_MIN + 1
    lengths = jax.random.randint(jax.random.fold_in(key, 11), (SEQS, candidates), DOC_MIN, DOC_MAX + 1, dtype=jnp.int32)
    chosen = jax.random.randint(jax.random.fold_in(key, 12), (), 0, SEQS, dtype=jnp.int32)
    step_on = jax.random.randint(jax.random.fold_in(key, 13), (), 1, SEQS, dtype=jnp.int32)
    crowded = (chosen + step_on) % SEQS
    seq_ids = jnp.arange(SEQS, dtype=jnp.int32)[:, None]
    first_doc = (seq_ids == chosen) & (jnp.arange(candidates, dtype=jnp.int32)[None, :] == 0)
    lengths = jnp.where(first_doc, DOC_MAX, lengths)
    lengths = jnp.where(seq_ids == crowded, DOC_MIN, lengths)
    doc_ends = jnp.cumsum(lengths, axis=1)
    places = jnp.arange(SEQ_LEN, dtype=jnp.int32)
    passed = doc_ends[:, None, :] <= places[None, :, None]
    segment = jnp.sum(passed.astype(jnp.int32), axis=-1)
    starts = jnp.max(jnp.where(passed, doc_ends[:, None, :], 0), axis=-1)
    position = places[None, :] - starts
    return (device_order(segment), device_order(position))


def draw_segments(key, part):
    return document_tables(key)[0]


def draw_positions(key, part):
    return document_tables(key)[1]


def steps_of(key, shape, cuts, smallest, largest):
    level = 1.0
    for dim, parts in cuts:
        steps = jax.random.uniform(jax.random.fold_in(jax.random.fold_in(key, 6), dim), (parts,), jnp.float32, smallest / len(cuts), largest / len(cuts))
        level = level * jnp.repeat(jnp.exp(steps), shape[dim] // parts).reshape((-1,) + (1,) * (len(shape) - 1 - dim))
    return level


def gaussian(stream_key, extent, spread, bound, shards=(), kind=jnp.bfloat16):
    values = jax.random.normal(stream_key, extent, jnp.float32) * spread
    if len(shards) > 0:
        values = steps_of(stream_key, extent, shards, -0.22, 0.18) * values
    return jnp.clip(values, min=-bound, max=bound).astype(kind)


def setup_inputs(seed: int = 0) -> dict:
    streams_of = jax.random.split(jax.random.key(seed), 16)
    tokens = gaussian(streams_of[0], (TOKENS, D), 1.0, 6.0, ((0, 16),))
    w_query = gaussian(streams_of[1], (D, HEADS * HD), D ** -0.5, 0.15625, ((1, 2),))
    w_key = gaussian(streams_of[2], (D, KV_HEADS * HD), D ** -0.5, 0.15625, ((1, 2),))
    w_value = gaussian(streams_of[3], (D, KV_HEADS * HD), D ** -0.5, 0.15625, ((1, 2),))
    w_output = gaussian(streams_of[4], (D, HEADS * HD), (HEADS * HD // 16) ** -0.5, 0.625, ((1, 2),))
    w_gate = gaussian(streams_of[5], (D, FF), D ** -0.5, 0.15625, ((1, 2),))
    w_up = gaussian(streams_of[6], (D, FF), D ** -0.5, 0.15625, ((1, 2),))
    w_down = gaussian(streams_of[7], (D, FF), FF ** -0.5, 0.078125, ((1, 2),))
    attn_gain = jnp.clip(1.0 + 0.18 * jax.random.normal(streams_of[8], (D,), jnp.float32), 0.1, 1.9)
    mlp_gain = jnp.clip(1.0 + 0.18 * jax.random.normal(streams_of[9], (D,), jnp.float32), 0.1, 1.9)
    query_gain = jnp.clip(1.0 + 0.18 * jax.random.normal(streams_of[10], (HD,), jnp.float32), 0.1, 1.9)
    key_gain = jnp.clip(1.0 + 0.18 * jax.random.normal(streams_of[11], (HD,), jnp.float32), 0.1, 1.9)
    segments = draw_segments(jax.random.fold_in(streams_of[15], 71), 0)
    positions = draw_positions(jax.random.fold_in(streams_of[15], 71), 0)
    cotangent = gaussian(streams_of[14], (TOKENS, D), 1.0, 6.0, ((0, 16),))
    return {"tokens": tokens, "w_query": w_query, "w_key": w_key, "w_value": w_value, "w_output": w_output, "w_gate": w_gate, "w_up": w_up, "w_down": w_down, "attn_gain": attn_gain, "mlp_gain": mlp_gain, "query_gain": query_gain, "key_gain": key_gain, "segments": segments, "positions": positions, "cotangent": cotangent}


@jax.custom_vjp
def low(v):
    return lax.optimization_barrier(v.astype(jnp.bfloat16)).astype(jnp.float32)

@jax.custom_vjp
def low_back(v):
    return v

def low_keep(v):
    return (low(v), None)

def low_pass(kept, grad):
    return (grad,)

def back_keep(v):
    return (v, None)

def back_low(kept, grad):
    return (low(grad),)
low.defvjp(low_keep, low_pass)
low_back.defvjp(back_keep, back_low)
EPSILON = 1e-05
ROPE_BASE = 1000000.0
MASKED = -1e+30
PRECISE = lax.Precision.HIGHEST

def matmul(left_side, right_side):
    return jnp.dot(left_side, right_side, precision=PRECISE, preferred_element_type=jnp.float32)

def norm_rows(values, gain):
    factor = lax.rsqrt(lax.optimization_barrier(jnp.mean(values * values, axis=-1, keepdims=True)) + EPSILON)
    return values * factor * gain

def rotate(values, positions):
    head_width = values.shape[-1]
    half_width = head_width // 2
    freqs = ROPE_BASE ** (-2.0 * jnp.arange(half_width, dtype=jnp.float32) / head_width)
    angles = positions.astype(jnp.float32)[:, None] * freqs[None, :]
    cosine = jnp.cos(angles)[:, None, :]
    sine = jnp.sin(angles)[:, None, :]
    first_half = values[..., :half_width]
    second_half = values[..., half_width:]
    return jnp.concatenate([first_half * cosine - second_half * sine, second_half * cosine + first_half * sine], axis=-1)

def to_sequences(values):
    trailing = values.shape[1:]
    blocks = values.reshape((PAIRS, SEQS, 2, BLK) + trailing)
    lower = blocks[:, :, 0]
    upper = jnp.flip(blocks[:, :, 1], axis=0)
    joined = jnp.concatenate([lower, upper], axis=0)
    joined = jnp.moveaxis(joined, 1, 0)
    return joined.reshape((SEQS, 2 * PAIRS * BLK) + trailing)

def from_sequences(values):
    trailing = values.shape[2:]
    blocks = jnp.moveaxis(values.reshape((SEQS, 2 * PAIRS, BLK) + trailing), 0, 1)
    lower = blocks[:PAIRS]
    upper = jnp.flip(blocks[PAIRS:], axis=0)
    joined = jnp.stack([lower, upper], axis=2)
    return joined.reshape((PAIRS * SEQS * 2 * BLK,) + trailing)

def attend_sequence(queries, keys_rot, values_low, segment_ids):
    length = queries.shape[0]
    block_rows = math.gcd(512, length)
    group_size = HEADS // KV_HEADS
    places = jnp.arange(length, dtype=jnp.int32)

    def one_block(block_index):
        begin = (block_index * block_rows).astype(jnp.int32)
        query_block = lax.dynamic_slice_in_dim(queries, begin, block_rows, 0).reshape(block_rows, KV_HEADS, group_size, HD)
        query_place = begin + jnp.arange(block_rows, dtype=jnp.int32)
        query_seg = lax.dynamic_slice_in_dim(segment_ids, begin, block_rows, 0)
        scores = jnp.einsum('qkgd,tkd->kgqt', query_block, keys_rot, precision=PRECISE) * HD ** (-0.5)
        scores = low_back(scores)
        visible = (query_seg[:, None] == segment_ids[None, :]) & (places[None, :] <= query_place[:, None])
        scores = jnp.where(visible, scores, MASKED)
        weights = low(jax.nn.softmax(scores, axis=-1))
        mixed = jnp.einsum('kgqt,tkd->qkgd', weights, values_low, precision=PRECISE)
        return mixed.reshape(block_rows, HEADS * HD)
    blocks_out = lax.map(jax.checkpoint(one_block), jnp.arange(length // block_rows, dtype=jnp.int32))
    return blocks_out.reshape(length, HEADS * HD)

def attention(queries, keys_rot, values_low, segments):

    def one_sequence(packed):
        return attend_sequence(packed[0], packed[1], packed[2], packed[3])
    packed_all = (to_sequences(queries), to_sequences(keys_rot), to_sequences(values_low), to_sequences(segments))
    result = lax.map(jax.checkpoint(one_sequence), packed_all)
    return from_sequences(result)

def forward(hidden_in, w_query, w_key, w_value, w_output, w_gate, w_up, w_down, attn_gain, mlp_gain, query_gain, key_gain, segments, positions):
    row_total = hidden_in.shape[0]
    input_low = low(norm_rows(hidden_in, attn_gain))
    query_raw = low_back(matmul(input_low, w_query)).reshape(row_total, HEADS, HD)
    queries = low(rotate(norm_rows(query_raw, query_gain), positions))
    key_raw = low_back(matmul(input_low, w_key)).reshape(row_total, KV_HEADS, HD)
    keys_rot = low(rotate(norm_rows(key_raw, key_gain), positions))
    values_low = low_back(low(matmul(input_low, w_value))).reshape(row_total, KV_HEADS, HD)
    attended = low_back(low(attention(queries, keys_rot, values_low, segments)))
    middle = hidden_in + low_back(matmul(attended, w_output.T))
    mlp_low = low(norm_rows(middle, mlp_gain))
    gate_pre = low_back(matmul(mlp_low, w_gate))
    up_pre = low_back(matmul(mlp_low, w_up))
    activation = low(jax.nn.silu(gate_pre) * up_pre)
    return middle + matmul(activation, w_down.T)

def reference(tokens, w_query, w_key, w_value, w_output, w_gate, w_up, w_down, attn_gain, mlp_gain, query_gain, key_gain, segments, positions, cotangent):
    floats = [member.astype(jnp.float32) for member in (tokens, w_query, w_key, w_value, w_output, w_gate, w_up, w_down, attn_gain, mlp_gain, query_gain, key_gain)]

    def forward_only(*arrays):
        return forward(*arrays, segments, positions)
    output, pull_back = jax.vjp(forward_only, *floats)
    grads = pull_back(cotangent.astype(jnp.float32))
    return (output.astype(jnp.bfloat16), grads[0].astype(jnp.bfloat16), grads[1], grads[2], grads[3], grads[4], grads[5], grads[6], grads[7], grads[8], grads[9], grads[10], grads[11])
```

```python
import functools

import jax
import jax.numpy as jnp
from jax import lax
from jax.experimental import pallas as pl
from jax.experimental.pallas import tpu as pltpu
from jax.sharding import PartitionSpec as P

BLK = 32
SEQS = 2
EPSILON = 1e-05
ROPE_BASE = 1000000.0
MASKED = -1e30
F32 = jnp.float32
BF16 = jnp.bfloat16
VMEM_LIMIT = 56 * 1024 * 1024


def dot(left, right):
    return jnp.dot(left, right, preferred_element_type=F32)


def contract_last(left, right):
    return lax.dot_general(left, right, (((1,), (1,)), ((), ())), preferred_element_type=F32)


def permutes(count):
    nz = count // 4

    def shift(step):
        return [(i, ((i // 4 + step) % nz) * 4 + i % 4) for i in range(count)]

    flips = {j: [(i, i ^ j) for i in range(count)] for j in (1, 2, 3)}
    return nz, shift, flips


def send(value, pairs):
    return lax.ppermute(value, "ctx", pairs)


def swap_cores(value):
    return lax.ppermute(value, "tp", [(0, 1), (1, 0)])


def core_sum(part):
    low = lax.reduce_precision(part, exponent_bits=8, mantissa_bits=7)
    return low + swap_cores(low.astype(BF16)).astype(F32)


def relative_owner(ctx_index, count, j, step):
    nz = count // 4
    z = (ctx_index // 4 - step + nz) % nz
    return z * 4 + ((ctx_index % 4) ^ j)


def relative_rows(array, ctx_index, count, j):
    rows = array.shape[0] // count
    return jnp.concatenate(
        [
            lax.dynamic_slice_in_dim(array, relative_owner(ctx_index, count, j, s) * rows, rows, 0)
            for s in range(count // 4)
        ],
        axis=0,
    )


def gather_all(block, count):
    nz, shift, flips = permutes(count)
    near = [send(block, flips[j]) for j in (1, 2, 3)]
    column = jnp.concatenate([send(block, shift(s)) for s in range(1, nz)], axis=0)
    far = [send(column, flips[j]) for j in (1, 2, 3)]
    pieces = [block, column]
    for a, b in zip(near, far):
        pieces += [a, b]
    return jnp.concatenate(pieces, axis=0)


def gather_plane(block, count):
    nz, shift, flips = permutes(count)
    near = send(block, flips[2])
    column = jnp.concatenate([send(block, shift(s)) for s in range(1, nz)], axis=0)
    far = send(column, flips[2])
    return jnp.concatenate([block, near, column, far], axis=0)


def scatter_sum(parts, count):
    nz, shift, flips = permutes(count)
    total = parts[0].astype(F32)
    for j in (1, 2, 3):
        total = total + send(parts[j], flips[j]).astype(F32)
    low = total.astype(BF16).reshape(nz, -1, parts[0].shape[1])
    result = low[0].astype(F32)
    for s in range(1, nz):
        result = result + send(low[s], shift(nz - s)).astype(F32)
    return result


def sum_everywhere(value, count):
    value = value + swap_cores(value)
    bit = 1
    while bit < count:
        value = value + send(value, [(i, i ^ bit) for i in range(count)])
        bit *= 2
    return value


def cost(flops, bytes_accessed, transcendentals=0):
    return pl.CostEstimate(
        flops=int(flops), bytes_accessed=int(bytes_accessed), transcendentals=int(transcendentals)
    )


def mask_bias(seg_q, place_q, seg_k, place_k):
    return jnp.where((seg_k == seg_q) & (place_k <= place_q), 0.0, MASKED)


def attention_forward_kernel(q_ref, kv_ref, sq_ref, pq_ref, sk_ref, pk_ref, o_ref, lse_ref):
    keys = kv_ref.shape[0] * kv_ref.shape[2]
    width = kv_ref.shape[3] // 2
    heads = q_ref.shape[1]
    head = width // heads
    k = kv_ref[:, 0, :, :width].reshape(keys, width)
    v_t = kv_ref[:, 0, :, width:].reshape(keys, width).T
    bias = mask_bias(sq_ref[0], pq_ref[...], sk_ref[0], pk_ref[...])
    for h in range(heads):
        s = contract_last(k, q_ref[0, h]) + bias
        top = jnp.max(s, axis=0, keepdims=True)
        p = jnp.exp(s - top)
        total = jnp.sum(p, axis=0, keepdims=True)
        o = dot(v_t[h * head : (h + 1) * head], p.astype(BF16))
        o_ref[0, h] = o / total
        lse_ref[0, h] = top + jnp.log(total)


def attention_backward_kernel(
    q_ref, do_ref, kv_ref, lse_ref, sq_ref, pq_ref, sk_ref, pk_ref, dq_ref, dkv_ref
):
    count, _, rows, both = kv_ref.shape
    keys = count * rows
    width = both // 2
    heads = q_ref.shape[1]
    head = width // heads
    k = kv_ref[:, 0, :, :width].reshape(keys, width)
    v = kv_ref[:, 0, :, width:].reshape(keys, width)
    k_t = k.T
    bias = mask_bias(sq_ref[0], pq_ref[...], sk_ref[0], pk_ref[...])
    dk = jnp.zeros((keys, width), F32)
    dv = jnp.zeros((keys, width), F32)
    for h in range(heads):
        q = q_ref[0, h]
        do = do_ref[0, h]
        p = jnp.exp(contract_last(k, q) + (bias - lse_ref[0, h]))
        dp = contract_last(v, do)
        delta = jnp.sum(p * dp, axis=0, keepdims=True)
        ds = (p * (dp - delta)).astype(BF16)
        dv = dv + dot(p.astype(BF16), do)
        dk = dk + dot(ds, q)
        dq_ref[0, h] = dot(k_t[h * head : (h + 1) * head], ds)
    dkv_ref[:, 0, :, :width] = dk.astype(BF16).reshape(count, rows, width)
    dkv_ref[:, 0, :, width:] = dv.astype(BF16).reshape(count, rows, width)


def whole_block(array):
    return pl.BlockSpec(array.shape, lambda *_: (0,) * array.ndim)


def seq_block(array, dim=0):
    shape = tuple(1 if d == dim else n for d, n in enumerate(array.shape))
    return pl.BlockSpec(shape, lambda s: tuple(s if d == dim else 0 for d in range(array.ndim)))


def attention_forward(q_wide, kv, seg_q, place_q, seg_k, place_k):
    seqs, heads, lanes, width = q_wide.shape
    keys = kv.shape[0] * kv.shape[2]
    head = width // heads
    out_shape = (
        jax.ShapeDtypeStruct((seqs, heads, head, lanes), F32),
        jax.ShapeDtypeStruct((seqs, heads, 1, lanes), F32),
    )
    work = seqs * heads * keys * lanes
    return pl.pallas_call(
        attention_forward_kernel,
        grid=(seqs,),
        in_specs=[
            seq_block(q_wide),
            seq_block(kv, 1),
            seq_block(seg_q),
            whole_block(place_q),
            seq_block(seg_k),
            whole_block(place_k),
        ],
        out_specs=[seq_block(o) for o in out_shape],
        out_shape=out_shape,
        compiler_params=pltpu.CompilerParams(vmem_limit_bytes=VMEM_LIMIT),
        cost_estimate=cost(4 * work * width, 2 * kv.size, work),
        name="attention_forward",
    )(q_wide, kv, seg_q, place_q, seg_k, place_k)


def attention_backward(q_wide, do_wide, kv, lse, seg_q, place_q, seg_k, place_k):
    seqs, heads, lanes, width = q_wide.shape
    keys = kv.shape[0] * kv.shape[2]
    head = width // heads
    out_shape = (
        jax.ShapeDtypeStruct((seqs, heads, head, lanes), F32),
        jax.ShapeDtypeStruct(kv.shape, BF16),
    )
    work = seqs * heads * keys * lanes
    return pl.pallas_call(
        attention_backward_kernel,
        grid=(seqs,),
        in_specs=[
            seq_block(q_wide),
            seq_block(do_wide),
            seq_block(kv, 1),
            seq_block(lse),
            seq_block(seg_q),
            whole_block(place_q),
            seq_block(seg_k),
            whole_block(place_k),
        ],
        out_specs=[seq_block(out_shape[0]), seq_block(out_shape[1], 1)],
        out_shape=out_shape,
        compiler_params=pltpu.CompilerParams(vmem_limit_bytes=VMEM_LIMIT),
        cost_estimate=cost(10 * work * width, 4 * kv.size, work),
        name="attention_backward",
    )(q_wide, do_wide, kv, lse, seg_q, place_q, seg_k, place_k)


def hidden_terms(h2, g, w_gate, w_up, w_down):
    gate = dot(h2, w_gate)
    up = dot(h2, w_up)
    da = dot(g, w_down)
    sg = jax.nn.sigmoid(gate)
    silu = gate * sg
    act = (silu * up).astype(BF16)
    dgate = (da * up * (sg * (1.0 + gate * (1.0 - sg)))).astype(BF16)
    dup = (da * silu).astype(BF16)
    return act, dgate, dup


def own_mlp_kernel(h2_ref, g_ref, wg_ref, wu_ref, wd_ref, down_ref, dh_ref):
    wg, wu, wd = wg_ref[...], wu_ref[...], wd_ref[...]
    act, dgate, dup = hidden_terms(h2_ref[...], g_ref[...], wg, wu, wd)
    down = contract_last(act, wd)
    dh = contract_last(dgate, wg) + contract_last(dup, wu)

    @pl.when(pl.program_id(0) == 0)
    def _():
        down_ref[...] = down
        dh_ref[...] = dh

    @pl.when(pl.program_id(0) > 0)
    def _():
        down_ref[...] += down
        dh_ref[...] += dh


def own_mlp(h2, g, w_gate, w_up, w_down):
    rows, width = h2.shape
    hidden = w_gate.shape[1]
    tile = next(t for t in (384, 256, 128, hidden) if hidden % t == 0)
    whole = pl.BlockSpec((rows, width), lambda i: (0, 0))
    weight = pl.BlockSpec((width, tile), lambda i: (0, i))
    out = jax.ShapeDtypeStruct((rows, width), F32)
    return pl.pallas_call(
        own_mlp_kernel,
        grid=(hidden // tile,),
        in_specs=[whole, whole, weight, weight, weight],
        out_specs=[whole, whole],
        out_shape=(out, out),
        compiler_params=pltpu.CompilerParams(vmem_limit_bytes=VMEM_LIMIT),
        cost_estimate=cost(12 * rows * width * hidden, 6 * width * hidden, rows * hidden),
        name="own_mlp",
    )(h2, g, w_gate, w_up, w_down)


def bulk_mlp_kernel(
    h2_ref, g_ref, h2c_ref, gc_ref, wg_ref, wu_ref, wd_ref, *rest, row_tile
):
    own_refs, other_refs = rest[:3], rest[3:]
    own_rows = own_refs[0].shape[0]
    tokens = h2_ref.shape[0]
    wg, wu, wd = wg_ref[...], wu_ref[...], wd_ref[...]
    totals = None
    for begin in range(0, tokens, row_tile):
        rows = slice(begin, begin + row_tile)
        act, dgate, dup = hidden_terms(h2_ref[rows], g_ref[rows], wg, wu, wd)
        h2c, gc = h2c_ref[:, rows], gc_ref[:, rows]
        terms = [dot(h2c, dgate), dot(h2c, dup), dot(gc, act)]
        totals = terms if totals is None else [a + b for a, b in zip(totals, terms)]
    for own, other, total in zip(own_refs, other_refs, totals):
        own[...] = total[:own_rows]
        other[...] = total[own_rows:].astype(BF16)


def bulk_mlp(h2, g, h2c, gc, w_gate, w_up, w_down):
    tokens, width = h2.shape
    hidden = w_gate.shape[1]
    pair_rows = h2c.shape[0]
    own_rows = pair_rows // 2
    tile = 512
    whole = pl.BlockSpec((tokens, width), lambda i: (0, 0), pipeline_mode=pl.Buffered(1))
    columns = pl.BlockSpec((pair_rows, tokens), lambda i: (0, 0), pipeline_mode=pl.Buffered(1))
    weight = pl.BlockSpec((width, tile), lambda i: (0, i))
    result = pl.BlockSpec((own_rows, tile), lambda i: (0, i))
    return pl.pallas_call(
        functools.partial(bulk_mlp_kernel, row_tile=min(tokens, 1024)),
        grid=(pl.cdiv(hidden, tile),),
        in_specs=[whole, whole, columns, columns, weight, weight, weight],
        out_specs=[result] * 6,
        out_shape=[jax.ShapeDtypeStruct((own_rows, hidden), F32)] * 3
        + [jax.ShapeDtypeStruct((own_rows, hidden), BF16)] * 3,
        compiler_params=pltpu.CompilerParams(vmem_limit_bytes=VMEM_LIMIT),
        cost_estimate=cost(
            6 * tokens * (width + pair_rows) * hidden,
            6 * width * hidden + 4 * tokens * width,
            tokens * hidden,
        ),
        name="bulk_mlp",
    )(h2, g, h2c, gc, w_gate, w_up, w_down)


def norm_rows(values, gain):
    factor = lax.rsqrt(jnp.mean(values * values, axis=-1, keepdims=True) + EPSILON)
    return (values * factor * gain, factor)


def norm_back(values, factor, gain, grad):
    scaled = grad * gain
    inner = jnp.mean(values * scaled, axis=-1, keepdims=True)
    return factor * scaled - values * (factor * factor * factor) * inner


def rotary_tables(positions, head_width):
    half_width = head_width // 2
    freqs = ROPE_BASE ** (-2.0 * jnp.arange(half_width, dtype=F32) / head_width)
    angles = positions.astype(F32)[:, None] * freqs[None, :]
    return (jnp.cos(angles)[:, None, :], jnp.sin(angles)[:, None, :])


def rotate(values, cosine, sine):
    half = values.shape[-1] // 2
    a, b = values[..., :half], values[..., half:]
    return jnp.concatenate([a * cosine - b * sine, b * cosine + a * sine], axis=-1)


def rotate_back(grad, cosine, sine):
    return rotate(grad, cosine, -sine)


def block_place(half_index, device_index, offset, pair_count):
    return (
        jnp.where(half_index == 0, device_index, 2 * pair_count - 1 - device_index) * BLK + offset
    )


def widen(values, seqs, kv_heads, group):
    rows, width = values.shape
    tokens = rows // seqs
    head = width // (kv_heads * group)
    parts = values.reshape(seqs, tokens, kv_heads, group, head).transpose(0, 2, 3, 1, 4)
    parts = parts.reshape(seqs, kv_heads, group * tokens, 1, head)
    eye = jnp.eye(kv_heads, dtype=values.dtype).reshape(1, kv_heads, 1, kv_heads, 1)
    return (parts * eye).reshape(seqs, kv_heads, group * tokens, kv_heads * head)


def narrow(values, group):
    seqs, kv_heads, head, lanes = values.shape
    tokens = lanes // group
    parts = values.reshape(seqs, kv_heads, head, group, tokens).transpose(0, 4, 1, 3, 2)
    return parts.reshape(seqs * tokens, kv_heads * group * head)


def shards(
    tokens,
    w_query,
    w_key,
    w_value,
    w_output,
    w_gate,
    w_up,
    w_down,
    attn_gain,
    mlp_gain,
    query_gain,
    key_gain,
    segments,
    positions,
    cotangent,
):
    count = lax.axis_size("ctx")
    me = lax.axis_index("ctx")
    core = lax.axis_index("tp")
    nz = count // 4
    _, _, flips = permutes(count)
    head = query_gain.shape[0]
    rows, model = tokens.shape
    q_heads = w_query.shape[1] // head
    kv_heads = w_key.shape[1] // head
    group = q_heads // kv_heads
    pair = rows // SEQS
    kv_width = kv_heads * head
    scale = head ** (-0.5)
    half_rows = rows // 2

    g_half = lax.dynamic_slice_in_dim(cotangent, core * half_rows, half_rows, 0)
    g_plane = gather_plane(g_half, count)
    g_bulk = jnp.concatenate([g_plane, swap_cores(g_plane)], axis=0)

    hidden_in = tokens.astype(F32)
    normed_one, factor_one = norm_rows(hidden_in, attn_gain)
    h1 = normed_one.astype(BF16)
    cosine, sine = rotary_tables(positions, head)
    key_raw = dot(h1, w_key).reshape(rows, kv_heads, head)
    key_normed, key_factor = norm_rows(key_raw, key_gain)
    keys_low = rotate(key_normed, cosine, sine).astype(BF16).reshape(rows, kv_width)
    values_low = dot(h1, w_value).astype(BF16)
    packed = jnp.concatenate([keys_low, values_low], axis=1)
    kv = gather_all(packed, count).reshape(count, SEQS, pair, 2 * kv_width)

    query_raw = dot(h1, w_query).reshape(rows, q_heads, head)
    query_normed, query_factor = norm_rows(query_raw, query_gain)
    queries = (rotate(query_normed, cosine, sine).astype(BF16) * BF16(scale)).reshape(rows, -1)
    q_wide = widen(queries, SEQS, kv_heads, group)

    offsets = jnp.arange(pair, dtype=jnp.int32)
    seg_rows = segments.reshape(count, SEQS * pair)
    owners = [relative_owner(me, count, j, s) for j in range(4) for s in range(nz)]
    seg_k = jnp.concatenate([lax.dynamic_slice_in_dim(seg_rows, o, 1, 0) for o in owners], axis=0)
    seg_k = seg_k.reshape(count, SEQS, pair).transpose(1, 0, 2).reshape(SEQS, count * pair, 1)
    place_k = jnp.concatenate([block_place(offsets // BLK, o, offsets % BLK, count) for o in owners])
    place_k = place_k.reshape(count * pair, 1)
    seg_q = lax.dynamic_slice_in_dim(seg_rows, me, 1, 0).reshape(SEQS, 1, pair)
    seg_q = jnp.tile(seg_q, (1, 1, group))
    place_q = jnp.tile(block_place(offsets // BLK, me, offsets % BLK, count), group)[None, :]

    o_t, lse = attention_forward(q_wide, kv, seg_q, place_q, seg_k, place_k)
    attn_low = narrow(o_t, group).astype(BF16)

    branch = core_sum(contract_last(attn_low, w_output))
    middle = hidden_in + branch
    normed_two, factor_two = norm_rows(middle, mlp_gain)
    h2 = normed_two.astype(BF16)
    h2_half = lax.dynamic_slice_in_dim(h2, core * half_rows, half_rows, 0)
    h2_plane = gather_plane(h2_half, count)
    h2_bulk = jnp.concatenate([h2_plane, swap_cores(h2_plane)], axis=0)

    down_part, dh2_part = own_mlp(h2, cotangent, w_gate, w_up, w_down)
    dh2 = core_sum(dh2_part)
    output = (middle + core_sum(down_part)).astype(BF16)
    mlp_gain_part = jnp.sum(dh2_part * middle * factor_two, axis=0)
    grad_middle = cotangent.astype(F32) + norm_back(middle, factor_two, mlp_gain, dh2)
    dy = grad_middle.astype(BF16)
    do = dot(dy, w_output).astype(BF16)
    do_wide = widen(do, SEQS, kv_heads, group)

    dq_t, dkv_part = attention_backward(
        q_wide, do_wide, kv, lse, seg_q, place_q, seg_k, place_k
    )
    dkv_part = dkv_part.reshape(4, nz * rows, 2 * kv_width)
    dkv = scatter_sum([dkv_part[j] for j in range(4)], count)

    dy_t = dy.T
    dy_rel = [relative_rows(dy_t, me, count, j) for j in range(4)]
    grad_wo = scatter_sum([dot(part, attn_low).astype(BF16) for part in dy_rel], count)

    own_cols = model // count
    other = me ^ 1

    def pair_columns(array):
        mine = lax.dynamic_slice_in_dim(array, me * own_cols, own_cols, 1)
        theirs = lax.dynamic_slice_in_dim(array, other * own_cols, own_cols, 1)
        return jnp.concatenate([mine, theirs], axis=1).T

    bulk = bulk_mlp(
        h2_bulk, g_bulk, pair_columns(h2_bulk), pair_columns(g_bulk), w_gate, w_up, w_down
    )
    mlp_grads = [a + send(b, flips[1]).astype(F32) for a, b in zip(bulk[:3], bulk[3:])]

    grad_q_rows = (narrow(dq_t, group) * scale).reshape(rows, q_heads, head)
    grad_q_normed = rotate_back(grad_q_rows, cosine, sine)
    query_gain_part = jnp.sum(grad_q_normed * query_raw * query_factor, axis=(0, 1))
    dq = (
        norm_back(query_raw, query_factor, query_gain, grad_q_normed)
        .reshape(rows, q_heads * head)
        .astype(BF16)
    )
    h1_t = h1.T
    h1_rel = [relative_rows(h1_t, me, count, j) for j in range(4)]
    grad_wq = scatter_sum([dot(part, dq).astype(BF16) for part in h1_rel], count)

    grad_k_normed = rotate_back(dkv[:, :kv_width].reshape(rows, kv_heads, head), cosine, sine)
    key_gain_part = jnp.sum(grad_k_normed * key_raw * key_factor, axis=(0, 1))
    dk = (
        norm_back(key_raw, key_factor, key_gain, grad_k_normed)
        .reshape(rows, kv_width)
        .astype(BF16)
    )
    dv = dkv[:, kv_width:].astype(BF16)
    dkv_low = jnp.concatenate([dk, dv], axis=1)
    grad_wkv = scatter_sum([dot(part, dkv_low).astype(BF16) for part in h1_rel], count)

    dh1_part = contract_last(dq, w_query) + contract_last(dk, w_key) + contract_last(dv, w_value)
    attn_gain_part = jnp.sum(dh1_part * hidden_in * factor_one, axis=0)
    dh1 = core_sum(dh1_part)
    grad_tokens = (grad_middle + norm_back(hidden_in, factor_one, attn_gain, dh1)).astype(BF16)

    gains = sum_everywhere(
        jnp.concatenate([attn_gain_part, mlp_gain_part, query_gain_part, key_gain_part]), count
    )
    return (
        output,
        grad_tokens,
        grad_wq,
        grad_wkv[:, :kv_width],
        grad_wkv[:, kv_width:],
        grad_wo,
        mlp_grads[0],
        mlp_grads[1],
        mlp_grads[2],
        gains[:model],
        gains[model : 2 * model],
        gains[2 * model : 2 * model + head],
        gains[2 * model + head :],
    )


def solution(mesh):
    rows = P("ctx", None)
    columns = P(None, "tp")
    both = P("ctx", "tp")
    in_specs = (rows,) + (columns,) * 7 + (P(),) * 5 + (P("ctx"), rows)
    out_specs = (rows, rows) + (both,) * 7 + (P(),) * 4
    return jax.shard_map(shards, mesh=mesh, in_specs=in_specs, out_specs=out_specs, check_vma=False)
```

```python
import functools

import jax
import jax.numpy as jnp
from jax import lax
from jax.experimental import pallas as pl
from jax.experimental.pallas import tpu as pltpu
from jax.sharding import PartitionSpec as P

BLK = 32
SEQS = 2
QUAD = 4
EPSILON = 1e-05
ROPE_BASE = 1000000.0
MASKED = -1e30
F32 = jnp.float32
BF16 = jnp.bfloat16
VMEM_LIMIT = 56 * 1024 * 1024


def dot(left, right):
    return jnp.dot(left, right, preferred_element_type=F32)


def contract_last(left, right):
    return lax.dot_general(left, right, (((1,), (1,)), ((), ())), preferred_element_type=F32)


def contract_first(left, right):
    return lax.dot_general(left, right, (((0,), (0,)), ((), ())), preferred_element_type=F32)


def shift_pairs(count, step):
    nz = count // QUAD
    return [(i, ((i // QUAD + step) % nz) * QUAD + i % QUAD) for i in range(count)]


def flip_pairs(count, bits):
    return [(i, i ^ bits) for i in range(count)]


def send(value, pairs):
    return lax.ppermute(value, "ctx", pairs)


def swap_cores(value):
    return lax.ppermute(value, "tp", [(0, 1), (1, 0)])


def gather_group(block, count):
    nz = count // QUAD
    pieces = []
    for step in range(nz):
        pairs = []
        for i, to in shift_pairs(count, step):
            pairs += [(2 * i, 2 * to), (2 * i + 1, 2 * (to ^ 2) + 1)]
        pieces.append(lax.ppermute(block, ("ctx", "tp"), pairs))
    return pieces + [swap_cores(p) for p in pieces]


def sum_everywhere(value, count):
    value = value + swap_cores(value)
    bit = 1
    while bit < count:
        value = value + send(value, flip_pairs(count, bit))
        bit *= 2
    return value


def cost(flops, bytes_accessed, transcendentals=0):
    return pl.CostEstimate(
        flops=int(flops), bytes_accessed=int(bytes_accessed), transcendentals=int(transcendentals)
    )


SCALARS = pl.BlockSpec(memory_space=pltpu.SMEM)


def kernel_call(body, name, args, out_shape, flops=0, scalars=False, scratch=()):
    vmem = pl.BlockSpec(memory_space=pltpu.VMEM)
    bytes_accessed = sum(a.size * a.dtype.itemsize for a in (*args, *out_shape))
    return pl.pallas_call(
        body,
        in_specs=[SCALARS if scalars and i == 0 else vmem for i in range(len(args))],
        out_specs=[vmem] * len(out_shape),
        out_shape=list(out_shape),
        scratch_shapes=list(scratch),
        compiler_params=pltpu.CompilerParams(vmem_limit_bytes=VMEM_LIMIT),
        cost_estimate=cost(flops, bytes_accessed),
        name=name,
    )(*args)


def shape(dims, dtype):
    return jax.ShapeDtypeStruct(dims, dtype)


def row_factor(x):
    return lax.rsqrt(jnp.mean(x * x, axis=-1, keepdims=True) + EPSILON)


def head_means(x, blocks):
    high = x.astype(BF16)
    low = (x - high.astype(F32)).astype(BF16)
    return dot(high, blocks) + dot(low, blocks)


def lanes_of(x):
    return lax.broadcasted_iota(jnp.int32, x.shape, 1)


def partner(x):
    return jnp.where(lanes_of(x) % 64 < 32, pltpu.roll(x, 96, 1), pltpu.roll(x, 32, 1))


def mask_kernel(ids_ref, seg_row_ref, seg_col_ref, bias_ref):
    me = ids_ref[0]
    count = seg_row_ref.shape[0]
    nz = count // QUAD
    tokens = seg_col_ref.shape[2]
    z, m = me // QUAD, me % QUAD

    def place(chip, offset):
        return jnp.where(offset < BLK, chip * BLK, (2 * count - 2 - chip) * BLK) + offset

    row_offset = lax.broadcasted_iota(jnp.int32, (1, tokens), 1)
    col_offset = lax.broadcasted_iota(jnp.int32, (tokens, 1), 0)
    place_q = jnp.concatenate([place(z * QUAD + (m ^ j), row_offset) for j in range(QUAD)], axis=1)
    for seq in range(SEQS):
        seg_q = jnp.concatenate(
            [
                seg_row_ref[pl.ds(z * QUAD + (m ^ j), 1), seq * tokens : (seq + 1) * tokens]
                for j in range(QUAD)
            ],
            axis=1,
        )
        for step in range(nz):
            for j in range(QUAD):
                chip = ((z + nz - step) % nz) * QUAD + (m ^ j)
                seen = (seg_col_ref[chip, seq] == seg_q) & (place(chip, col_offset) <= place_q)
                begin = (step * QUAD + j) * tokens
                bias_ref[seq, begin : begin + tokens, :] = jnp.where(seen, 0.0, MASKED)


def qkv_kernel(ids_ref, own_ref, *refs):
    mine, theirs = refs[:3], refs[3:6]
    gain_ref, w_ref, gains_ref, scale_ref, cos_ref, sin_ref, blocks_ref = refs[6:13]
    h1_ref, raw_ref, q_ref, kv_ref = refs[13:]
    core = ids_ref[1]
    gain = gain_ref[...]

    def put(seq, j, piece):
        x = piece.astype(F32)
        h1_ref[seq, j] = (x * row_factor(x) * gain).astype(BF16)

    put(0, 0, own_ref[0])
    put(1, 0, own_ref[1])
    for j in range(1, QUAD):
        put(core, j, mine[j - 1][...])
        put(1 - core, j, theirs[j - 1][...])
    rows = raw_ref.shape[0]
    raw = dot(h1_ref[...].reshape(rows, -1), w_ref[...])
    raw_ref[...] = raw
    cos, sin, blocks = cos_ref[...], sin_ref[...], blocks_ref[...]
    out = []
    for c in range(3):
        lanes = slice(128 * c, 128 * (c + 1))
        x = raw[:, lanes]
        n = x * lax.rsqrt(head_means(x * x, blocks) + EPSILON) * gains_ref[:, lanes]
        out.append((n * cos + partner(n) * sin) * scale_ref[:, lanes])
    kv_ref[...] = jnp.where(lanes_of(out[0]) < 64, out[0], raw[:, :128]).astype(BF16)
    q_ref[...] = jnp.concatenate(out[1:], axis=1).astype(BF16)


def head_lanes(x, g, upper):
    part = x[:, 128 * (g // 2) : 128 * (g // 2) + 128]
    if (g % 2 == 1) != upper:
        part = pltpu.roll(part, 64, 1)
    keep = (lanes_of(part) >= 64) if upper else (lanes_of(part) < 64)
    return jnp.where(keep, part, 0.0).astype(BF16)


def attention_forward_kernel(q_ref, bias_ref, *refs):
    kv_refs, o_ref, lse_ref = refs[:-2], refs[-2], refs[-1]
    group = lse_ref.shape[1]
    kv = jnp.concatenate([r[...] for r in kv_refs], axis=0)
    v_t = kv.T[64:]
    q = q_ref[...].astype(F32)
    bias = bias_ref[0]
    out = []
    for g in range(group):
        s = contract_last(kv, head_lanes(q, g, False)) + bias
        top = jnp.max(s, axis=0, keepdims=True)
        p = jnp.exp(s - top)
        total = jnp.sum(p, axis=0, keepdims=True)
        out.append(dot(v_t, p.astype(BF16)) / total)
        lse_ref[0, g] = top + jnp.log(total)
    o = jnp.concatenate(out, axis=0).T.astype(BF16)
    o_ref[:, 0] = o.reshape(QUAD, -1, o.shape[1])


def attention_backward_kernel(q_ref, bias_ref, lse_ref, *refs):
    do_refs, kv_refs, dq_ref, dkv_refs = refs[:QUAD], None, None, None
    rest = refs[QUAD:]
    pieces = (len(rest) - 1) // 2
    kv_refs, dq_ref, dkv_refs = rest[:pieces], rest[pieces], rest[pieces + 1 :]
    group = lse_ref.shape[1]
    kv = jnp.concatenate([r[...] for r in kv_refs], axis=0)
    k_t = kv.T[:64]
    q = q_ref[...].astype(F32)
    do = jnp.concatenate([r[0].astype(F32) for r in do_refs], axis=0)
    do = jnp.concatenate([do, jnp.zeros((do.shape[0], 64), F32)], axis=1)
    rows = q.shape[0]
    bias = bias_ref[0]
    total = jnp.zeros(kv.shape, F32)
    dq = []
    for g in range(group):
        both = jnp.concatenate([head_lanes(q, g, False), head_lanes(do, g, True)], axis=0)
        products = contract_last(kv, both)
        p = jnp.exp(products[:, :rows] + (bias - lse_ref[0, g]))
        dp = products[:, rows:]
        delta = jnp.sum(p * dp, axis=0, keepdims=True)
        ds = (p * (dp - delta)).astype(BF16)
        total = total + dot(jnp.concatenate([ds, p.astype(BF16)], axis=1), both)
        dq.append(dot(k_t, ds))
    dq.append(jnp.zeros(dq[0].shape, F32))
    dq_ref[...] = jnp.concatenate(dq, axis=0).T
    for i, ref in enumerate(dkv_refs):
        ref[...] = total[i * rows : (i + 1) * rows].astype(BF16)


def attention_specs(rows, keys, pieces):
    q = pl.BlockSpec((rows, 256), lambda s: (s, 0))
    bias = pl.BlockSpec((1, keys, rows), lambda s: (s, 0, 0))
    kv = [pl.BlockSpec((rows, 128), lambda s: (s, 0))] * pieces
    return q, bias, kv


def attention_forward(q, bias, kv, group):
    seqs, keys, rows = bias.shape
    q_spec, bias_spec, kv_specs = attention_specs(rows, keys, len(kv))
    work = seqs * group * keys * rows
    return pl.pallas_call(
        attention_forward_kernel,
        grid=(seqs,),
        in_specs=[q_spec, bias_spec, *kv_specs],
        out_specs=[
            pl.BlockSpec((QUAD, 1, rows // QUAD, group * 64), lambda s: (0, s, 0, 0)),
            pl.BlockSpec((1, group, 1, rows), lambda s: (s, 0, 0, 0)),
        ],
        out_shape=[
            shape((QUAD, seqs, rows // QUAD, group * 64), BF16),
            shape((seqs, group, 1, rows), F32),
        ],
        compiler_params=pltpu.CompilerParams(vmem_limit_bytes=VMEM_LIMIT),
        cost_estimate=cost(6 * work * 128, 4 * bias.size, work),
        name="attention_forward",
    )(q, bias, *kv)


def attention_backward(q, bias, lse, do, kv):
    seqs, keys, rows = bias.shape
    group = lse.shape[1]
    q_spec, bias_spec, kv_specs = attention_specs(rows, keys, len(kv))
    work = seqs * group * keys * rows
    return pl.pallas_call(
        attention_backward_kernel,
        grid=(seqs,),
        in_specs=[
            q_spec,
            bias_spec,
            pl.BlockSpec((1, group, 1, rows), lambda s: (s, 0, 0, 0)),
            *[pl.BlockSpec((1, rows // QUAD, group * 64), lambda s: (s, 0, 0))] * QUAD,
            *kv_specs,
        ],
        out_specs=[q_spec, *kv_specs],
        out_shape=[shape(q.shape, F32)] + [shape(k.shape, BF16) for k in kv],
        compiler_params=pltpu.CompilerParams(vmem_limit_bytes=VMEM_LIMIT),
        cost_estimate=cost(10 * work * 128, 4 * bias.size, work),
        name="attention_backward",
    )(q, bias, lse, *do, *kv)


def branch_kernel(ids_ref, *refs):
    pieces, w_ref, out_ref, stack_ref = refs[:QUAD], refs[QUAD], refs[QUAD + 1], refs[QUAD + 2]
    m = ids_ref[0] % QUAD
    for j in range(QUAD):
        stack_ref[j] = pieces[j][...]
    attn = jnp.concatenate([stack_ref[m ^ k] for k in range(QUAD)], axis=1)
    out_ref[...] = contract_last(attn, w_ref[...]).astype(BF16)


def middle_kernel(x_ref, a_ref, b_ref, gain_ref, mid_ref, h2_ref):
    mid = x_ref[...].astype(F32) + (a_ref[...].astype(F32) + b_ref[...].astype(F32))
    mid_ref[...] = mid
    h2_ref[...] = (mid * row_factor(mid) * gain_ref[...]).astype(BF16)


def hidden_terms(h2, g, w_gate, w_up, w_down):
    gate = dot(h2, w_gate)
    up = dot(h2, w_up)
    da = dot(g, w_down)
    sg = jax.nn.sigmoid(gate)
    silu = gate * sg
    act = (silu * up).astype(BF16)
    dgate = (da * up * (sg * (1.0 + gate * (1.0 - sg)))).astype(BF16)
    dup = (da * silu).astype(BF16)
    return act, dgate, dup


def own_mlp_kernel(h2_ref, g_ref, wg_ref, wu_ref, wd_ref, down_ref, dh_ref, down_sum, dh_sum):
    step = pl.program_id(0)

    @pl.when(step == 0)
    def _():
        down_sum[...] = jnp.zeros_like(down_sum)
        dh_sum[...] = jnp.zeros_like(dh_sum)

    wg, wu, wd = wg_ref[...], wu_ref[...], wd_ref[...]
    act, dgate, dup = hidden_terms(h2_ref[...], g_ref[...], wg, wu, wd)
    down_sum[...] += contract_last(act, wd)
    dh_sum[...] += contract_last(dgate, wg) + contract_last(dup, wu)

    @pl.when(step == pl.num_programs(0) - 1)
    def _():
        down_ref[...] = down_sum[...].astype(BF16)
        dh_ref[...] = dh_sum[...].astype(BF16)


def own_mlp(h2, g, w_gate, w_up, w_down):
    rows, width = h2.shape
    hidden = w_gate.shape[1]
    tile = next(t for t in (384, 256, 128, hidden) if hidden % t == 0)
    whole = pl.BlockSpec((rows, width), lambda i: (0, 0))
    weight = pl.BlockSpec((width, tile), lambda i: (0, i))
    return pl.pallas_call(
        own_mlp_kernel,
        grid=(hidden // tile,),
        in_specs=[whole, whole, weight, weight, weight],
        out_specs=[whole, whole],
        out_shape=[shape((rows, width), BF16)] * 2,
        scratch_shapes=[pltpu.VMEM((rows, width), F32)] * 2,
        compiler_params=pltpu.CompilerParams(vmem_limit_bytes=VMEM_LIMIT),
        cost_estimate=cost(12 * rows * width * hidden, 6 * width * hidden, rows * hidden),
        name="own_mlp",
    )(h2, g, w_gate, w_up, w_down)


def back_kernel(ids_ref, mid_ref, a_ref, b_ref, g_ref, gain_ref, w_ref, dx_ref, dy_ref, part_ref, *do_refs):
    m = ids_ref[0] % QUAD
    stack_ref, do_refs = do_refs[-1], do_refs[:-1]
    mid = mid_ref[...]
    factor = row_factor(mid)
    dh2 = a_ref[...].astype(F32) + b_ref[...].astype(F32)
    part_ref[...] = jnp.sum(dh2 * mid * factor, axis=0, keepdims=True)
    scaled = dh2 * gain_ref[...]
    inner = jnp.mean(mid * scaled, axis=-1, keepdims=True)
    dx = g_ref[...].astype(F32) + (factor * scaled - mid * (factor * factor * factor) * inner)
    dx_ref[...] = dx
    dy = dx.astype(BF16)
    dy_ref[...] = dy
    do = dot(dy, w_ref[...]).astype(BF16)
    columns = do.shape[1] // QUAD
    for k in range(QUAD):
        stack_ref[m ^ k] = do[:, k * columns : (k + 1) * columns]
    for j in range(QUAD):
        do_refs[j][...] = stack_ref[j]


def norm_rotate_back(grad, raw, gain, cos, sin, blocks):
    normed = grad * cos - partner(grad) * sin
    factor = lax.rsqrt(head_means(raw * raw, blocks) + EPSILON)
    scaled = normed * gain
    inner = head_means(raw * scaled, blocks)
    part = jnp.sum(normed * raw * factor, axis=0, keepdims=True)
    return factor * scaled - raw * (factor * factor * factor) * inner, part


def store_by_owner(ids_ref, total_ref, out_refs):
    nz = len(out_refs)
    z = ids_ref[0] // QUAD
    rows = out_refs[0].shape[0]
    for step, ref in enumerate(out_refs):
        begin = pl.multiple_of(((z + nz - step) % nz) * rows, 8)
        ref[...] = total_ref[pl.ds(begin, rows), :].astype(BF16)


def query_kernel(ids_ref, dq_ref, raw_ref, h1_ref, attn_ref, *refs):
    dy_refs, refs = refs[:QUAD], refs[QUAD:]
    gains_ref, cos_ref, sin_ref, blocks_ref = refs[:4]
    out_ref, part_ref, *w_refs = refs[4:-2]
    total_ref, dy_all = refs[-2:]
    cos, sin, blocks = cos_ref[...], sin_ref[...], blocks_ref[...]
    scale = 64 ** (-0.5)
    for c in range(2):
        lanes = slice(128 * c, 128 * (c + 1))
        raw_lanes = slice(128 * (c + 1), 128 * (c + 2))
        grad, part = norm_rotate_back(
            dq_ref[:, lanes] * scale,
            raw_ref[:, raw_lanes],
            gains_ref[:, raw_lanes],
            cos,
            sin,
            blocks,
        )
        out_ref[:, lanes] = grad.astype(BF16)
        part_ref[:, lanes] = part
    rows = out_ref.shape[0]
    attn = []
    for seq in range(SEQS):
        for j in range(QUAD):
            dy_all[seq, j] = dy_refs[j][seq]
            attn.append(attn_ref[j, seq])
    columns = attn[0].shape[1]
    dy = dy_all[...].reshape(rows, -1)
    grad_wq = contract_first(h1_ref[...].reshape(rows, -1), out_ref[...])
    grad_wo = contract_first(dy, jnp.concatenate(attn, axis=0))
    total_ref[...] = jnp.concatenate([grad_wq[:, :columns], grad_wo], axis=1)
    store_by_owner(ids_ref, total_ref, w_refs)


def key_kernel(ids_ref, raw_ref, h1_ref, dq_ref, gains_ref, cos_ref, sin_ref, blocks_ref, *refs):
    nz = (len(refs) - 2 - QUAD) // 2
    dkv_refs, refs = refs[:nz], refs[nz:]
    part_ref, piece_refs, w_refs, total_ref = refs[0], refs[1 : 1 + QUAD], refs[1 + QUAD : -1], refs[-1]
    dkv = dkv_refs[0][...].astype(F32)
    for ref in dkv_refs[1:]:
        dkv = dkv + ref[...].astype(F32)
    grad, part = norm_rotate_back(
        dkv, raw_ref[:, :128], gains_ref[:, :128], cos_ref[...], sin_ref[...], blocks_ref[...]
    )
    part_ref[...] = part
    low = jnp.where(lanes_of(dkv) < 64, grad, dkv).astype(BF16)
    rows = low.shape[0]
    tokens = rows // (SEQS * QUAD)
    for j in range(QUAD):
        for seq in range(SEQS):
            begin = (seq * QUAD + j) * tokens
            to = slice(seq * tokens, (seq + 1) * tokens)
            piece_refs[j][to, :128] = low[begin : begin + tokens]
            piece_refs[j][to, 128:] = dq_ref[begin : begin + tokens]
    total_ref[...] = contract_first(h1_ref[...].reshape(rows, -1), low)
    store_by_owner(ids_ref, total_ref, w_refs)


def spread_kernel(ids_ref, *refs):
    nz = (len(refs) - QUAD - 1) // 2
    first, second, (own_ref, *out_refs), total_ref = (
        refs[:nz],
        refs[nz : 2 * nz],
        refs[2 * nz : -1],
        refs[-1],
    )
    sums = []
    for group in (first, second):
        total = group[0][...].astype(F32)
        for ref in group[1:]:
            total = total + ref[...].astype(F32)
        sums.append(total)
    total_ref[...] = jnp.concatenate(sums, axis=1)
    m = ids_ref[0] % QUAD
    rows = own_ref.shape[0]
    for j in range(QUAD):
        part = total_ref[pl.ds(pl.multiple_of((m ^ j) * rows, 8), rows), :]
        if j == 0:
            own_ref[...] = part
        else:
            out_refs[j - 1][...] = part.astype(BF16)


def assemble_kernel(ids_ref, own_ref, a_ref, b_ref, c_ref, wq_ref, wk_ref, wv_ref, wo_ref, stack_ref):
    m = ids_ref[0] % QUAD
    stack_ref[0] = own_ref[...]
    for j, ref in enumerate((a_ref, b_ref, c_ref)):
        stack_ref[j + 1] = ref[...].astype(F32)
    parts = [stack_ref[m ^ k] for k in range(QUAD)]
    columns = wq_ref.shape[1] // QUAD
    wq_ref[...] = jnp.concatenate([p[:, :columns] for p in parts], axis=1)
    wo_ref[...] = jnp.concatenate([p[:, columns : 2 * columns] for p in parts], axis=1)
    wk_ref[...] = jnp.concatenate([p[:, 2 * columns : 2 * columns + 64] for p in parts], axis=1)
    wv_ref[...] = jnp.concatenate([p[:, 2 * columns + 64 : 2 * columns + 128] for p in parts], axis=1)


def input_grad_kernel(ids_ref, *refs):
    pieces, (x_ref, wq_ref, wk_ref, wv_ref, out_ref, part_ref, stack_ref) = refs[:QUAD], refs[QUAD:]
    m = ids_ref[0] % QUAD
    for j in range(QUAD):
        stack_ref[j] = pieces[j][...]
    parts = [stack_ref[m ^ k] for k in range(QUAD)]
    columns = wq_ref.shape[1] // QUAD
    dk = jnp.concatenate([p[:, :64] for p in parts], axis=1)
    dv = jnp.concatenate([p[:, 64:128] for p in parts], axis=1)
    dq = jnp.concatenate([p[:, 128 : 128 + columns] for p in parts], axis=1)
    total = (
        contract_last(dq, wq_ref[...])
        + contract_last(dk, wk_ref[...])
        + contract_last(dv, wv_ref[...])
    )
    out_ref[...] = total.astype(BF16)
    x = x_ref[...].astype(F32)
    part_ref[...] = jnp.sum(total * x * row_factor(x), axis=0, keepdims=True)


def tokens_kernel(x_ref, dx_ref, a_ref, b_ref, gain_ref, out_ref):
    x = x_ref[...].astype(F32)
    factor = row_factor(x)
    scaled = (a_ref[...].astype(F32) + b_ref[...].astype(F32)) * gain_ref[...]
    inner = jnp.mean(x * scaled, axis=-1, keepdims=True)
    back = factor * scaled - x * (factor * factor * factor) * inner
    out_ref[...] = (dx_ref[...] + back).astype(BF16)


def output_kernel(mid_ref, a_ref, b_ref, out_ref):
    out_ref[...] = (mid_ref[...] + (a_ref[...].astype(F32) + b_ref[...].astype(F32))).astype(BF16)


def bulk_mlp_kernel(ids_ref, *refs, pieces, row_tile):
    h2_pieces, g_pieces = refs[:pieces], refs[pieces : 2 * pieces]
    wg_ref, wu_ref, wd_ref = refs[2 * pieces : 2 * pieces + 3]
    own_refs, other_refs = refs[2 * pieces + 3 : 2 * pieces + 6], refs[2 * pieces + 6 : 2 * pieces + 9]
    h2_ref, g_ref, h2c_ref, gc_ref, sems = refs[2 * pieces + 9 :]
    rows = h2_pieces[0].shape[0]
    tokens, width = h2_ref.shape
    own_rows = own_refs[0].shape[0]
    pair_rows = 2 * own_rows

    @pl.when(pl.program_id(0) == 0)
    def _():
        copies = []
        for side, (source, target) in enumerate(((h2_pieces, h2_ref), (g_pieces, g_ref))):
            for i in range(pieces):
                copies.append(
                    pltpu.make_async_copy(
                        source[i], target.at[pl.ds(i * rows, rows)], sems.at[side * pieces + i]
                    )
                )
        for copy in copies:
            copy.start()
        me = ids_ref[0]
        row = lax.broadcasted_iota(jnp.int32, (pair_rows, width), 0)
        col = lax.broadcasted_iota(jnp.int32, (pair_rows, width), 1)
        target = jnp.where(row < own_rows, me * own_rows + row, ((me ^ 1) - 1) * own_rows + row)
        chosen = jnp.where(col == target, 1.0, 0.0).astype(BF16)
        for copy in copies:
            copy.wait()
        h2c_ref[...] = contract_last(chosen, h2_ref[...]).astype(BF16)
        gc_ref[...] = contract_last(chosen, g_ref[...]).astype(BF16)

    wg, wu, wd = wg_ref[...], wu_ref[...], wd_ref[...]
    totals = None
    for begin in range(0, tokens, row_tile):
        part = slice(begin, begin + row_tile)
        act, dgate, dup = hidden_terms(h2_ref[part], g_ref[part], wg, wu, wd)
        h2c, gc = h2c_ref[:, part], gc_ref[:, part]
        terms = [dot(h2c, dgate), dot(h2c, dup), dot(gc, act)]
        totals = terms if totals is None else [a + b for a, b in zip(totals, terms)]
    for own, other, total in zip(own_refs, other_refs, totals):
        own[...] = total[:own_rows]
        other[...] = total[own_rows:].astype(BF16)


def bulk_mlp(ids, h2, g, weights, own_rows, begin, end, tile):
    rows, width = h2[0].shape
    pieces = len(h2)
    tokens = pieces * rows
    hidden = weights[0].shape[1]
    out_hidden = min(end * tile, hidden) - begin * tile
    anywhere = pl.BlockSpec(memory_space=pl.ANY)
    weight = pl.BlockSpec((width, tile), lambda i: (0, i + begin))
    result = pl.BlockSpec((own_rows, tile), lambda i: (0, i))
    return pl.pallas_call(
        functools.partial(bulk_mlp_kernel, pieces=pieces, row_tile=min(tokens, 1024)),
        grid=(end - begin,),
        in_specs=[SCALARS] + [anywhere] * (2 * pieces) + [weight] * 3,
        out_specs=[result] * 6,
        out_shape=[shape((own_rows, out_hidden), F32)] * 3 + [shape((own_rows, out_hidden), BF16)] * 3,
        scratch_shapes=[pltpu.VMEM((tokens, width), BF16)] * 2
        + [pltpu.VMEM((2 * own_rows, tokens), BF16)] * 2
        + [pltpu.SemaphoreType.DMA((2 * pieces,))],
        compiler_params=pltpu.CompilerParams(vmem_limit_bytes=VMEM_LIMIT),
        cost_estimate=cost(
            6 * tokens * (width + 2 * own_rows) * out_hidden,
            6 * width * out_hidden + 4 * tokens * width,
            tokens * out_hidden,
        ),
        name="bulk_mlp",
    )(ids, *h2, *g, *weights)


def shards(
    tokens,
    w_query,
    w_key,
    w_value,
    w_output,
    w_gate,
    w_up,
    w_down,
    attn_gain,
    mlp_gain,
    query_gain,
    key_gain,
    segments,
    positions,
    cotangent,
):
    count = lax.axis_size("ctx")
    me = lax.axis_index("ctx")
    core = lax.axis_index("tp")
    nz = count // QUAD
    m = me % QUAD
    head = query_gain.shape[0]
    rows, model = tokens.shape
    q_heads = w_query.shape[1] // head
    kv_heads = w_key.shape[1] // head
    group = q_heads // kv_heads
    pair = rows // SEQS
    quad_rows = QUAD * rows
    columns = group * head
    own_rows = model // count
    flips = [flip_pairs(count, j) for j in range(QUAD)]
    ids = jnp.stack([me, core]).astype(jnp.int32)
    attn_gain_row = attn_gain[None, :]
    mlp_gain_row = mlp_gain[None, :]

    def quad_exchange(pieces):
        return [pieces[0]] + [send(pieces[j], flips[j]) for j in range(1, QUAD)]

    own_tokens = tokens.reshape(SEQS, pair, model)
    half = lax.dynamic_index_in_dim(own_tokens, core, 0, keepdims=False)
    mine = [send(half, flips[j]) for j in range(1, QUAD)]
    theirs = [swap_cores(p) for p in mine]
    quad_positions = [positions] + [send(positions, flips[j]) for j in range(1, QUAD)]
    g_group = gather_group(cotangent, count)

    place = jnp.stack(quad_positions).reshape(QUAD, SEQS, pair).transpose(1, 0, 2).reshape(-1, 1)
    freqs = ROPE_BASE ** (-2.0 * jnp.arange(head // 2, dtype=F32) / head)
    angles = place.astype(F32) * jnp.tile(freqs, 4)[None, :]
    sign = jnp.tile(jnp.repeat(jnp.array([-1.0, 1.0], F32), head // 2), 2)[None, :]
    cos, sin = jnp.cos(angles), jnp.sin(angles) * sign
    lane_head = jnp.arange(2 * head) // head
    blocks = jnp.where(lane_head[:, None] == lane_head[None, :], 1.0 / head, 0.0).astype(BF16)
    ones = jnp.ones((head,), F32)
    head_gains = jnp.concatenate([key_gain, ones] + [query_gain] * group + [ones])[None, :]
    lane_scale = jnp.repeat(jnp.array([1.0] * 2 + [head ** (-0.5)] * (group + 1), F32), head)[None, :]
    w_head = jnp.concatenate(
        [
            lax.dynamic_slice_in_dim(w_key, m * head, head, 1),
            lax.dynamic_slice_in_dim(w_value, m * head, head, 1),
            lax.dynamic_slice_in_dim(w_query, m * columns, columns, 1),
            jnp.zeros((model, head), BF16),
        ],
        axis=1,
    )
    seg_rows = segments.reshape(count, SEQS * pair)
    (bias,) = kernel_call(
        mask_kernel,
        "visible",
        (ids, seg_rows, seg_rows.reshape(count, SEQS, pair, 1)),
        [shape((SEQS, count * pair, QUAD * pair), F32)],
        scalars=True,
    )

    h1, raw, q, kv_own = kernel_call(
        qkv_kernel,
        "query_key_value",
        (
            ids,
            own_tokens,
            *mine,
            *theirs,
            attn_gain_row,
            w_head,
            head_gains,
            lane_scale,
            cos,
            sin,
            blocks,
        ),
        [
            shape((SEQS, QUAD, pair, model), BF16),
            shape((quad_rows, 6 * head), F32),
            shape((quad_rows, 4 * head), BF16),
            shape((quad_rows, 2 * head), BF16),
        ],
        flops=2 * quad_rows * model * 6 * head,
        scalars=True,
    )
    kv = [kv_own] + [send(kv_own, shift_pairs(count, s)) for s in range(1, nz)]
    attn, lse = attention_forward(q, bias, kv, group)
    attn_pieces = quad_exchange([attn[j].reshape(rows, columns) for j in range(QUAD)])
    (branch,) = kernel_call(
        branch_kernel,
        "branch",
        (ids, *attn_pieces, w_output),
        [shape((rows, model), BF16)],
        flops=2 * rows * model * w_output.shape[1],
        scalars=True,
        scratch=[pltpu.VMEM((QUAD, rows, columns), BF16)],
    )
    middle, h2 = kernel_call(
        middle_kernel,
        "middle",
        (tokens, branch, swap_cores(branch), mlp_gain_row),
        [shape((rows, model), F32), shape((rows, model), BF16)],
    )
    h2_group = gather_group(h2, count)

    down, dh2 = own_mlp(h2, cotangent, w_gate, w_up, w_down)
    grad_middle, dy, mlp_gain_part, *do = kernel_call(
        back_kernel,
        "back",
        (ids, middle, dh2, swap_cores(dh2), cotangent, mlp_gain_row, w_output),
        [
            shape((rows, model), F32),
            shape((rows, model), BF16),
            shape((1, model), F32),
            *[shape((rows, columns), BF16)] * QUAD,
        ],
        flops=2 * rows * model * w_output.shape[1],
        scalars=True,
        scratch=[pltpu.VMEM((QUAD, rows, columns), BF16)],
    )
    (output,) = kernel_call(
        output_kernel, "output", (middle, down, swap_cores(down)), [shape((rows, model), BF16)]
    )
    do_pieces = [d.reshape(SEQS, pair, columns) for d in quad_exchange(do)]
    dq, *dkv = attention_backward(q, bias, lse, do_pieces, kv)
    dkv = [dkv[0]] + [send(dkv[s], shift_pairs(count, nz - s)) for s in range(1, nz)]

    dy_pieces = [p.reshape(SEQS, pair, model) for p in quad_exchange([dy] * QUAD)]
    z_rows = model // nz
    dq_low, query_part, *w_first = kernel_call(
        query_kernel,
        "query_grad",
        (ids, dq, raw, h1, attn, *dy_pieces, head_gains, cos, sin, blocks),
        [
            shape((quad_rows, 4 * head), BF16),
            shape((1, 4 * head), F32),
            *[shape((z_rows, 2 * columns), BF16)] * nz,
        ],
        flops=2 * quad_rows * model * 7 * head,
        scalars=True,
        scratch=[
            pltpu.VMEM((model, 2 * columns), F32),
            pltpu.VMEM((SEQS, QUAD, pair, model), BF16),
        ],
    )
    w_first = [w_first[0]] + [send(w_first[s], shift_pairs(count, nz - s)) for s in range(1, nz)]

    key_part, *rest = kernel_call(
        key_kernel,
        "key_grad",
        (ids, raw, h1, dq_low, head_gains, cos, sin, blocks, *dkv),
        [
            shape((1, 2 * head), F32),
            *[shape((rows, 6 * head), BF16)] * QUAD,
            *[shape((z_rows, 2 * head), BF16)] * nz,
        ],
        flops=2 * quad_rows * model * 2 * head,
        scalars=True,
        scratch=[pltpu.VMEM((model, 2 * head), F32)],
    )
    grad_pieces, w_second = quad_exchange(rest[:QUAD]), rest[QUAD:]
    w_second = [w_second[0]] + [send(w_second[s], shift_pairs(count, nz - s)) for s in range(1, nz)]
    dh1, attn_gain_part = kernel_call(
        input_grad_kernel,
        "input_grad",
        (ids, *grad_pieces, tokens, w_query, w_key, w_value),
        [shape((rows, model), BF16), shape((1, model), F32)],
        flops=2 * rows * model * (q_heads + 2 * kv_heads) * head,
        scalars=True,
        scratch=[pltpu.VMEM((QUAD, rows, 6 * head), BF16)],
    )
    (grad_tokens,) = kernel_call(
        tokens_kernel,
        "tokens_grad",
        (tokens, grad_middle, dh1, swap_cores(dh1), attn_gain_row),
        [shape((rows, model), BF16)],
    )
    spread = kernel_call(
        spread_kernel,
        "spread",
        (ids, *w_first, *w_second),
        [shape((own_rows, 8 * head), F32)] + [shape((own_rows, 8 * head), BF16)] * (QUAD - 1),
        scalars=True,
        scratch=[pltpu.VMEM((z_rows, 8 * head), F32)],
    )
    grad_wq, grad_wk, grad_wv, grad_wo = kernel_call(
        assemble_kernel,
        "assemble",
        (ids, *quad_exchange(spread)),
        [
            shape((own_rows, q_heads * head), F32),
            shape((own_rows, kv_heads * head), F32),
            shape((own_rows, kv_heads * head), F32),
            shape((own_rows, q_heads * head), F32),
        ],
        scalars=True,
        scratch=[pltpu.VMEM((QUAD, own_rows, 8 * head), F32)],
    )

    tile = 512
    tiles = pl.cdiv(w_gate.shape[1], tile)
    bulk = bulk_mlp(ids, h2_group, g_group, (w_gate, w_up, w_down), own_rows, 0, tiles, tile)
    mlp_grads = [a + send(b, flips[1]).astype(F32) for a, b in zip(bulk[:3], bulk[3:])]

    gains = sum_everywhere(
        jnp.concatenate([attn_gain_part, 0.5 * mlp_gain_part, query_part, key_part], axis=1)[0], count
    )
    query_sum = gains[2 * model : 2 * model + columns].reshape(group, head)
    return (
        output,
        grad_tokens,
        grad_wq,
        grad_wk,
        grad_wv,
        grad_wo,
        mlp_grads[0],
        mlp_grads[1],
        mlp_grads[2],
        gains[:model],
        gains[model : 2 * model],
        jnp.sum(query_sum, axis=0),
        gains[2 * model + 4 * head : 2 * model + 5 * head],
    )


def solution(mesh):
    rows = P("ctx", None)
    columns = P(None, "tp")
    both = P("ctx", "tp")
    in_specs = (rows,) + (columns,) * 7 + (P(),) * 5 + (P("ctx"), rows)
    out_specs = (rows, rows) + (both,) * 7 + (P(),) * 4
    return jax.shard_map(shards, mesh=mesh, in_specs=in_specs, out_specs=out_specs, check_vma=False)
```

```python
import functools

import jax
import jax.numpy as jnp
import numpy as np
from jax import lax
from jax.experimental import pallas as pl
from jax.experimental.pallas import tpu as pltpu
from jax.sharding import PartitionSpec as P

BLK = 32
SEQS = 2
QUAD = 4
EPSILON = 1e-05
ROPE_BASE = 1000000.0
MASKED = -1e30
F32 = jnp.float32
BF16 = jnp.bfloat16
VMEM_LIMIT = 56 * 1024 * 1024


def dot(left, right):
    return jnp.dot(left, right, preferred_element_type=F32)


def contract_last(left, right):
    return lax.dot_general(left, right, (((1,), (1,)), ((), ())), preferred_element_type=F32)


def contract_first(left, right):
    return lax.dot_general(left, right, (((0,), (0,)), ((), ())), preferred_element_type=F32)


def shift_pairs(count, step):
    nz = count // QUAD
    return [(i, ((i // QUAD + step) % nz) * QUAD + i % QUAD) for i in range(count)]


def flip_pairs(count, bits):
    return [(i, i ^ bits) for i in range(count)]


def send(value, pairs):
    return lax.ppermute(value, "ctx", pairs)


def swap_cores(value):
    return lax.ppermute(value, "tp", [(0, 1), (1, 0)])


def core_pairs(count):
    return [pair for i in range(count) for pair in ((2 * i, 2 * i), (2 * i + 1, 2 * (i ^ 2) + 1))]


def gather_column(half, count):
    return [half] + [send(half, shift_pairs(count, s)) for s in range(1, count // QUAD)]


def sum_but_x(value, count):
    value = value + swap_cores(value)
    bit = 2
    while bit < count:
        value = value + send(value, flip_pairs(count, bit))
        bit *= 2
    return value


COST_SCALE = 0.01


def cost(flops, bytes_accessed, transcendentals=0, scale=COST_SCALE):
    return pl.CostEstimate(
        flops=int(flops * scale),
        bytes_accessed=int(bytes_accessed * scale),
        transcendentals=int(transcendentals * scale),
    )


SCALARS = pl.BlockSpec(memory_space=pltpu.SMEM)


ANYWHERE = pl.BlockSpec(memory_space=pl.ANY)


def ordered(body, extra):
    return lambda *refs: body(*refs[extra:])


def kernel_call(
    body, name, args, out_shape, flops=0, scalars=False, scratch=(), after=(), scale=COST_SCALE
):
    vmem = pl.BlockSpec(memory_space=pltpu.VMEM)
    bytes_accessed = sum(a.size * a.dtype.itemsize for a in (*args, *out_shape))
    return pl.pallas_call(
        ordered(body, len(after)),
        in_specs=[ANYWHERE] * len(after)
        + [SCALARS if scalars and i == 0 else vmem for i in range(len(args))],
        out_specs=[vmem] * len(out_shape),
        out_shape=list(out_shape),
        scratch_shapes=list(scratch),
        compiler_params=pltpu.CompilerParams(vmem_limit_bytes=VMEM_LIMIT),
        cost_estimate=cost(flops, bytes_accessed, scale=scale),
        name=name,
    )(*after, *args)


def shape(dims, dtype):
    return jax.ShapeDtypeStruct(dims, dtype)


def pack_kernel(*refs):
    pieces, out_ref = refs[:-1], refs[-1]
    rows = pieces[0].shape[0]
    for i, piece in enumerate(pieces):
        out_ref[i * rows : (i + 1) * rows] = piece[...]


def pack(pieces, after=()):
    rows, width = pieces[0].shape
    out = shape((len(pieces) * rows, width), pieces[0].dtype)
    return kernel_call(pack_kernel, "pack", pieces, [out], after=after)[0]


def touch(value, after):
    return pl.pallas_call(
        lambda *refs: None,
        in_specs=[ANYWHERE] * (1 + len(after)),
        out_specs=ANYWHERE,
        out_shape=shape(value.shape, value.dtype),
        input_output_aliases={0: 0},
        name="touch",
    )(value, *after)


def row_factor(x):
    return lax.rsqrt(jnp.mean(x * x, axis=-1, keepdims=True) + EPSILON)


def head_means(x, blocks):
    high = x.astype(BF16)
    low = (x - high.astype(F32)).astype(BF16)
    return dot(high, blocks) + dot(low, blocks)


def head_blocks():
    row = lax.broadcasted_iota(jnp.int32, (128, 128), 0)
    col = lax.broadcasted_iota(jnp.int32, (128, 128), 1)
    return jnp.where(row // 64 == col // 64, 1.0 / 64, 0.0).astype(BF16)


def row_of(ref):
    return ref[...].reshape(1, -1)


def head_gain_rows(key_ref, query_ref):
    key, query = row_of(key_ref), row_of(query_ref)
    return jnp.concatenate([key, key], axis=1), jnp.concatenate([query, query], axis=1)


def lanes_of(x):
    return lax.broadcasted_iota(jnp.int32, x.shape, 1)


def partner(x):
    return jnp.where(lanes_of(x) % 64 < 32, pltpu.roll(x, 96, 1), pltpu.roll(x, 32, 1))


def mask_kernel(ids_ref, freq_ref, seg_ref, bias_ref, angle_ref):
    me = ids_ref[0]
    count = seg_ref.shape[0]
    nz = count // QUAD
    tokens = seg_ref.shape[1] // SEQS
    z, m = me // QUAD, me % QUAD

    def place(chip, offset):
        return jnp.where(offset < BLK, chip * BLK, (2 * count - 2 - chip) * BLK) + offset

    chips = [((z + nz - step) % nz) * QUAD + (m ^ j) for step in range(nz) for j in range(QUAD)]
    seg_rows = [seg_ref[pl.ds(chip, 1), :].astype(F32) for chip in chips]
    fill = jnp.zeros((128 - count, SEQS * tokens), F32)
    seg_cols = jnp.concatenate([*seg_rows, fill], axis=0).T
    row_offset = lax.broadcasted_iota(jnp.int32, (1, tokens), 1)
    col_offset = lax.broadcasted_iota(jnp.int32, (tokens, 1), 0)
    place_q = jnp.concatenate([place(chip, row_offset) for chip in chips[:QUAD]], axis=1)
    far = 2 * count * BLK
    for seq in range(SEQS):
        of_seq = slice(seq * tokens, (seq + 1) * tokens)
        seg_q = jnp.concatenate([row[:, of_seq] for row in seg_rows[:QUAD]], axis=1)
        first = jnp.full((tokens, QUAD * tokens), far, jnp.int32)
        for i, chip in enumerate(chips):
            place_k = place(chip, col_offset)
            same = seg_cols[of_seq, i : i + 1] == seg_q
            bias_ref[seq, i * tokens : (i + 1) * tokens, :] = jnp.where(
                same & (place_k <= place_q), 0.0, MASKED
            )
            first = jnp.minimum(first, jnp.where(same, place_k, far))
        position = (place_q - jnp.min(first, axis=0, keepdims=True)).astype(F32)
        rows = position.shape[1]
        angle_ref[seq * rows : (seq + 1) * rows, :] = (
            jnp.broadcast_to(position, (128, rows)).T * freq_ref[...]
        )


def qkv_kernel(ids_ref, own_ref, *refs):
    mine, theirs = refs[:3], refs[3:6]
    gain_ref, w_ref, key_gain_ref, query_gain_ref, cos_ref, sin_ref, g_ref = refs[6:13]
    h1_ref, raw_ref, q_ref, kv_ref, copy_ref = refs[13:]
    core = ids_ref[1]
    gain = row_of(gain_ref)
    copy_ref[...] = g_ref[...]

    def put(seq, j, piece):
        x = piece.astype(F32)
        h1_ref[seq, j] = (x * row_factor(x) * gain).astype(BF16)

    put(0, 0, own_ref[0])
    put(1, 0, own_ref[1])
    for j in range(1, QUAD):
        put(core, j, mine[j - 1][...])
        put(1 - core, j, theirs[j - 1][...])
    rows = raw_ref.shape[0]
    raw = dot(h1_ref[...].reshape(rows, -1), w_ref[...])
    raw_ref[...] = raw
    cos, sin, blocks = cos_ref[...], sin_ref[...], head_blocks()
    key_gain, query_gain = head_gain_rows(key_gain_ref, query_gain_ref)
    out = []
    for c in range(3):
        x = raw[:, 128 * c : 128 * (c + 1)]
        gain = key_gain if c == 0 else query_gain * 64 ** (-0.5)
        n = x * lax.rsqrt(head_means(x * x, blocks) + EPSILON) * gain
        out.append(n * cos + partner(n) * sin)
    kv_ref[...] = jnp.where(lanes_of(out[0]) < 64, out[0], raw[:, :128]).astype(BF16)
    q_ref[...] = jnp.concatenate(out[1:], axis=1).astype(BF16)


def head_lanes(x, g, upper):
    part = x[:, 128 * (g // 2) : 128 * (g // 2) + 128]
    if (g % 2 == 1) != upper:
        part = pltpu.roll(part, 64, 1)
    keep = (lanes_of(part) >= 64) if upper else (lanes_of(part) < 64)
    return jnp.where(keep, part, 0.0).astype(BF16)


def attention_forward_kernel(q_ref, bias_ref, *refs):
    kv_refs, o_refs, lse_ref = refs[: -QUAD - 1], refs[-QUAD - 1 : -1], refs[-1]
    group = lse_ref.shape[1]
    kv = jnp.concatenate([r[...] for r in kv_refs], axis=0)
    v_t = kv.T[64:]
    q = q_ref[...].astype(F32)
    bias = bias_ref[0]
    out = []
    for g in range(group):
        s = contract_last(kv, head_lanes(q, g, False)) + bias
        top = jnp.max(s, axis=0, keepdims=True)
        p = jnp.exp(s - top)
        total = jnp.sum(p, axis=0, keepdims=True)
        out.append(dot(v_t, p.astype(BF16)) / total)
        lse_ref[0, g] = top + jnp.log(total)
    o = jnp.concatenate(out, axis=0).T.astype(BF16)
    rows = o.shape[0] // QUAD
    for j in range(QUAD):
        o_refs[j][0] = o[j * rows : (j + 1) * rows]


def attention_backward_kernel(q_ref, bias_ref, lse_ref, *refs):
    do_refs, kv_refs, dq_ref, dkv_refs = refs[:QUAD], None, None, None
    rest = refs[QUAD:]
    pieces = (len(rest) - 1) // 2
    kv_refs, dq_ref, dkv_refs = rest[:pieces], rest[pieces], rest[pieces + 1 :]
    group = lse_ref.shape[1]
    kv = jnp.concatenate([r[...] for r in kv_refs], axis=0)
    k_t = kv.T[:64]
    q = q_ref[...].astype(F32)
    do = jnp.concatenate([r[0].astype(F32) for r in do_refs], axis=0)
    do = jnp.concatenate([do, jnp.zeros((do.shape[0], 64), F32)], axis=1)
    rows = q.shape[0]
    bias = bias_ref[0]
    total = jnp.zeros(kv.shape, F32)
    dq = []
    for g in range(group):
        both = jnp.concatenate([head_lanes(q, g, False), head_lanes(do, g, True)], axis=0)
        products = contract_last(kv, both)
        p = jnp.exp(products[:, :rows] + (bias - lse_ref[0, g]))
        dp = products[:, rows:]
        delta = jnp.sum(p * dp, axis=0, keepdims=True)
        ds = (p * (dp - delta)).astype(BF16)
        total = total + dot(jnp.concatenate([ds, p.astype(BF16)], axis=1), both)
        dq.append(dot(k_t, ds))
    dq.append(jnp.zeros(dq[0].shape, F32))
    dq_ref[...] = jnp.concatenate(dq, axis=0).T
    for i, ref in enumerate(dkv_refs):
        ref[...] = total[i * rows : (i + 1) * rows].astype(BF16)


def attention_specs(rows, keys, pieces):
    q = pl.BlockSpec((rows, 256), lambda s: (s, 0))
    bias = pl.BlockSpec((1, keys, rows), lambda s: (s, 0, 0))
    kv = [pl.BlockSpec((rows, 128), lambda s: (s, 0))] * pieces
    return q, bias, kv


def attention_forward(q, bias, kv, group, after):
    seqs, keys, rows = bias.shape
    q_spec, bias_spec, kv_specs = attention_specs(rows, keys, len(kv))
    work = seqs * group * keys * rows
    return pl.pallas_call(
        ordered(attention_forward_kernel, len(after)),
        grid=(seqs,),
        in_specs=[*[ANYWHERE] * len(after), q_spec, bias_spec, *kv_specs],
        out_specs=[
            *[pl.BlockSpec((1, rows // QUAD, group * 64), lambda s: (s, 0, 0))] * QUAD,
            pl.BlockSpec((1, group, 1, rows), lambda s: (s, 0, 0, 0)),
        ],
        out_shape=[
            *[shape((seqs, rows // QUAD, group * 64), BF16)] * QUAD,
            shape((seqs, group, 1, rows), F32),
        ],
        compiler_params=pltpu.CompilerParams(vmem_limit_bytes=VMEM_LIMIT),
        cost_estimate=cost(6 * work * 128, 4 * bias.size, work),
        name="attention_forward",
    )(*after, q, bias, *kv)


def attention_backward(q, bias, lse, do, kv, after=()):
    seqs, keys, rows = bias.shape
    group = lse.shape[1]
    q_spec, bias_spec, kv_specs = attention_specs(rows, keys, len(kv))
    work = seqs * group * keys * rows
    return pl.pallas_call(
        ordered(attention_backward_kernel, len(after)),
        grid=(seqs,),
        in_specs=[
            *[ANYWHERE] * len(after),
            q_spec,
            bias_spec,
            pl.BlockSpec((1, group, 1, rows), lambda s: (s, 0, 0, 0)),
            *[pl.BlockSpec((1, rows // QUAD, group * 64), lambda s: (s, 0, 0))] * QUAD,
            *kv_specs,
        ],
        out_specs=[q_spec, *kv_specs],
        out_shape=[shape(q.shape, F32)] + [shape(k.shape, BF16) for k in kv],
        compiler_params=pltpu.CompilerParams(vmem_limit_bytes=VMEM_LIMIT),
        cost_estimate=cost(10 * work * 128, 4 * bias.size, work),
        name="attention_backward",
    )(*after, q, bias, lse, *do, *kv)


def put_halves(refs, value):
    rows = refs[0].shape[0]
    for i, ref in enumerate(refs):
        ref[...] = value[i * rows : (i + 1) * rows].astype(ref.dtype)


def sum_halves(refs):
    own = jnp.concatenate([refs[0][...], refs[1][...]], axis=0).astype(F32)
    return own + jnp.concatenate([refs[2][...], refs[3][...]], axis=0).astype(F32)


def branch_kernel(ids_ref, *refs):
    pieces, w_ref, out_refs, stack_ref = refs[:QUAD], refs[QUAD], refs[QUAD + 1 : -1], refs[-1]
    m = ids_ref[0] % QUAD
    for j in range(QUAD):
        stack_ref[j] = pieces[j][...]
    attn = jnp.concatenate([stack_ref[m ^ k] for k in range(QUAD)], axis=1)
    put_halves(out_refs, contract_last(attn, w_ref[...]))


def middle_kernel(ids_ref, x_ref, *refs):
    branch_refs, (gain_ref, mid_ref, h2_ref, half_ref) = refs[:4], refs[4:]
    mid = x_ref[...].astype(F32) + sum_halves(branch_refs)
    mid_ref[...] = mid
    h2 = (mid * row_factor(mid) * row_of(gain_ref)).astype(BF16)
    h2_ref[...] = h2
    rows = half_ref.shape[0]
    half_ref[...] = jnp.where(ids_ref[1] == 0, h2[:rows], h2[rows:])


def hidden_terms(gate, up, da):
    sg = jax.nn.sigmoid(gate)
    silu = gate * sg
    act = (silu * up).astype(BF16)
    dgate = (da * up * (sg + silu * (1.0 - sg))).astype(BF16)
    dup = (da * silu).astype(BF16)
    return act, dgate, dup


def hidden_tile(hidden):
    return next(t for t in (1152, 384, 128, hidden) if hidden % t == 0)


def hidden_call(body, name, args, out_shape, scratch=(), matmuls=1, after=()):
    hidden = max(a.shape[-1] for a in args)
    tile = hidden_tile(hidden)

    def spec(a):
        if a.shape[-1] == hidden:
            return pl.BlockSpec((a.shape[0], tile), lambda i: (0, i))
        return pl.BlockSpec(a.shape, lambda i: (0, 0))

    rows, width = args[0].shape[0], 1536
    return pl.pallas_call(
        ordered(body, len(after)),
        grid=(hidden // tile,),
        in_specs=[ANYWHERE] * len(after) + [spec(a) for a in args],
        out_specs=[spec(o) for o in out_shape],
        out_shape=list(out_shape),
        scratch_shapes=list(scratch),
        compiler_params=pltpu.CompilerParams(vmem_limit_bytes=VMEM_LIMIT),
        cost_estimate=cost(
            4 * matmuls * rows * width * hidden,
            sum(a.size * a.dtype.itemsize for a in (*args, *out_shape)),
        ),
        name=name,
    )(*after, *args)


def accumulate(total_ref, out_refs, term):
    step = pl.program_id(0)

    @pl.when(step == 0)
    def _():
        total_ref[...] = term

    @pl.when(step > 0)
    def _():
        total_ref[...] += term

    @pl.when(step == pl.num_programs(0) - 1)
    def _():
        put_halves(out_refs, total_ref[...].T)


def hidden_grad_kernel(g_ref, wd_ref, da_ref):
    da_ref[...] = dot(g_ref[...], wd_ref[...])


def own_mlp_kernel(
    h2_ref, da_ref, wg_ref, wu_ref, dh_top_ref, dh_ref, act_ref, dgate_ref, dup_ref, total_ref
):
    wg, wu, h2 = wg_ref[...], wu_ref[...], h2_ref[...]
    act, dgate, dup = hidden_terms(dot(h2, wg), dot(h2, wu), da_ref[...])
    act_ref[...] = act
    dgate_ref[...] = dgate
    dup_ref[...] = dup
    accumulate(
        total_ref, (dh_top_ref, dh_ref), contract_last(wg, dgate) + contract_last(wu, dup)
    )


def down_kernel(act_ref, wd_ref, down_ref, total_ref):
    accumulate(total_ref, (down_ref,), contract_last(wd_ref[...], act_ref[...]))


def back_kernel(
    ids_ref, mid_ref, a_ref, b_ref, c_ref, d_ref, g_ref, gain_ref, w_ref, dx_ref, dy_ref, *refs
):
    half_ref, part_ref, do_refs = refs[0], refs[1], refs[2:]
    m = ids_ref[0] % QUAD
    stack_ref, do_refs = do_refs[-1], do_refs[:-1]
    mid = mid_ref[...]
    factor = row_factor(mid)
    dh2 = sum_halves((a_ref, b_ref, c_ref, d_ref))
    part_ref[...] = jnp.sum(dh2 * mid * factor, axis=0, keepdims=True)
    scaled = dh2 * row_of(gain_ref)
    inner = jnp.mean(mid * scaled, axis=-1, keepdims=True)
    dx = g_ref[...].astype(F32) + (factor * scaled - mid * (factor * factor * factor) * inner)
    dx_ref[...] = dx
    dy = dx.astype(BF16)
    dy_ref[...] = dy
    half = half_ref.shape[0]
    half_ref[...] = jnp.where(ids_ref[1] == 0, dy[:half], dy[half:])
    do = dot(dy, w_ref[...]).astype(BF16)
    columns = do.shape[1] // QUAD
    for k in range(QUAD):
        stack_ref[m ^ k] = do[:, k * columns : (k + 1) * columns]
    for j in range(QUAD):
        do_refs[j][...] = stack_ref[j]


def norm_rotate_back(grad, raw, gain, cos, sin, blocks):
    normed = grad * cos - partner(grad) * sin
    factor = lax.rsqrt(head_means(raw * raw, blocks) + EPSILON)
    scaled = normed * gain
    inner = head_means(raw * scaled, blocks)
    part = jnp.sum(normed * raw * factor, axis=0, keepdims=True)
    return factor * scaled - raw * (factor * factor * factor) * inner, part


def head_grad_kernel(ids_ref, dq_ref, raw_ref, h1_ref, *refs):
    attn_refs, dy_ref, mine, theirs, refs = refs[:4], refs[4], refs[5:8], refs[8:11], refs[11:]
    core = ids_ref[1]
    key_gain_ref, query_gain_ref, cos_ref, sin_ref, refs = *refs[:4], refs[4:]
    nz = (len(refs) - QUAD - 3) // 2
    dkv_refs, refs = refs[:nz], refs[nz:]
    part_ref, piece_refs, w_refs = refs[0], refs[1 : 1 + QUAD], refs[1 + QUAD : -2]
    total_ref, dy_all = refs[-2:]
    cos, sin, blocks = cos_ref[...], sin_ref[...], head_blocks()
    key_gain, query_gain = head_gain_rows(key_gain_ref, query_gain_ref)
    dkv = dkv_refs[0][...].astype(F32)
    for ref in dkv_refs[1:]:
        dkv = dkv + ref[...].astype(F32)
    scale = 64 ** (-0.5)
    low = []
    for c in range(3):
        lanes = slice(128 * c, 128 * (c + 1))
        given = dkv if c == 0 else dq_ref[:, 128 * (c - 1) : 128 * c] * scale
        gain = key_gain if c == 0 else query_gain
        grad, part = norm_rotate_back(given, raw_ref[:, lanes], gain, cos, sin, blocks)
        if c == 0:
            grad = jnp.where(lanes_of(grad) < 64, grad, dkv)
        part_ref[:, lanes] = part
        low.append(grad.astype(BF16))
    low = jnp.concatenate(low, axis=1)
    rows = low.shape[0]
    tokens = rows // (SEQS * QUAD)
    attn = []
    for seq in range(SEQS):
        for j in range(QUAD):
            begin = (seq * QUAD + j) * tokens
            piece_refs[j][seq * tokens : (seq + 1) * tokens] = low[begin : begin + tokens]
            if j == 0:
                dy_all[seq, j] = dy_ref[seq]
            attn.append(attn_refs[j][seq])
    for j in range(1, QUAD):
        dy_all[core, j] = mine[j - 1][...]
        dy_all[1 - core, j] = theirs[j - 1][...]
    columns = attn[0].shape[1]
    grad_wqkv = contract_first(h1_ref[...].reshape(rows, -1), low)
    grad_wo = contract_first(dy_all[...].reshape(rows, -1), jnp.concatenate(attn, axis=0))
    total_ref[...] = jnp.concatenate([grad_wqkv[:, : 128 + columns], grad_wo], axis=1)
    z = ids_ref[0] // QUAD
    owned = w_refs[0].shape[0]
    for step, ref in enumerate(w_refs):
        begin = pl.multiple_of(((z + nz - step) % nz) * owned, 8)
        ref[...] = total_ref[pl.ds(begin, owned), :].astype(BF16)


def spread_kernel(ids_ref, *refs):
    nz = len(refs) - QUAD - 1
    terms, (own_ref, *out_refs), total_ref = refs[:nz], refs[nz:-1], refs[-1]
    total = terms[0][...].astype(F32)
    for ref in terms[1:]:
        total = total + ref[...].astype(F32)
    total_ref[...] = total
    m = ids_ref[0] % QUAD
    rows = own_ref.shape[0]
    for j in range(QUAD):
        part = total_ref[pl.ds(pl.multiple_of((m ^ j) * rows, 8), rows), :]
        if j == 0:
            own_ref[...] = part
        else:
            out_refs[j - 1][...] = part.astype(BF16)


def assemble_kernel(ids_ref, own_ref, a_ref, b_ref, c_ref, wq_ref, wk_ref, wv_ref, wo_ref, stack_ref):
    m = ids_ref[0] % QUAD
    stack_ref[0] = own_ref[...]
    for j, ref in enumerate((a_ref, b_ref, c_ref)):
        stack_ref[j + 1] = ref[...].astype(F32)
    parts = [stack_ref[m ^ k] for k in range(QUAD)]
    columns = wq_ref.shape[1] // QUAD
    wk_ref[...] = jnp.concatenate([p[:, :64] for p in parts], axis=1)
    wv_ref[...] = jnp.concatenate([p[:, 64:128] for p in parts], axis=1)
    wq_ref[...] = jnp.concatenate([p[:, 128 : 128 + columns] for p in parts], axis=1)
    wo_ref[...] = jnp.concatenate([p[:, 128 + columns :] for p in parts], axis=1)


def input_grad_kernel(ids_ref, *refs):
    pieces, (x_ref, wq_ref, wk_ref, wv_ref, out_ref, part_ref, stack_ref) = refs[:QUAD], refs[QUAD:]
    m = ids_ref[0] % QUAD
    for j in range(QUAD):
        stack_ref[j] = pieces[j][...]
    parts = [stack_ref[m ^ k] for k in range(QUAD)]
    columns = wq_ref.shape[1] // QUAD
    dk = jnp.concatenate([p[:, :64] for p in parts], axis=1)
    dv = jnp.concatenate([p[:, 64:128] for p in parts], axis=1)
    dq = jnp.concatenate([p[:, 128 : 128 + columns] for p in parts], axis=1)
    total = (
        contract_last(dq, wq_ref[...])
        + contract_last(dk, wk_ref[...])
        + contract_last(dv, wv_ref[...])
    )
    out_ref[...] = total.astype(BF16)
    x = x_ref[...].astype(F32)
    part_ref[...] = jnp.sum(total * x * row_factor(x), axis=0, keepdims=True)


def tokens_kernel(x_ref, dx_ref, a_ref, b_ref, gain_ref, out_ref):
    x = x_ref[...].astype(F32)
    factor = row_factor(x)
    scaled = (a_ref[...].astype(F32) + b_ref[...].astype(F32)) * row_of(gain_ref)
    inner = jnp.mean(x * scaled, axis=-1, keepdims=True)
    back = factor * scaled - x * (factor * factor * factor) * inner
    out_ref[...] = (dx_ref[...] + back).astype(BF16)


def output_kernel(mid_ref, a_ref, b_ref, out_ref):
    out_ref[...] = (mid_ref[...] + (a_ref[...].astype(F32) + b_ref[...].astype(F32))).astype(BF16)


def bulk_mlp_kernel(ids_ref, *refs, pieces, row_tile, first):
    sides, refs = (refs[: pieces[0]], refs[pieces[0] : sum(pieces)]), refs[sum(pieces) :]
    act_ref, dgate_ref, dup_ref, wg_ref, wu_ref, wd_ref, refs = *refs[:6], refs[6:]
    if first:
        own_refs, other_ref, h2c_ref, gc_ref, h2_ref, g_ref, sems = refs[:3], *refs[3:]
    else:
        h2c_ref, gc_ref, own_refs, other_ref, h2_ref, g_ref, sems = *refs[:2], refs[2:5], *refs[5:]
    rows = act_ref.shape[0]
    tokens, width = h2_ref.shape
    own_rows = own_refs[0].shape[0]
    pair_rows = 2 * own_rows

    @pl.when(pl.program_id(0) == 0)
    def _():
        half = rows // 2
        places = pieces[1] // 2
        copies = []

        def copy_rows(source, skip, size, target, begin, sem):
            return pltpu.make_async_copy(
                source.at[pl.ds(skip, size)], target.at[pl.ds(begin, size)], sems.at[sem]
            )

        begin = 0
        for i, source in enumerate(sides[0]):
            skip = half if i in (0, 2) else 0
            copies.append(copy_rows(source, skip, source.shape[0] - skip, h2_ref, begin, i))
            begin += source.shape[0] - skip
        for copy in copies:
            copy.start()
        for core in range(2):

            @pl.when(ids_ref[1] == core)
            def _():
                own_y, other_y = sides[1][:places], sides[1][places : 2 * places]
                if core == 1:
                    own_y, other_y = other_y, own_y
                blocks = [*own_y[1:], *other_y]
                for i, source in enumerate(blocks):
                    for part in range(2):
                        to = (i + part * len(blocks)) * half
                        sem = len(sides[0]) + 2 * i + part
                        copy_rows(source, (core ^ part) * half, half, g_ref, to, sem).start()
                last = len(sides[0]) + 4 * places - 2
                copy_rows(sides[1][-1], 0, rows, g_ref, tokens - rows, last).start()

        for i in range(2 * (2 * places - 1)):
            copies.append(copy_rows(sides[1][0], 0, half, g_ref, 0, len(sides[0]) + i))
        last = len(sides[0]) + 4 * places - 2
        copies.append(copy_rows(sides[1][-1], 0, rows, g_ref, tokens - rows, last))
        if first:
            me = ids_ref[0]
            row = lax.broadcasted_iota(jnp.int32, (width, pair_rows), 0)
            col = lax.broadcasted_iota(jnp.int32, (width, pair_rows), 1)
            target = jnp.where(col < own_rows, me * own_rows + col, ((me ^ 1) - 1) * own_rows + col)
            chosen = jnp.where(row == target, 1.0, 0.0).astype(BF16)
        for copy in copies:
            copy.wait()
        if first:
            h2c_ref[...] = dot(h2_ref[...], chosen).T.astype(BF16)
            gc_ref[...] = dot(g_ref[...], chosen).T.astype(BF16)

    wg, wu, wd = wg_ref[...], wu_ref[...], wd_ref[...]
    last = slice(tokens - rows, tokens)
    totals = [
        dot(left[:, last], term[...])
        for left, term in ((h2c_ref, dgate_ref), (h2c_ref, dup_ref), (gc_ref, act_ref))
    ]
    for begin in range(0, tokens - rows, row_tile):
        part = slice(begin, min(begin + row_tile, tokens - rows))
        h2 = h2_ref[part]
        act, dgate, dup = hidden_terms(dot(h2, wg), dot(h2, wu), dot(g_ref[part], wd))
        h2c, gc = h2c_ref[:, part], gc_ref[:, part]
        terms = [dot(h2c, dgate), dot(h2c, dup), dot(gc, act)]
        totals = [a + b for a, b in zip(totals, terms)]
    for i, (own, total) in enumerate(zip(own_refs, totals)):
        own[...] = total[:own_rows]
        other_ref[i] = total[own_rows:].astype(BF16)


def bulk_mlp(ids, h2, g, own_terms, weights, chosen, own_rows, begin, end, tile, after):
    width = h2[0].shape[1]
    rows, hidden = own_terms[0].shape
    tokens = sum(piece.shape[0] for piece in h2) - rows
    out_hidden = min(end * tile, hidden) - begin * tile
    weight = pl.BlockSpec((width, tile), lambda i: (0, i + begin))
    term = pl.BlockSpec((rows, tile), lambda i: (0, i + begin))
    result = pl.BlockSpec((own_rows, tile), lambda i: (0, i))
    columns = pl.BlockSpec((2 * own_rows, tokens), lambda i: (0, 0))
    first = not chosen
    pieces = (len(h2), len(g))
    body = functools.partial(
        bulk_mlp_kernel, pieces=pieces, row_tile=min(tokens, 1024), first=first
    )
    return pl.pallas_call(
        ordered(body, len(after)),
        grid=(end - begin,),
        in_specs=[ANYWHERE] * len(after)
        + [SCALARS]
        + [ANYWHERE] * sum(pieces)
        + [term] * 3
        + [weight] * 3
        + [columns] * len(chosen),
        out_specs=[result] * 3
        + [pl.BlockSpec((3, own_rows, tile), lambda i: (0, 0, i))]
        + [columns] * (2 if first else 0),
        out_shape=[shape((own_rows, out_hidden), F32)] * 3
        + [shape((3, own_rows, out_hidden), BF16)]
        + [shape((2 * own_rows, tokens), BF16)] * (2 if first else 0),
        scratch_shapes=[pltpu.VMEM((tokens, width), BF16)] * 2 + [pltpu.SemaphoreType.DMA((len(h2) + 2 * len(g) - 3,))],
        compiler_params=pltpu.CompilerParams(vmem_limit_bytes=VMEM_LIMIT),
        cost_estimate=cost(
            6 * tokens * (width + 2 * own_rows) * out_hidden,
            6 * width * out_hidden + 4 * tokens * width,
            tokens * out_hidden,
            scale=0.12,
        ),
        name="bulk_mlp",
    )(*after, ids, *h2, *g, *own_terms, *weights, *chosen)


def shards(
    tokens,
    w_query,
    w_key,
    w_value,
    w_output,
    w_gate,
    w_up,
    w_down,
    attn_gain,
    mlp_gain,
    query_gain,
    key_gain,
    segments,
    positions,
    cotangent,
):
    count = lax.axis_size("ctx")
    me = lax.axis_index("ctx")
    core = lax.axis_index("tp")
    nz = count // QUAD
    m = me % QUAD
    head = query_gain.shape[0]
    rows, model = tokens.shape
    q_heads = w_query.shape[1] // head
    kv_heads = w_key.shape[1] // head
    group = q_heads // kv_heads
    pair = rows // SEQS
    quad_rows = QUAD * rows
    columns = group * head
    own_rows = model // count
    flips = [flip_pairs(count, j) for j in range(QUAD)]
    ids = jnp.stack([me, core]).astype(jnp.int32)

    def quad_exchange(pieces):
        return [pieces[0]] + [send(pieces[j], flips[j]) for j in range(1, QUAD)]

    own_tokens = tokens.reshape(SEQS, pair, model)
    half = lax.dynamic_index_in_dim(own_tokens, core, 0, keepdims=False)
    mine = [send(half, flips[j]) for j in range(1, QUAD)]
    theirs = [swap_cores(p) for p in mine]

    freqs = ROPE_BASE ** (-2.0 * np.arange(head // 2) / head)
    freqs = jnp.asarray(np.tile(freqs, 4)[None, :], F32)
    bias, angles = kernel_call(
        mask_kernel,
        "visible",
        (ids, freqs, segments.reshape(count, SEQS * pair)),
        [shape((SEQS, count * pair, QUAD * pair), F32), shape((quad_rows, 2 * head), F32)],
        scalars=True,
    )
    sign = jnp.asarray(np.tile(np.repeat([-1.0, 1.0], head // 2), 2)[None, :], F32)
    cos, sin = jnp.cos(angles), jnp.sin(angles) * sign
    w_head = jnp.concatenate(
        [
            lax.dynamic_slice_in_dim(w_key, m * head, head, 1),
            lax.dynamic_slice_in_dim(w_value, m * head, head, 1),
            lax.dynamic_slice_in_dim(w_query, m * columns, columns, 1),
            jnp.zeros((model, head), BF16),
        ],
        axis=1,
    )
    h1, raw, q, kv_own, g_copy = kernel_call(
        qkv_kernel,
        "query_key_value",
        (
            ids,
            own_tokens,
            *mine,
            *theirs,
            attn_gain,
            w_head,
            key_gain,
            query_gain,
            cos,
            sin,
            cotangent,
        ),
        [
            shape((SEQS, QUAD, pair, model), BF16),
            shape((quad_rows, 6 * head), F32),
            shape((quad_rows, 4 * head), BF16),
            shape((quad_rows, 2 * head), BF16),
            shape((rows, model), BF16),
        ],
        flops=2 * quad_rows * model * 6 * head,
        scalars=True,
    )
    kv = [kv_own] + [send(kv_own, shift_pairs(count, s)) for s in range(1, nz)]
    hidden = w_down.shape[1]
    (da,) = hidden_call(
        hidden_grad_kernel,
        "hidden_grad",
        (cotangent, w_down),
        [shape((rows, hidden), F32)],
        after=(kv_own,),
    )
    g_blocks = [lax.ppermute(g_copy, ("ctx", "tp"), core_pairs(count))]

    def next_cotangents(after):
        g_blocks.append(send(touch(g_blocks[-1], after), shift_pairs(count, 1)))

    *attn, lse = attention_forward(q, bias, kv, group, (da,))
    next_cotangents((lse,))
    attn_pieces = quad_exchange([a.reshape(rows, columns) for a in attn])
    branch = kernel_call(
        branch_kernel,
        "branch",
        (ids, *attn_pieces, w_output),
        [shape((rows // 2, model), BF16)] * 2,
        flops=2 * rows * model * w_output.shape[1],
        scalars=True,
        scratch=[pltpu.VMEM((QUAD, rows, columns), BF16)],
    )
    for _ in range(2, nz - 1):
        next_cotangents((branch[0],))
    middle, h2, h2_half = kernel_call(
        middle_kernel,
        "middle",
        (ids, tokens, *branch, *[swap_cores(b) for b in branch], mlp_gain),
        [shape((rows, model), F32), shape((rows, model), BF16), shape((rows // 2, model), BF16)],
        scalars=True,
    )
    h2_pieces = gather_column(h2_half, count)

    g_first = swap_cores(g_blocks[0])
    *dh2, act, dgate, dup = hidden_call(
        own_mlp_kernel,
        "own_mlp",
        (h2, da, w_gate, w_up),
        [shape((rows // 2, model), BF16)] * 2 + [shape((rows, hidden), BF16)] * 3,
        scratch=[pltpu.VMEM((model, rows), F32)],
        matmuls=4,
        after=(g_first,),
    )
    h2_packed = pack(h2_pieces, (act,))
    next_cotangents((act,))
    g_swapped = [g_first] + [swap_cores(g) for g in g_blocks[1:-1]]
    grad_middle, dy, dy_half, mlp_gain_part, *do = kernel_call(
        back_kernel,
        "back",
        (ids, middle, *dh2, *[swap_cores(d) for d in dh2], cotangent, mlp_gain, w_output),
        [
            shape((rows, model), F32),
            shape((rows, model), BF16),
            shape((rows // 2, model), BF16),
            shape((1, model), F32),
            *[shape((rows, columns), BF16)] * QUAD,
        ],
        flops=2 * rows * model * w_output.shape[1],
        scalars=True,
        scratch=[pltpu.VMEM((QUAD, rows, columns), BF16)],
        after=(h2_packed, *g_blocks[2:-1], *g_swapped[1:-1]),
    )
    do_pieces = [d.reshape(SEQS, pair, columns) for d in quad_exchange(do)]
    dy_half = touch(dy_half, do_pieces[1:])
    dy_mine = [send(dy_half, flips[j]) for j in range(1, QUAD)]
    dy_theirs = [swap_cores(p) for p in dy_mine]
    dy_pieces = (dy.reshape(SEQS, pair, model), *dy_mine, *dy_theirs)
    dq, *dkv = attention_backward(
        q, bias, lse, do_pieces, kv, (g_blocks[-1], *g_swapped[-1:])
    )
    h2_column = touch(h2_packed, (dq, *dy_mine))
    h2_other = send(h2_column, flips[2])
    (down,) = hidden_call(
        down_kernel,
        "down",
        (act, w_down),
        [shape((rows, model), BF16)],
        scratch=[pltpu.VMEM((model, rows), F32)],
        after=(dq,),
    )
    dkv = [dkv[0]] + [send(dkv[s], shift_pairs(count, nz - s)) for s in range(1, nz)]

    (output,) = kernel_call(
        output_kernel, "output", (middle, down, swap_cores(down)), [shape((rows, model), BF16)]
    )

    h2_column = touch(h2_column, (down, h2_other, *dkv[1:]))
    h2_other = touch(h2_other, (h2_column,))
    g_blocks[-1] = touch(g_blocks[-1], (h2_column,))
    h2_rows = (h2_column, h2_other, swap_cores(h2_column), swap_cores(h2_other), h2)
    g_rows = (*g_blocks, *g_swapped, swap_cores(g_blocks[-1]), cotangent)

    tile = 512
    tiles = pl.cdiv(hidden, tile)
    cut = (2 * tiles + 2) // 3

    def bulk_part(chosen, begin, end, after):
        result = bulk_mlp(
            ids,
            h2_rows,
            g_rows,
            (act, dgate, dup),
            (w_gate, w_up, w_down),
            chosen,
            own_rows,
            begin,
            end,
            tile,
            after,
        )
        return result[:3], result[3], result[4:]

    z_rows = model // nz
    head_part, *rest = kernel_call(
        head_grad_kernel,
        "head_grad",
        (ids, dq, raw, h1, *attn, *dy_pieces, key_gain, query_gain, cos, sin, *dkv),
        [
            shape((1, 6 * head), F32),
            *[shape((rows, 6 * head), BF16)] * QUAD,
            *[shape((z_rows, 8 * head), BF16)] * nz,
        ],
        flops=2 * quad_rows * model * 9 * head,
        scalars=True,
        scratch=[
            pltpu.VMEM((model, 8 * head), F32),
            pltpu.VMEM((SEQS, QUAD, pair, model), BF16),
        ],
        after=(down,),
    )
    grad_pieces, w_parts = quad_exchange(rest[:QUAD]), rest[QUAD:]
    w_parts = [w_parts[0]] + [send(w_parts[s], shift_pairs(count, nz - s)) for s in range(1, nz)]
    bulk_first = bulk_part((), 0, cut, (head_part,))
    dh1, attn_gain_part = kernel_call(
        input_grad_kernel,
        "input_grad",
        (ids, *grad_pieces, tokens, w_query, w_key, w_value),
        [shape((rows, model), BF16), shape((1, model), F32)],
        flops=2 * rows * model * (q_heads + 2 * kv_heads) * head,
        scalars=True,
        scratch=[pltpu.VMEM((QUAD, rows, 6 * head), BF16)],
        after=(bulk_first[0][0], *w_parts),
    )
    (grad_tokens,) = kernel_call(
        tokens_kernel,
        "tokens_grad",
        (tokens, grad_middle, dh1, swap_cores(dh1), attn_gain),
        [shape((rows, model), BF16)],
    )
    spread = kernel_call(
        spread_kernel,
        "spread",
        (ids, *w_parts),
        [shape((own_rows, 8 * head), F32)] + [shape((own_rows, 8 * head), BF16)] * (QUAD - 1),
        scalars=True,
        scratch=[pltpu.VMEM((z_rows, 8 * head), F32)],
        after=(bulk_first[0][0],),
    )
    gains = sum_but_x(
        jnp.concatenate([attn_gain_part, 0.5 * mlp_gain_part, head_part], axis=1)[0], count
    )
    theirs_first = send(bulk_first[1], flips[1])
    bulk_second = bulk_part(
        bulk_first[2], cut, tiles, (spread[0], grad_tokens, output, gains)
    )
    gains = gains + send(gains, flips[1])
    spread = quad_exchange(spread)
    theirs_second = send(touch(bulk_second[1], (gains, *spread[1:])), flips[1])
    mlp_grads = [
        jnp.concatenate(
            [
                bulk_first[0][i] + theirs_first[i].astype(F32),
                bulk_second[0][i] + theirs_second[i].astype(F32),
            ],
            axis=1,
        )
        for i in range(3)
    ]
    grad_wq, grad_wk, grad_wv, grad_wo = kernel_call(
        assemble_kernel,
        "assemble",
        (ids, *spread),
        [
            shape((own_rows, q_heads * head), F32),
            shape((own_rows, kv_heads * head), F32),
            shape((own_rows, kv_heads * head), F32),
            shape((own_rows, q_heads * head), F32),
        ],
        scalars=True,
        scratch=[pltpu.VMEM((QUAD, own_rows, 8 * head), F32)],
    )

    head_sums = gains[2 * model :].reshape(-1, head)
    return (
        output,
        grad_tokens,
        grad_wq,
        grad_wk,
        grad_wv,
        grad_wo,
        mlp_grads[0],
        mlp_grads[1],
        mlp_grads[2],
        gains[:model],
        gains[model : 2 * model],
        jnp.sum(head_sums[2 : 2 + group], axis=0),
        head_sums[0],
    )


def solution(mesh):
    rows = P("ctx", None)
    columns = P(None, "tp")
    both = P("ctx", "tp")
    in_specs = (rows,) + (columns,) * 7 + (P(),) * 5 + (P("ctx"), rows)
    out_specs = (rows, rows) + (both,) * 7 + (P(),) * 4
    return jax.shard_map(shards, mesh=mesh, in_specs=in_specs, out_specs=out_specs, check_vma=False)
```

```python
import functools

import jax
import jax.numpy as jnp
import numpy as np
from jax import lax
from jax.experimental import pallas as pl
from jax.experimental.pallas import tpu as pltpu
from jax.sharding import PartitionSpec as P

BLK = 32
SEQS = 2
QUAD = 4
EPSILON = 1e-05
ROPE_BASE = 1000000.0
MASKED = -1e30
F32 = jnp.float32
BF16 = jnp.bfloat16
VMEM_LIMIT = 56 * 1024 * 1024


def dot(left, right):
    return jnp.dot(left, right, preferred_element_type=F32)


def contract_last(left, right):
    return lax.dot_general(left, right, (((1,), (1,)), ((), ())), preferred_element_type=F32)


def contract_first(left, right):
    return lax.dot_general(left, right, (((0,), (0,)), ((), ())), preferred_element_type=F32)


def shift_pairs(count, step):
    nz = count // QUAD
    return [(i, ((i // QUAD + step) % nz) * QUAD + i % QUAD) for i in range(count)]


def flip_pairs(count, bits):
    return [(i, i ^ bits) for i in range(count)]


def send(value, pairs):
    return lax.ppermute(value, "ctx", pairs)


def swap_cores(value):
    return lax.ppermute(value, "tp", [(0, 1), (1, 0)])


def core_pairs(count):
    return [pair for i in range(count) for pair in ((2 * i, 2 * i), (2 * i + 1, 2 * (i ^ 2) + 1))]


def gather_column(half, count):
    return [half] + [send(half, shift_pairs(count, s)) for s in range(1, count // QUAD)]


COST_SCALE = 0.01


def cost(flops, bytes_accessed, transcendentals=0, scale=COST_SCALE):
    return pl.CostEstimate(
        flops=int(flops * scale),
        bytes_accessed=int(bytes_accessed * scale),
        transcendentals=int(transcendentals * scale),
    )


SCALARS = pl.BlockSpec(memory_space=pltpu.SMEM)


ANYWHERE = pl.BlockSpec(memory_space=pl.ANY)


def ordered(body, extra):
    return lambda *refs: body(*refs[extra:])


def kernel_call(
    body, name, args, out_shape, flops=0, scalars=False, scratch=(), after=(), scale=COST_SCALE
):
    vmem = pl.BlockSpec(memory_space=pltpu.VMEM)
    bytes_accessed = sum(a.size * a.dtype.itemsize for a in (*args, *out_shape))
    return pl.pallas_call(
        ordered(body, len(after)),
        in_specs=[ANYWHERE] * len(after)
        + [SCALARS if scalars and i == 0 else vmem for i in range(len(args))],
        out_specs=[vmem] * len(out_shape),
        out_shape=list(out_shape),
        scratch_shapes=list(scratch),
        compiler_params=pltpu.CompilerParams(vmem_limit_bytes=VMEM_LIMIT),
        cost_estimate=cost(flops, bytes_accessed, scale=scale),
        name=name,
    )(*after, *args)


def shape(dims, dtype):
    return jax.ShapeDtypeStruct(dims, dtype)


def pack_kernel(*refs):
    pieces, out_ref = refs[:-1], refs[-1]
    rows = pieces[0].shape[0]
    for i, piece in enumerate(pieces):
        out_ref[i * rows : (i + 1) * rows] = piece[...]


def pack(pieces, after=()):
    rows, width = pieces[0].shape
    out = shape((len(pieces) * rows, width), pieces[0].dtype)
    return kernel_call(pack_kernel, "pack", pieces, [out], after=after)[0]


def touch(value, after):
    return pl.pallas_call(
        lambda *refs: None,
        in_specs=[ANYWHERE] * (1 + len(after)),
        out_specs=ANYWHERE,
        out_shape=shape(value.shape, value.dtype),
        input_output_aliases={0: 0},
        name="touch",
    )(value, *after)


def row_factor(x):
    return lax.rsqrt(jnp.mean(x * x, axis=-1, keepdims=True) + EPSILON)


def head_means(x, blocks):
    high = x.astype(BF16)
    low = (x - high.astype(F32)).astype(BF16)
    return dot(high, blocks) + dot(low, blocks)


def head_blocks():
    row = lax.broadcasted_iota(jnp.int32, (128, 128), 0)
    col = lax.broadcasted_iota(jnp.int32, (128, 128), 1)
    return jnp.where(row // 64 == col // 64, 1.0 / 64, 0.0).astype(BF16)


def row_of(ref):
    return ref[...].reshape(1, -1)


def head_gain_rows(key_ref, query_ref):
    key, query = row_of(key_ref), row_of(query_ref)
    return jnp.concatenate([key, key], axis=1), jnp.concatenate([query, query], axis=1)


def lanes_of(x):
    return lax.broadcasted_iota(jnp.int32, x.shape, 1)


def partner(x):
    return jnp.where(lanes_of(x) % 64 < 32, pltpu.roll(x, 96, 1), pltpu.roll(x, 32, 1))


def mask_kernel(ids_ref, freq_ref, seg_ref, bias_ref, angle_ref):
    me = ids_ref[0]
    count = seg_ref.shape[0]
    nz = count // QUAD
    tokens = seg_ref.shape[1] // SEQS
    z, m = me // QUAD, me % QUAD

    def place(chip, offset):
        return jnp.where(offset < BLK, chip * BLK, (2 * count - 2 - chip) * BLK) + offset

    chips = [((z + nz - step) % nz) * QUAD + (m ^ j) for step in range(nz) for j in range(QUAD)]
    seg_rows = [seg_ref[pl.ds(chip, 1), :].astype(F32) for chip in chips]
    fill = jnp.zeros((128 - count, SEQS * tokens), F32)
    seg_cols = jnp.concatenate([*seg_rows, fill], axis=0).T
    row_offset = lax.broadcasted_iota(jnp.int32, (1, tokens), 1)
    col_offset = lax.broadcasted_iota(jnp.int32, (tokens, 1), 0)
    place_q = jnp.concatenate([place(chip, row_offset) for chip in chips[:QUAD]], axis=1)
    far = 2 * count * BLK
    for seq in range(SEQS):
        of_seq = slice(seq * tokens, (seq + 1) * tokens)
        seg_q = jnp.concatenate([row[:, of_seq] for row in seg_rows[:QUAD]], axis=1)
        first = jnp.full((tokens, QUAD * tokens), far, jnp.int32)
        for i, chip in enumerate(chips):
            place_k = place(chip, col_offset)
            same = seg_cols[of_seq, i : i + 1] == seg_q
            bias_ref[seq, i * tokens : (i + 1) * tokens, :] = jnp.where(
                same & (place_k <= place_q), 0.0, MASKED
            )
            first = jnp.minimum(first, jnp.where(same, place_k, far))
        position = (place_q - jnp.min(first, axis=0, keepdims=True)).astype(F32)
        rows = position.shape[1]
        angle_ref[seq * rows : (seq + 1) * rows, :] = (
            jnp.broadcast_to(position, (128, rows)).T * freq_ref[...]
        )


def qkv_kernel(ids_ref, own_ref, *refs):
    mine, theirs = refs[:3], refs[3:6]
    gain_ref, w_ref, key_gain_ref, query_gain_ref, cos_ref, sin_ref, g_ref = refs[6:13]
    h1_ref, raw_ref, q_ref, kv_ref, copy_ref = refs[13:]
    core = ids_ref[1]
    gain = row_of(gain_ref)
    copy_ref[...] = g_ref[...]

    def put(seq, j, piece):
        x = piece.astype(F32)
        h1_ref[seq, j] = (x * row_factor(x) * gain).astype(BF16)

    put(0, 0, own_ref[0])
    put(1, 0, own_ref[1])
    for j in range(1, QUAD):
        put(core, j, mine[j - 1][...])
        put(1 - core, j, theirs[j - 1][...])
    rows = raw_ref.shape[0]
    raw = dot(h1_ref[...].reshape(rows, -1), w_ref[...])
    raw_ref[...] = raw
    cos, sin, blocks = cos_ref[...], sin_ref[...], head_blocks()
    key_gain, query_gain = head_gain_rows(key_gain_ref, query_gain_ref)
    out = []
    for c in range(3):
        x = raw[:, 128 * c : 128 * (c + 1)]
        gain = key_gain if c == 0 else query_gain * 64 ** (-0.5)
        n = x * lax.rsqrt(head_means(x * x, blocks) + EPSILON) * gain
        out.append(n * cos + partner(n) * sin)
    kv_ref[...] = jnp.where(lanes_of(out[0]) < 64, out[0], raw[:, :128]).astype(BF16)
    q_ref[...] = jnp.concatenate(out[1:], axis=1).astype(BF16)


def head_lanes(x, g, upper):
    part = x[:, 128 * (g // 2) : 128 * (g // 2) + 128]
    if (g % 2 == 1) != upper:
        part = pltpu.roll(part, 64, 1)
    keep = (lanes_of(part) >= 64) if upper else (lanes_of(part) < 64)
    return jnp.where(keep, part, 0.0).astype(BF16)


def attention_forward_kernel(q_ref, bias_ref, *refs):
    kv_refs, o_refs, lse_ref = refs[: -QUAD - 1], refs[-QUAD - 1 : -1], refs[-1]
    group = lse_ref.shape[1]
    kv = jnp.concatenate([r[...] for r in kv_refs], axis=0)
    v_t = kv.T[64:]
    q = q_ref[...].astype(F32)
    bias = bias_ref[0]
    out = []
    for g in range(group):
        s = contract_last(kv, head_lanes(q, g, False)) + bias
        top = jnp.max(s, axis=0, keepdims=True)
        p = jnp.exp(s - top)
        total = jnp.sum(p, axis=0, keepdims=True)
        out.append(dot(v_t, p.astype(BF16)) / total)
        lse_ref[0, g] = top + jnp.log(total)
    o = jnp.concatenate(out, axis=0).T.astype(BF16)
    rows = o.shape[0] // QUAD
    for j in range(QUAD):
        o_refs[j][0] = o[j * rows : (j + 1) * rows]


def attention_backward_kernel(q_ref, bias_ref, lse_ref, *refs):
    do_refs, kv_refs, dq_ref, dkv_refs = refs[:QUAD], None, None, None
    rest = refs[QUAD:]
    pieces = (len(rest) - 1) // 2
    kv_refs, dq_ref, dkv_refs = rest[:pieces], rest[pieces], rest[pieces + 1 :]
    group = lse_ref.shape[1]
    kv = jnp.concatenate([r[...] for r in kv_refs], axis=0)
    k_t = kv.T[:64]
    q = q_ref[...].astype(F32)
    do = jnp.concatenate([r[0].astype(F32) for r in do_refs], axis=0)
    do = jnp.concatenate([do, jnp.zeros((do.shape[0], 64), F32)], axis=1)
    rows = q.shape[0]
    bias = bias_ref[0]
    total = jnp.zeros(kv.shape, F32)
    dq = []
    for g in range(group):
        both = jnp.concatenate([head_lanes(q, g, False), head_lanes(do, g, True)], axis=0)
        products = contract_last(kv, both)
        p = jnp.exp(products[:, :rows] + (bias - lse_ref[0, g]))
        dp = products[:, rows:]
        delta = jnp.sum(p * dp, axis=0, keepdims=True)
        ds = (p * (dp - delta)).astype(BF16)
        total = total + dot(jnp.concatenate([ds, p.astype(BF16)], axis=1), both)
        dq.append(dot(k_t, ds))
    dq.append(jnp.zeros(dq[0].shape, F32))
    dq_ref[...] = jnp.concatenate(dq, axis=0).T
    for i, ref in enumerate(dkv_refs):
        ref[...] = total[i * rows : (i + 1) * rows].astype(BF16)


def attention_specs(rows, keys, pieces):
    q = pl.BlockSpec((rows, 256), lambda s: (s, 0))
    bias = pl.BlockSpec((1, keys, rows), lambda s: (s, 0, 0))
    kv = [pl.BlockSpec((rows, 128), lambda s: (s, 0))] * pieces
    return q, bias, kv


def attention_forward(q, bias, kv, group, after):
    seqs, keys, rows = bias.shape
    q_spec, bias_spec, kv_specs = attention_specs(rows, keys, len(kv))
    work = seqs * group * keys * rows
    return pl.pallas_call(
        ordered(attention_forward_kernel, len(after)),
        grid=(seqs,),
        in_specs=[*[ANYWHERE] * len(after), q_spec, bias_spec, *kv_specs],
        out_specs=[
            *[pl.BlockSpec((1, rows // QUAD, group * 64), lambda s: (s, 0, 0))] * QUAD,
            pl.BlockSpec((1, group, 1, rows), lambda s: (s, 0, 0, 0)),
        ],
        out_shape=[
            *[shape((seqs, rows // QUAD, group * 64), BF16)] * QUAD,
            shape((seqs, group, 1, rows), F32),
        ],
        compiler_params=pltpu.CompilerParams(vmem_limit_bytes=VMEM_LIMIT),
        cost_estimate=cost(6 * work * 128, 4 * bias.size, work),
        name="attention_forward",
    )(*after, q, bias, *kv)


def attention_backward(q, bias, lse, do, kv, after=()):
    seqs, keys, rows = bias.shape
    group = lse.shape[1]
    q_spec, bias_spec, kv_specs = attention_specs(rows, keys, len(kv))
    work = seqs * group * keys * rows
    return pl.pallas_call(
        ordered(attention_backward_kernel, len(after)),
        grid=(seqs,),
        in_specs=[
            *[ANYWHERE] * len(after),
            q_spec,
            bias_spec,
            pl.BlockSpec((1, group, 1, rows), lambda s: (s, 0, 0, 0)),
            *[pl.BlockSpec((1, rows // QUAD, group * 64), lambda s: (s, 0, 0))] * QUAD,
            *kv_specs,
        ],
        out_specs=[q_spec, *kv_specs],
        out_shape=[shape(q.shape, F32)] + [shape(k.shape, BF16) for k in kv],
        compiler_params=pltpu.CompilerParams(vmem_limit_bytes=VMEM_LIMIT),
        cost_estimate=cost(10 * work * 128, 4 * bias.size, work),
        name="attention_backward",
    )(*after, q, bias, lse, *do, *kv)


def put_halves(refs, value):
    rows = refs[0].shape[0]
    for i, ref in enumerate(refs):
        ref[...] = value[i * rows : (i + 1) * rows].astype(ref.dtype)


def sum_halves(refs):
    own = jnp.concatenate([refs[0][...], refs[1][...]], axis=0).astype(F32)
    return own + jnp.concatenate([refs[2][...], refs[3][...]], axis=0).astype(F32)


def branch_kernel(ids_ref, *refs):
    pieces, w_ref, out_refs, stack_ref = refs[:QUAD], refs[QUAD], refs[QUAD + 1 : -1], refs[-1]
    m = ids_ref[0] % QUAD
    for j in range(QUAD):
        stack_ref[j] = pieces[j][...]
    attn = jnp.concatenate([stack_ref[m ^ k] for k in range(QUAD)], axis=1)
    put_halves(out_refs, contract_last(attn, w_ref[...]))


def middle_kernel(ids_ref, x_ref, *refs):
    branch_refs, (gain_ref, mid_ref, h2_ref, half_ref) = refs[:4], refs[4:]
    mid = x_ref[...].astype(F32) + sum_halves(branch_refs)
    mid_ref[...] = mid
    h2 = (mid * row_factor(mid) * row_of(gain_ref)).astype(BF16)
    h2_ref[...] = h2
    rows = half_ref.shape[0]
    half_ref[...] = jnp.where(ids_ref[1] == 0, h2[:rows], h2[rows:])


def hidden_terms(gate, up, da):
    sg = jax.nn.sigmoid(gate)
    silu = gate * sg
    act = (silu * up).astype(BF16)
    dgate = (da * up * (sg + silu * (1.0 - sg))).astype(BF16)
    dup = (da * silu).astype(BF16)
    return act, dgate, dup


def hidden_tile(hidden):
    return next(t for t in (1152, 384, 128, hidden) if hidden % t == 0)


def hidden_call(body, name, args, out_shape, scratch=(), matmuls=1, after=()):
    hidden = max(a.shape[-1] for a in args)
    tile = hidden_tile(hidden)

    def spec(a):
        if a.shape[-1] == hidden:
            return pl.BlockSpec((a.shape[0], tile), lambda i: (0, i))
        return pl.BlockSpec(a.shape, lambda i: (0, 0))

    rows, width = args[0].shape[0], 1536
    return pl.pallas_call(
        ordered(body, len(after)),
        grid=(hidden // tile,),
        in_specs=[ANYWHERE] * len(after) + [spec(a) for a in args],
        out_specs=[spec(o) for o in out_shape],
        out_shape=list(out_shape),
        scratch_shapes=list(scratch),
        compiler_params=pltpu.CompilerParams(vmem_limit_bytes=VMEM_LIMIT),
        cost_estimate=cost(
            4 * matmuls * rows * width * hidden,
            sum(a.size * a.dtype.itemsize for a in (*args, *out_shape)),
        ),
        name=name,
    )(*after, *args)


def accumulate(total_ref, out_refs, term):
    step = pl.program_id(0)

    @pl.when(step == 0)
    def _():
        total_ref[...] = term

    @pl.when(step > 0)
    def _():
        total_ref[...] += term

    @pl.when(step == pl.num_programs(0) - 1)
    def _():
        put_halves(out_refs, total_ref[...].T)


def hidden_grad_kernel(g_ref, wd_ref, da_ref):
    da_ref[...] = dot(g_ref[...], wd_ref[...])


def own_mlp_kernel(
    h2_ref, da_ref, wg_ref, wu_ref, dh_top_ref, dh_ref, act_ref, dgate_ref, dup_ref, total_ref
):
    wg, wu, h2 = wg_ref[...], wu_ref[...], h2_ref[...]
    act, dgate, dup = hidden_terms(dot(h2, wg), dot(h2, wu), da_ref[...])
    act_ref[...] = act
    dgate_ref[...] = dgate
    dup_ref[...] = dup
    accumulate(
        total_ref, (dh_top_ref, dh_ref), contract_last(wg, dgate) + contract_last(wu, dup)
    )


def down_kernel(act_ref, wd_ref, down_ref, total_ref):
    accumulate(total_ref, (down_ref,), contract_last(wd_ref[...], act_ref[...]))


def back_kernel(
    ids_ref, mid_ref, a_ref, b_ref, c_ref, d_ref, g_ref, gain_ref, w_ref, dx_ref, dy_ref, *refs
):
    half_ref, part_ref, do_refs = refs[0], refs[1], refs[2:]
    m = ids_ref[0] % QUAD
    stack_ref, do_refs = do_refs[-1], do_refs[:-1]
    mid = mid_ref[...]
    factor = row_factor(mid)
    dh2 = sum_halves((a_ref, b_ref, c_ref, d_ref))
    part_ref[...] = jnp.sum(dh2 * mid * factor, axis=0, keepdims=True)
    scaled = dh2 * row_of(gain_ref)
    inner = jnp.mean(mid * scaled, axis=-1, keepdims=True)
    dx = g_ref[...].astype(F32) + (factor * scaled - mid * (factor * factor * factor) * inner)
    dx_ref[...] = dx
    dy = dx.astype(BF16)
    dy_ref[...] = dy
    half = half_ref.shape[0]
    half_ref[...] = jnp.where(ids_ref[1] == 0, dy[:half], dy[half:])
    do = dot(dy, w_ref[...]).astype(BF16)
    columns = do.shape[1] // QUAD
    for k in range(QUAD):
        stack_ref[m ^ k] = do[:, k * columns : (k + 1) * columns]
    for j in range(QUAD):
        do_refs[j][...] = stack_ref[j]


def norm_rotate_back(grad, raw, gain, cos, sin, blocks):
    normed = grad * cos - partner(grad) * sin
    factor = lax.rsqrt(head_means(raw * raw, blocks) + EPSILON)
    scaled = normed * gain
    inner = head_means(raw * scaled, blocks)
    part = jnp.sum(normed * raw * factor, axis=0, keepdims=True)
    return factor * scaled - raw * (factor * factor * factor) * inner, part


def head_grad_kernel(ids_ref, dq_ref, raw_ref, h1_ref, *refs):
    attn_refs, dy_ref, mine, theirs, refs = refs[:4], refs[4], refs[5:8], refs[8:11], refs[11:]
    core = ids_ref[1]
    key_gain_ref, query_gain_ref, cos_ref, sin_ref, refs = *refs[:4], refs[4:]
    nz = (len(refs) - QUAD - 3) // 2
    dkv_refs, refs = refs[:nz], refs[nz:]
    part_ref, piece_refs, w_refs = refs[0], refs[1 : 1 + QUAD], refs[1 + QUAD : -2]
    total_ref, dy_all = refs[-2:]
    cos, sin, blocks = cos_ref[...], sin_ref[...], head_blocks()
    key_gain, query_gain = head_gain_rows(key_gain_ref, query_gain_ref)
    dkv = dkv_refs[0][...].astype(F32)
    for ref in dkv_refs[1:]:
        dkv = dkv + ref[...].astype(F32)
    scale = 64 ** (-0.5)
    low = []
    for c in range(3):
        lanes = slice(128 * c, 128 * (c + 1))
        given = dkv if c == 0 else dq_ref[:, 128 * (c - 1) : 128 * c] * scale
        gain = key_gain if c == 0 else query_gain
        grad, part = norm_rotate_back(given, raw_ref[:, lanes], gain, cos, sin, blocks)
        if c == 0:
            grad = jnp.where(lanes_of(grad) < 64, grad, dkv)
        part_ref[:, lanes] = part
        low.append(grad.astype(BF16))
    low = jnp.concatenate(low, axis=1)
    rows = low.shape[0]
    tokens = rows // (SEQS * QUAD)
    attn = []
    for seq in range(SEQS):
        for j in range(QUAD):
            begin = (seq * QUAD + j) * tokens
            piece_refs[j][seq * tokens : (seq + 1) * tokens] = low[begin : begin + tokens]
            if j == 0:
                dy_all[seq, j] = dy_ref[seq]
            attn.append(attn_refs[j][seq])
    for j in range(1, QUAD):
        dy_all[core, j] = mine[j - 1][...]
        dy_all[1 - core, j] = theirs[j - 1][...]
    columns = attn[0].shape[1]
    grad_wqkv = contract_first(h1_ref[...].reshape(rows, -1), low)
    grad_wo = contract_first(dy_all[...].reshape(rows, -1), jnp.concatenate(attn, axis=0))
    total_ref[...] = jnp.concatenate([grad_wqkv[:, : 128 + columns], grad_wo], axis=1)
    z = ids_ref[0] // QUAD
    owned = w_refs[0].shape[0]
    for step, ref in enumerate(w_refs):
        begin = pl.multiple_of(((z + nz - step) % nz) * owned, 8)
        ref[...] = total_ref[pl.ds(begin, owned), :].astype(BF16)


def spread_kernel(ids_ref, *refs):
    nz = len(refs) - QUAD - 1
    terms, (own_ref, *out_refs), total_ref = refs[:nz], refs[nz:-1], refs[-1]
    total = terms[0][...].astype(F32)
    for ref in terms[1:]:
        total = total + ref[...].astype(F32)
    total_ref[...] = total
    m = ids_ref[0] % QUAD
    rows = own_ref.shape[0]
    for j in range(QUAD):
        part = total_ref[pl.ds(pl.multiple_of((m ^ j) * rows, 8), rows), :]
        if j == 0:
            own_ref[...] = part
        else:
            out_refs[j - 1][...] = part.astype(BF16)


def assemble_kernel(ids_ref, own_ref, a_ref, b_ref, c_ref, wq_ref, wk_ref, wv_ref, wo_ref, stack_ref):
    m = ids_ref[0] % QUAD
    stack_ref[0] = own_ref[...]
    for j, ref in enumerate((a_ref, b_ref, c_ref)):
        stack_ref[j + 1] = ref[...].astype(F32)
    parts = [stack_ref[m ^ k] for k in range(QUAD)]
    columns = wq_ref.shape[1] // QUAD
    wk_ref[...] = jnp.concatenate([p[:, :64] for p in parts], axis=1)
    wv_ref[...] = jnp.concatenate([p[:, 64:128] for p in parts], axis=1)
    wq_ref[...] = jnp.concatenate([p[:, 128 : 128 + columns] for p in parts], axis=1)
    wo_ref[...] = jnp.concatenate([p[:, 128 + columns :] for p in parts], axis=1)


def input_grad_kernel(ids_ref, *refs):
    pieces, (x_ref, wq_ref, wk_ref, wv_ref, out_ref, part_ref, stack_ref) = refs[:QUAD], refs[QUAD:]
    m = ids_ref[0] % QUAD
    for j in range(QUAD):
        stack_ref[j] = pieces[j][...]
    parts = [stack_ref[m ^ k] for k in range(QUAD)]
    columns = wq_ref.shape[1] // QUAD
    dk = jnp.concatenate([p[:, :64] for p in parts], axis=1)
    dv = jnp.concatenate([p[:, 64:128] for p in parts], axis=1)
    dq = jnp.concatenate([p[:, 128 : 128 + columns] for p in parts], axis=1)
    total = (
        contract_last(dq, wq_ref[...])
        + contract_last(dk, wk_ref[...])
        + contract_last(dv, wv_ref[...])
    )
    out_ref[...] = total.astype(BF16)
    x = x_ref[...].astype(F32)
    part_ref[...] = jnp.sum(total * x * row_factor(x), axis=0, keepdims=True)


def tokens_kernel(x_ref, dx_ref, a_ref, b_ref, gain_ref, out_ref):
    x = x_ref[...].astype(F32)
    factor = row_factor(x)
    scaled = (a_ref[...].astype(F32) + b_ref[...].astype(F32)) * row_of(gain_ref)
    inner = jnp.mean(x * scaled, axis=-1, keepdims=True)
    back = factor * scaled - x * (factor * factor * factor) * inner
    out_ref[...] = (dx_ref[...] + back).astype(BF16)


def output_kernel(mid_ref, a_ref, b_ref, out_ref):
    out_ref[...] = (mid_ref[...] + (a_ref[...].astype(F32) + b_ref[...].astype(F32))).astype(BF16)


def bulk_mlp_kernel(ids_ref, *refs, pieces, row_tile, first):
    sides, refs = (refs[: pieces[0]], refs[pieces[0] : sum(pieces)]), refs[sum(pieces) :]
    act_ref, dgate_ref, dup_ref, wg_ref, wu_ref, wd_ref, refs = *refs[:6], refs[6:]
    if first:
        own_refs, other_ref, h2c_ref, gc_ref, h2_ref, g_ref, sems = refs[:3], *refs[3:]
    else:
        h2c_ref, gc_ref, own_refs, other_ref, h2_ref, g_ref, sems = *refs[:2], refs[2:5], *refs[5:]
    rows = act_ref.shape[0]
    tokens, width = h2_ref.shape
    own_rows = own_refs[0].shape[0]
    pair_rows = 2 * own_rows

    @pl.when(pl.program_id(0) == 0)
    def _():
        half = rows // 2
        places = pieces[1] // 2
        copies = []

        def copy_rows(source, skip, size, target, begin, sem):
            return pltpu.make_async_copy(
                source.at[pl.ds(skip, size)], target.at[pl.ds(begin, size)], sems.at[sem]
            )

        begin = 0
        for i, source in enumerate(sides[0]):
            skip = half if i in (0, 2) else 0
            copies.append(copy_rows(source, skip, source.shape[0] - skip, h2_ref, begin, i))
            begin += source.shape[0] - skip
        for copy in copies:
            copy.start()
        for core in range(2):

            @pl.when(ids_ref[1] == core)
            def _():
                own_y, other_y = sides[1][:places], sides[1][places : 2 * places]
                if core == 1:
                    own_y, other_y = other_y, own_y
                blocks = [*own_y[1:], *other_y]
                for i, source in enumerate(blocks):
                    for part in range(2):
                        to = (i + part * len(blocks)) * half
                        sem = len(sides[0]) + 2 * i + part
                        copy_rows(source, (core ^ part) * half, half, g_ref, to, sem).start()
                last = len(sides[0]) + 4 * places - 2
                copy_rows(sides[1][-1], 0, rows, g_ref, tokens - rows, last).start()

        for i in range(2 * (2 * places - 1)):
            copies.append(copy_rows(sides[1][0], 0, half, g_ref, 0, len(sides[0]) + i))
        last = len(sides[0]) + 4 * places - 2
        copies.append(copy_rows(sides[1][-1], 0, rows, g_ref, tokens - rows, last))
        if first:
            me = ids_ref[0]
            row = lax.broadcasted_iota(jnp.int32, (width, pair_rows), 0)
            col = lax.broadcasted_iota(jnp.int32, (width, pair_rows), 1)
            target = jnp.where(col < own_rows, me * own_rows + col, ((me ^ 1) - 1) * own_rows + col)
            chosen = jnp.where(row == target, 1.0, 0.0).astype(BF16)
        for copy in copies:
            copy.wait()
        if first:
            h2c_ref[...] = dot(h2_ref[...], chosen).T.astype(BF16)
            gc_ref[...] = dot(g_ref[...], chosen).T.astype(BF16)

    wg, wu, wd = wg_ref[...], wu_ref[...], wd_ref[...]
    last = slice(tokens - rows, tokens)
    totals = [
        dot(left[:, last], term[...])
        for left, term in ((h2c_ref, dgate_ref), (h2c_ref, dup_ref), (gc_ref, act_ref))
    ]
    for begin in range(0, tokens - rows, row_tile):
        part = slice(begin, min(begin + row_tile, tokens - rows))
        h2 = h2_ref[part]
        act, dgate, dup = hidden_terms(dot(h2, wg), dot(h2, wu), dot(g_ref[part], wd))
        h2c, gc = h2c_ref[:, part], gc_ref[:, part]
        terms = [dot(h2c, dgate), dot(h2c, dup), dot(gc, act)]
        totals = [a + b for a, b in zip(totals, terms)]
    for i, (own, total) in enumerate(zip(own_refs, totals)):
        own[...] = total[:own_rows]
        other_ref[i] = total[own_rows:].astype(BF16)


def bulk_mlp(ids, h2, g, own_terms, weights, chosen, own_rows, begin, end, tile, after):
    width = h2[0].shape[1]
    rows, hidden = own_terms[0].shape
    tokens = sum(piece.shape[0] for piece in h2) - rows
    out_hidden = min(end * tile, hidden) - begin * tile
    weight = pl.BlockSpec((width, tile), lambda i: (0, i + begin))
    term = pl.BlockSpec((rows, tile), lambda i: (0, i + begin))
    result = pl.BlockSpec((own_rows, tile), lambda i: (0, i))
    columns = pl.BlockSpec((2 * own_rows, tokens), lambda i: (0, 0))
    first = not chosen
    pieces = (len(h2), len(g))
    body = functools.partial(
        bulk_mlp_kernel, pieces=pieces, row_tile=min(tokens, 1024), first=first
    )
    return pl.pallas_call(
        ordered(body, len(after)),
        grid=(end - begin,),
        in_specs=[ANYWHERE] * len(after)
        + [SCALARS]
        + [ANYWHERE] * sum(pieces)
        + [term] * 3
        + [weight] * 3
        + [columns] * len(chosen),
        out_specs=[result] * 3
        + [pl.BlockSpec((3, own_rows, tile), lambda i: (0, 0, i))]
        + [columns] * (2 if first else 0),
        out_shape=[shape((own_rows, out_hidden), F32)] * 3
        + [shape((3, own_rows, out_hidden), BF16)]
        + [shape((2 * own_rows, tokens), BF16)] * (2 if first else 0),
        scratch_shapes=[pltpu.VMEM((tokens, width), BF16)] * 2 + [pltpu.SemaphoreType.DMA((len(h2) + 2 * len(g) - 3,))],
        compiler_params=pltpu.CompilerParams(vmem_limit_bytes=VMEM_LIMIT),
        cost_estimate=cost(
            6 * tokens * (width + 2 * own_rows) * out_hidden,
            6 * width * out_hidden + 4 * tokens * width,
            tokens * out_hidden,
            scale=1,
        ),
        name="bulk_mlp",
    )(*after, ids, *h2, *g, *own_terms, *weights, *chosen)


def finish_kernel(*refs):
    first, second, theirs, outs = refs[:3], refs[3:6], refs[6:8], refs[8:]
    cut = first[0].shape[1]
    for i in range(3):
        outs[i][:, :cut] = first[i][...] + theirs[0][i].astype(F32)
        outs[i][:, cut:] = second[i][...] + theirs[1][i].astype(F32)


def bulk_finish(first, second, theirs_first, theirs_second):
    rows, first_hidden = first[0].shape
    second_hidden = second[0].shape[1]
    hidden = first_hidden + second_hidden
    block = rows // 3 if rows % 48 == 0 else rows

    def spec(columns):
        return pl.BlockSpec((block, columns), lambda i: (i, 0))

    def theirs_spec(columns):
        return pl.BlockSpec((3, block, columns), lambda i: (0, i, 0))

    return pl.pallas_call(
        finish_kernel,
        grid=(rows // block,),
        in_specs=[spec(first_hidden)] * 3
        + [spec(second_hidden)] * 3
        + [theirs_spec(first_hidden), theirs_spec(second_hidden)],
        out_specs=[spec(hidden)] * 3,
        out_shape=[shape((rows, hidden), F32)] * 3,
        compiler_params=pltpu.CompilerParams(vmem_limit_bytes=VMEM_LIMIT),
        cost_estimate=cost(rows * hidden, 30 * rows * hidden),
        name="bulk_finish",
    )(*first, *second, theirs_first, theirs_second)


def gains_kernel(a_ref, b_ref, attn_ref, mlp_ref, query_ref, key_ref):
    total = a_ref[...] + b_ref[...]
    width = attn_ref.shape[0]
    attn_ref[...] = total[:width]
    mlp_ref[...] = total[width : 2 * width]
    heads = total[2 * width :]
    key_ref[...] = heads[:64]
    query_ref[...] = heads[128:192] + heads[192:256] + heads[256:320]


def shards(
    tokens,
    w_query,
    w_key,
    w_value,
    w_output,
    w_gate,
    w_up,
    w_down,
    attn_gain,
    mlp_gain,
    query_gain,
    key_gain,
    segments,
    positions,
    cotangent,
):
    count = lax.axis_size("ctx")
    me = lax.axis_index("ctx")
    core = lax.axis_index("tp")
    nz = count // QUAD
    m = me % QUAD
    head = query_gain.shape[0]
    rows, model = tokens.shape
    q_heads = w_query.shape[1] // head
    kv_heads = w_key.shape[1] // head
    group = q_heads // kv_heads
    pair = rows // SEQS
    quad_rows = QUAD * rows
    columns = group * head
    own_rows = model // count
    flips = [flip_pairs(count, j) for j in range(QUAD)]
    ids = jnp.stack([me, core]).astype(jnp.int32)

    def quad_exchange(pieces):
        return [pieces[0]] + [send(pieces[j], flips[j]) for j in range(1, QUAD)]

    own_tokens = tokens.reshape(SEQS, pair, model)
    half = lax.dynamic_index_in_dim(own_tokens, core, 0, keepdims=False)
    mine = [send(half, flips[j]) for j in range(1, QUAD)]
    theirs = [swap_cores(p) for p in mine]

    freqs = ROPE_BASE ** (-2.0 * np.arange(head // 2) / head)
    freqs = jnp.asarray(np.tile(freqs, 4)[None, :], F32)
    bias, angles = kernel_call(
        mask_kernel,
        "visible",
        (ids, freqs, segments.reshape(count, SEQS * pair)),
        [shape((SEQS, count * pair, QUAD * pair), F32), shape((quad_rows, 2 * head), F32)],
        scalars=True,
    )
    sign = jnp.asarray(np.tile(np.repeat([-1.0, 1.0], head // 2), 2)[None, :], F32)
    cos, sin = jnp.cos(angles), jnp.sin(angles) * sign
    w_head = jnp.concatenate(
        [
            lax.dynamic_slice_in_dim(w_key, m * head, head, 1),
            lax.dynamic_slice_in_dim(w_value, m * head, head, 1),
            lax.dynamic_slice_in_dim(w_query, m * columns, columns, 1),
            jnp.zeros((model, head), BF16),
        ],
        axis=1,
    )
    h1, raw, q, kv_own, g_copy = kernel_call(
        qkv_kernel,
        "query_key_value",
        (
            ids,
            own_tokens,
            *mine,
            *theirs,
            attn_gain,
            w_head,
            key_gain,
            query_gain,
            cos,
            sin,
            cotangent,
        ),
        [
            shape((SEQS, QUAD, pair, model), BF16),
            shape((quad_rows, 6 * head), F32),
            shape((quad_rows, 4 * head), BF16),
            shape((quad_rows, 2 * head), BF16),
            shape((rows, model), BF16),
        ],
        flops=2 * quad_rows * model * 6 * head,
        scalars=True,
    )
    kv = [kv_own] + [send(kv_own, shift_pairs(count, s)) for s in range(1, nz)]
    hidden = w_down.shape[1]
    (da,) = hidden_call(
        hidden_grad_kernel,
        "hidden_grad",
        (cotangent, w_down),
        [shape((rows, hidden), F32)],
        after=(kv_own,),
    )
    g_blocks = [lax.ppermute(g_copy, ("ctx", "tp"), core_pairs(count))]

    def next_cotangents(after):
        g_blocks[-1] = touch(g_blocks[-1], after)
        g_blocks.append(send(g_blocks[-1], shift_pairs(count, 1)))

    *attn, lse = attention_forward(q, bias, kv, group, (da,))
    next_cotangents((lse,))
    attn_pieces = quad_exchange([a.reshape(rows, columns) for a in attn])
    branch = kernel_call(
        branch_kernel,
        "branch",
        (ids, *attn_pieces, w_output),
        [shape((rows // 2, model), BF16)] * 2,
        flops=2 * rows * model * w_output.shape[1],
        scalars=True,
        scratch=[pltpu.VMEM((QUAD, rows, columns), BF16)],
    )
    for _ in range(2, nz - 1):
        next_cotangents((branch[0],))
    middle, h2, h2_half = kernel_call(
        middle_kernel,
        "middle",
        (ids, tokens, *branch, *[swap_cores(b) for b in branch], mlp_gain),
        [shape((rows, model), F32), shape((rows, model), BF16), shape((rows // 2, model), BF16)],
        scalars=True,
    )
    h2_pieces = gather_column(h2_half, count)

    g_first = swap_cores(g_blocks[0])
    *dh2, act, dgate, dup = hidden_call(
        own_mlp_kernel,
        "own_mlp",
        (h2, da, w_gate, w_up),
        [shape((rows // 2, model), BF16)] * 2 + [shape((rows, hidden), BF16)] * 3,
        scratch=[pltpu.VMEM((model, rows), F32)],
        matmuls=4,
        after=(g_first,),
    )
    h2_packed = pack(h2_pieces, (act,))
    next_cotangents((act,))
    g_swapped = [g_first] + [swap_cores(g) for g in g_blocks[1:-1]]
    grad_middle, dy, dy_half, mlp_gain_part, *do = kernel_call(
        back_kernel,
        "back",
        (ids, middle, *dh2, *[swap_cores(d) for d in dh2], cotangent, mlp_gain, w_output),
        [
            shape((rows, model), F32),
            shape((rows, model), BF16),
            shape((rows // 2, model), BF16),
            shape((1, model), F32),
            *[shape((rows, columns), BF16)] * QUAD,
        ],
        flops=2 * rows * model * w_output.shape[1],
        scalars=True,
        scratch=[pltpu.VMEM((QUAD, rows, columns), BF16)],
        after=(h2_packed, *g_blocks[2:-1], *g_swapped[1:-1]),
    )
    do_pieces = [d.reshape(SEQS, pair, columns) for d in quad_exchange(do)]
    dy_half = touch(dy_half, do_pieces[1:])
    dy_mine = [send(dy_half, flips[j]) for j in range(1, QUAD)]
    dy_theirs = [swap_cores(p) for p in dy_mine]
    dy_pieces = (dy.reshape(SEQS, pair, model), *dy_mine, *dy_theirs)
    dq, *dkv = attention_backward(
        q, bias, lse, do_pieces, kv, (g_blocks[-1], *g_swapped[-1:])
    )
    h2_column = touch(h2_packed, (dq, *dy_mine))
    h2_other = send(h2_column, flips[2])
    (down,) = hidden_call(
        down_kernel,
        "down",
        (act, w_down),
        [shape((rows, model), BF16)],
        scratch=[pltpu.VMEM((model, rows), F32)],
        after=(dq,),
    )
    dkv = [dkv[0]] + [send(dkv[s], shift_pairs(count, nz - s)) for s in range(1, nz)]


    z_rows = model // nz
    head_part, *rest = kernel_call(
        head_grad_kernel,
        "head_grad",
        (ids, dq, raw, h1, *attn, *dy_pieces, key_gain, query_gain, cos, sin, *dkv),
        [
            shape((1, 6 * head), F32),
            *[shape((rows, 6 * head), BF16)] * QUAD,
            *[shape((z_rows, 8 * head), BF16)] * nz,
        ],
        flops=2 * quad_rows * model * 9 * head,
        scalars=True,
        scratch=[
            pltpu.VMEM((model, 8 * head), F32),
            pltpu.VMEM((SEQS, QUAD, pair, model), BF16),
        ],
        after=(down,),
    )
    grad_pieces, w_parts = quad_exchange(rest[:QUAD]), rest[QUAD:]
    w_parts = [w_parts[0]] + [send(w_parts[s], shift_pairs(count, nz - s)) for s in range(1, nz)]
    h2_column = touch(h2_column, (h2_other, head_part))
    h2_other = touch(h2_other, (h2_column,))
    g_blocks[-1] = touch(g_blocks[-1], (h2_column,))
    h2_rows = (h2_column, h2_other, swap_cores(h2_column), swap_cores(h2_other), h2)
    g_rows = (*g_blocks, *g_swapped, swap_cores(g_blocks[-1]), cotangent)

    tile = 512
    tiles = pl.cdiv(hidden, tile)
    cut = (2 * tiles + 2) // 3

    def bulk_part(chosen, begin, end, after):
        result = bulk_mlp(
            ids,
            h2_rows,
            g_rows,
            (act, dgate, dup),
            (w_gate, w_up, w_down),
            chosen,
            own_rows,
            begin,
            end,
            tile,
            after,
        )
        return result[:3], result[3], result[4:]

    bulk_first = bulk_part((), 0, cut, (head_part,))
    theirs_first = send(touch(bulk_first[1], grad_pieces[1:]), flips[1])
    bulk_second = bulk_part(bulk_first[2], cut, tiles, ())
    theirs_second = send(bulk_second[1], flips[1])
    after_bulk = (bulk_second[0][0],)
    down = touch(down, after_bulk)
    (output,) = kernel_call(
        output_kernel, "output", (middle, down, swap_cores(down)), [shape((rows, model), BF16)]
    )
    dh1, attn_gain_part = kernel_call(
        input_grad_kernel,
        "input_grad",
        (ids, *grad_pieces, tokens, w_query, w_key, w_value),
        [shape((rows, model), BF16), shape((1, model), F32)],
        flops=2 * rows * model * (q_heads + 2 * kv_heads) * head,
        scalars=True,
        scratch=[pltpu.VMEM((QUAD, rows, 6 * head), BF16)],
        after=after_bulk,
    )
    (grad_tokens,) = kernel_call(
        tokens_kernel,
        "tokens_grad",
        (tokens, grad_middle, dh1, swap_cores(dh1), attn_gain),
        [shape((rows, model), BF16)],
    )
    spread = kernel_call(
        spread_kernel,
        "spread",
        (ids, *w_parts),
        [shape((own_rows, 8 * head), F32)] + [shape((own_rows, 8 * head), BF16)] * (QUAD - 1),
        scalars=True,
        scratch=[pltpu.VMEM((z_rows, 8 * head), F32)],
        after=after_bulk,
    )
    gains = jnp.concatenate([attn_gain_part, 0.5 * mlp_gain_part, head_part], axis=1)[0]
    gains = gains + swap_cores(gains)
    gains = gains + send(gains, flips[2])
    fillers = [spread[0], output]
    for i in range(2, count.bit_length() - 1):
        gains = touch(gains, (fillers[min(i, 3) - 2],))
        gains = gains + send(gains, flip_pairs(count, 1 << i))
    gains = touch(gains, (grad_tokens,))
    grad_attn_gain, grad_mlp_gain, grad_query_gain, grad_key_gain = kernel_call(
        gains_kernel,
        "gains",
        (gains, send(gains, flips[1])),
        [shape((model,), F32)] * 2 + [shape((head,), F32)] * 2,
    )
    spread = quad_exchange(spread)
    grad_wq, grad_wk, grad_wv, grad_wo = kernel_call(
        assemble_kernel,
        "assemble",
        (ids, *spread),
        [
            shape((own_rows, q_heads * head), F32),
            shape((own_rows, kv_heads * head), F32),
            shape((own_rows, kv_heads * head), F32),
            shape((own_rows, q_heads * head), F32),
        ],
        scalars=True,
        scratch=[pltpu.VMEM((QUAD, own_rows, 8 * head), F32)],
    )

    mlp_grads = bulk_finish(bulk_first[0], bulk_second[0], theirs_first, theirs_second)
    return (
        output,
        grad_tokens,
        grad_wq,
        grad_wk,
        grad_wv,
        grad_wo,
        mlp_grads[0],
        mlp_grads[1],
        mlp_grads[2],
        grad_attn_gain,
        grad_mlp_gain,
        grad_query_gain,
        grad_key_gain,
    )


def solution(mesh):
    rows = P("ctx", None)
    columns = P(None, "tp")
    both = P("ctx", "tp")
    in_specs = (rows,) + (columns,) * 7 + (P(),) * 5 + (P("ctx"), rows)
    out_specs = (rows, rows) + (both,) * 7 + (P(),) * 4
    return jax.shard_map(shards, mesh=mesh, in_specs=in_specs, out_specs=out_specs, check_vma=False)
```

```python
import functools

import jax
import jax.numpy as jnp
import numpy as np
from jax import lax
from jax.experimental import pallas as pl
from jax.experimental.pallas import tpu as pltpu
from jax.sharding import PartitionSpec as P

BLK = 32
SEQS = 2
QUAD = 4
EPSILON = 1e-05
ROPE_BASE = 1000000.0
MASKED = -1e30
F32 = jnp.float32
BF16 = jnp.bfloat16
MIB = 1024 * 1024
VMEM_LIMIT = 56 * MIB
ROOMY = ("pack", "back", "spread", "head_grad", "middle",)


def dot(left, right):
    return jnp.dot(left, right, preferred_element_type=F32)


def contract_last(left, right):
    return lax.dot_general(left, right, (((1,), (1,)), ((), ())), preferred_element_type=F32)


def contract_first(left, right):
    return lax.dot_general(left, right, (((0,), (0,)), ((), ())), preferred_element_type=F32)


def shift_pairs(count, step):
    nz = count // QUAD
    return [(i, ((i // QUAD + step) % nz) * QUAD + i % QUAD) for i in range(count)]


def flip_pairs(count, bits):
    return [(i, i ^ bits) for i in range(count)]


def send(value, pairs):
    return lax.ppermute(value, "ctx", pairs)


def swap_cores(value):
    return lax.ppermute(value, "tp", [(0, 1), (1, 0)])


def core_pairs(count):
    return [pair for i in range(count) for pair in ((2 * i, 2 * i), (2 * i + 1, 2 * (i ^ 2) + 1))]


def gather_column(half, count):
    return [half] + [send(half, shift_pairs(count, s)) for s in range(1, count // QUAD)]


COST_SCALE = 0.01


def cost(flops, bytes_accessed, transcendentals=0, scale=COST_SCALE):
    return pl.CostEstimate(
        flops=int(flops * scale),
        bytes_accessed=int(bytes_accessed * scale),
        transcendentals=int(transcendentals * scale),
    )


SCALARS = pl.BlockSpec(memory_space=pltpu.SMEM)


ANYWHERE = pl.BlockSpec(memory_space=pl.ANY)


def ordered(body, extra):
    return lambda *refs: body(*refs[extra:])


def kernel_call(
    body, name, args, out_shape, flops=0, scalars=False, scratch=(), after=(), scale=COST_SCALE
):
    vmem = pl.BlockSpec(memory_space=pltpu.VMEM)
    roomy = name in ROOMY
    bytes_accessed = sum(a.size * a.dtype.itemsize for a in (*args, *out_shape))
    return pl.pallas_call(
        ordered(body, len(after)),
        in_specs=[ANYWHERE] * len(after)
        + [SCALARS if scalars and i == 0 else vmem for i in range(len(args))],
        out_specs=[vmem] * len(out_shape),
        out_shape=list(out_shape),
        scratch_shapes=list(scratch),
        compiler_params=pltpu.CompilerParams(
            vmem_limit_bytes=VMEM_LIMIT if roomy else min(3 * bytes_accessed + 8 * MIB, VMEM_LIMIT)
        ),
        cost_estimate=cost(flops, bytes_accessed, scale=scale),
        name=name,
    )(*after, *args)


def shape(dims, dtype):
    return jax.ShapeDtypeStruct(dims, dtype)


def pack_kernel(*refs):
    pieces, out_ref = refs[:-1], refs[-1]
    rows = pieces[0].shape[0]
    for i, piece in enumerate(pieces):
        out_ref[i * rows : (i + 1) * rows] = piece[...]


def pack(pieces, after=()):
    rows, width = pieces[0].shape
    out = shape((len(pieces) * rows, width), pieces[0].dtype)
    return kernel_call(pack_kernel, "pack", pieces, [out], after=after)[0]


def touch(value, after):
    return pl.pallas_call(
        lambda *refs: None,
        in_specs=[ANYWHERE] * (1 + len(after)),
        out_specs=ANYWHERE,
        out_shape=shape(value.shape, value.dtype),
        input_output_aliases={0: 0},
        name="touch",
    )(value, *after)


def row_factor(x):
    return lax.rsqrt(jnp.mean(x * x, axis=-1, keepdims=True) + EPSILON)


def head_means(x, blocks):
    high = x.astype(BF16)
    low = (x - high.astype(F32)).astype(BF16)
    return dot(high, blocks) + dot(low, blocks)


def head_blocks():
    row = lax.broadcasted_iota(jnp.int32, (128, 128), 0)
    col = lax.broadcasted_iota(jnp.int32, (128, 128), 1)
    return jnp.where(row // 64 == col // 64, 1.0 / 64, 0.0).astype(BF16)


def row_of(ref):
    return ref[...].reshape(1, -1)


def head_gain_rows(key_ref, query_ref):
    key, query = row_of(key_ref), row_of(query_ref)
    return jnp.concatenate([key, key], axis=1), jnp.concatenate([query, query], axis=1)


def lanes_of(x):
    return lax.broadcasted_iota(jnp.int32, x.shape, 1)


def partner(x):
    return jnp.where(lanes_of(x) % 64 < 32, pltpu.roll(x, 96, 1), pltpu.roll(x, 32, 1))


def mask_kernel(ids_ref, freq_ref, seg_ref, bias_ref, angle_ref):
    me = ids_ref[0]
    count = seg_ref.shape[0]
    nz = count // QUAD
    tokens = seg_ref.shape[1] // SEQS
    z, m = me // QUAD, me % QUAD

    def place(chip, offset):
        return jnp.where(offset < BLK, chip * BLK, (2 * count - 2 - chip) * BLK) + offset

    chips = [((z + nz - step) % nz) * QUAD + (m ^ j) for step in range(nz) for j in range(QUAD)]
    seg_rows = [seg_ref[pl.ds(chip, 1), :].astype(F32) for chip in chips]
    fill = jnp.zeros((128 - count, SEQS * tokens), F32)
    seg_cols = jnp.concatenate([*seg_rows, fill], axis=0).T
    row_offset = lax.broadcasted_iota(jnp.int32, (1, tokens), 1)
    col_offset = lax.broadcasted_iota(jnp.int32, (tokens, 1), 0)
    place_q = jnp.concatenate([place(chip, row_offset) for chip in chips[:QUAD]], axis=1)
    far = 2 * count * BLK
    for seq in range(SEQS):
        of_seq = slice(seq * tokens, (seq + 1) * tokens)
        seg_q = jnp.concatenate([row[:, of_seq] for row in seg_rows[:QUAD]], axis=1)
        first = jnp.full((tokens, QUAD * tokens), far, jnp.int32)
        for i, chip in enumerate(chips):
            place_k = place(chip, col_offset)
            same = seg_cols[of_seq, i : i + 1] == seg_q
            bias_ref[seq, i * tokens : (i + 1) * tokens, :] = jnp.where(
                same & (place_k <= place_q), 0.0, MASKED
            )
            first = jnp.minimum(first, jnp.where(same, place_k, far))
        position = (place_q - jnp.min(first, axis=0, keepdims=True)).astype(F32)
        rows = position.shape[1]
        angle_ref[seq * rows : (seq + 1) * rows, :] = (
            jnp.broadcast_to(position, (128, rows)).T * freq_ref[...]
        )


def qkv_kernel(ids_ref, own_ref, *refs):
    mine, theirs = refs[:3], refs[3:6]
    gain_ref, w_ref, key_gain_ref, query_gain_ref, cos_ref, sin_ref, g_ref = refs[6:13]
    h1_ref, raw_ref, q_ref, kv_ref, copy_ref = refs[13:]
    core = ids_ref[1]
    gain = row_of(gain_ref)
    copy_ref[...] = g_ref[...]

    def put(seq, j, piece):
        x = piece.astype(F32)
        h1_ref[seq, j] = (x * row_factor(x) * gain).astype(BF16)

    put(0, 0, own_ref[0])
    put(1, 0, own_ref[1])
    for j in range(1, QUAD):
        put(core, j, mine[j - 1][...])
        put(1 - core, j, theirs[j - 1][...])
    rows = raw_ref.shape[0]
    raw = dot(h1_ref[...].reshape(rows, -1), w_ref[...])
    raw_ref[...] = raw
    cos, sin, blocks = cos_ref[...], sin_ref[...], head_blocks()
    key_gain, query_gain = head_gain_rows(key_gain_ref, query_gain_ref)
    out = []
    for c in range(3):
        x = raw[:, 128 * c : 128 * (c + 1)]
        gain = key_gain if c == 0 else query_gain * 64 ** (-0.5)
        n = x * lax.rsqrt(head_means(x * x, blocks) + EPSILON) * gain
        out.append(n * cos + partner(n) * sin)
    kv_ref[...] = jnp.where(lanes_of(out[0]) < 64, out[0], raw[:, :128]).astype(BF16)
    q_ref[...] = jnp.concatenate(out[1:], axis=1).astype(BF16)


def head_lanes(x, g, upper):
    part = x[:, 128 * (g // 2) : 128 * (g // 2) + 128]
    if (g % 2 == 1) != upper:
        part = pltpu.roll(part, 64, 1)
    keep = (lanes_of(part) >= 64) if upper else (lanes_of(part) < 64)
    return jnp.where(keep, part, 0.0).astype(BF16)


def attention_forward_kernel(q_ref, bias_ref, *refs):
    kv_refs, o_refs, lse_ref = refs[: -QUAD - 1], refs[-QUAD - 1 : -1], refs[-1]
    group = lse_ref.shape[1]
    kv = jnp.concatenate([r[...] for r in kv_refs], axis=0)
    v_t = kv.T[64:]
    q = q_ref[...].astype(F32)
    bias = bias_ref[0]
    out = []
    for g in range(group):
        s = contract_last(kv, head_lanes(q, g, False)) + bias
        top = jnp.max(s, axis=0, keepdims=True)
        p = jnp.exp(s - top)
        total = jnp.sum(p, axis=0, keepdims=True)
        out.append(dot(v_t, p.astype(BF16)) / total)
        lse_ref[0, g] = top + jnp.log(total)
    o = jnp.concatenate(out, axis=0).T.astype(BF16)
    rows = o.shape[0] // QUAD
    for j in range(QUAD):
        o_refs[j][0] = o[j * rows : (j + 1) * rows]


def attention_backward_kernel(q_ref, bias_ref, lse_ref, *refs):
    do_refs, kv_refs, dq_ref, dkv_refs = refs[:QUAD], None, None, None
    rest = refs[QUAD:]
    pieces = (len(rest) - 1) // 2
    kv_refs, dq_ref, dkv_refs = rest[:pieces], rest[pieces], rest[pieces + 1 :]
    group = lse_ref.shape[1]
    kv = jnp.concatenate([r[...] for r in kv_refs], axis=0)
    k_t = kv.T[:64]
    q = q_ref[...].astype(F32)
    do = jnp.concatenate([r[0].astype(F32) for r in do_refs], axis=0)
    do = jnp.concatenate([do, jnp.zeros((do.shape[0], 64), F32)], axis=1)
    rows = q.shape[0]
    bias = bias_ref[0]
    total = jnp.zeros(kv.shape, F32)
    dq = []
    for g in range(group):
        both = jnp.concatenate([head_lanes(q, g, False), head_lanes(do, g, True)], axis=0)
        products = contract_last(kv, both)
        p = jnp.exp(products[:, :rows] + (bias - lse_ref[0, g]))
        dp = products[:, rows:]
        delta = jnp.sum(p * dp, axis=0, keepdims=True)
        ds = (p * (dp - delta)).astype(BF16)
        total = total + dot(jnp.concatenate([ds, p.astype(BF16)], axis=1), both)
        dq.append(dot(k_t, ds))
    dq.append(jnp.zeros(dq[0].shape, F32))
    dq_ref[...] = jnp.concatenate(dq, axis=0).T
    for i, ref in enumerate(dkv_refs):
        ref[...] = total[i * rows : (i + 1) * rows].astype(BF16)


def attention_specs(rows, keys, pieces):
    q = pl.BlockSpec((rows, 256), lambda s: (s, 0))
    bias = pl.BlockSpec((1, keys, rows), lambda s: (s, 0, 0))
    kv = [pl.BlockSpec((rows, 128), lambda s: (s, 0))] * pieces
    return q, bias, kv


def attention_forward(q, bias, kv, group, after):
    seqs, keys, rows = bias.shape
    q_spec, bias_spec, kv_specs = attention_specs(rows, keys, len(kv))
    work = seqs * group * keys * rows
    return pl.pallas_call(
        ordered(attention_forward_kernel, len(after)),
        grid=(seqs,),
        in_specs=[*[ANYWHERE] * len(after), q_spec, bias_spec, *kv_specs],
        out_specs=[
            *[pl.BlockSpec((1, rows // QUAD, group * 64), lambda s: (s, 0, 0))] * QUAD,
            pl.BlockSpec((1, group, 1, rows), lambda s: (s, 0, 0, 0)),
        ],
        out_shape=[
            *[shape((seqs, rows // QUAD, group * 64), BF16)] * QUAD,
            shape((seqs, group, 1, rows), F32),
        ],
        compiler_params=pltpu.CompilerParams(vmem_limit_bytes=VMEM_LIMIT),
        cost_estimate=cost(6 * work * 128, 4 * bias.size, work),
        name="attention_forward",
    )(*after, q, bias, *kv)


def attention_backward(q, bias, lse, do, kv, after=()):
    seqs, keys, rows = bias.shape
    group = lse.shape[1]
    q_spec, bias_spec, kv_specs = attention_specs(rows, keys, len(kv))
    work = seqs * group * keys * rows
    return pl.pallas_call(
        ordered(attention_backward_kernel, len(after)),
        grid=(seqs,),
        in_specs=[
            *[ANYWHERE] * len(after),
            q_spec,
            bias_spec,
            pl.BlockSpec((1, group, 1, rows), lambda s: (s, 0, 0, 0)),
            *[pl.BlockSpec((1, rows // QUAD, group * 64), lambda s: (s, 0, 0))] * QUAD,
            *kv_specs,
        ],
        out_specs=[q_spec, *kv_specs],
        out_shape=[shape(q.shape, F32)] + [shape(k.shape, BF16) for k in kv],
        compiler_params=pltpu.CompilerParams(vmem_limit_bytes=VMEM_LIMIT),
        cost_estimate=cost(10 * work * 128, 4 * bias.size, work),
        name="attention_backward",
    )(*after, q, bias, lse, *do, *kv)


def put_halves(refs, value):
    rows = refs[0].shape[0]
    for i, ref in enumerate(refs):
        ref[...] = value[i * rows : (i + 1) * rows].astype(ref.dtype)


def sum_halves(refs):
    own = jnp.concatenate([refs[0][...], refs[1][...]], axis=0).astype(F32)
    return own + jnp.concatenate([refs[2][...], refs[3][...]], axis=0).astype(F32)


def branch_kernel(ids_ref, *refs):
    pieces, w_ref, out_refs, stack_ref = refs[:QUAD], refs[QUAD], refs[QUAD + 1 : -1], refs[-1]
    m = ids_ref[0] % QUAD
    for j in range(QUAD):
        stack_ref[j] = pieces[j][...]
    attn = jnp.concatenate([stack_ref[m ^ k] for k in range(QUAD)], axis=1)
    put_halves(out_refs, contract_last(attn, w_ref[...]))


def middle_kernel(ids_ref, x_ref, *refs):
    branch_refs, (gain_ref, mid_ref, h2_ref, half_ref) = refs[:4], refs[4:]
    mid = x_ref[...].astype(F32) + sum_halves(branch_refs)
    mid_ref[...] = mid
    h2 = (mid * row_factor(mid) * row_of(gain_ref)).astype(BF16)
    h2_ref[...] = h2
    rows = half_ref.shape[0]
    half_ref[...] = jnp.where(ids_ref[1] == 0, h2[:rows], h2[rows:])


def hidden_terms(gate, up, da):
    sg = jax.nn.sigmoid(gate)
    silu = gate * sg
    act = (silu * up).astype(BF16)
    dgate = (da * up * (sg + silu * (1.0 - sg))).astype(BF16)
    dup = (da * silu).astype(BF16)
    return act, dgate, dup


def hidden_tile(hidden):
    return next(t for t in (1152, 384, 128, hidden) if hidden % t == 0)


def hidden_call(body, name, args, out_shape, scratch=(), matmuls=1, after=()):
    hidden = max(a.shape[-1] for a in args)
    tile = hidden_tile(hidden)

    def spec(a):
        if a.shape[-1] == hidden:
            return pl.BlockSpec((a.shape[0], tile), lambda i: (0, i))
        return pl.BlockSpec(a.shape, lambda i: (0, 0))

    rows, width = args[0].shape[0], 1536
    return pl.pallas_call(
        ordered(body, len(after)),
        grid=(hidden // tile,),
        in_specs=[ANYWHERE] * len(after) + [spec(a) for a in args],
        out_specs=[spec(o) for o in out_shape],
        out_shape=list(out_shape),
        scratch_shapes=list(scratch),
        compiler_params=pltpu.CompilerParams(vmem_limit_bytes=VMEM_LIMIT),
        cost_estimate=cost(
            4 * matmuls * rows * width * hidden,
            sum(a.size * a.dtype.itemsize for a in (*args, *out_shape)),
        ),
        name=name,
    )(*after, *args)


def accumulate(total_ref, out_refs, term):
    step = pl.program_id(0)

    @pl.when(step == 0)
    def _():
        total_ref[...] = term

    @pl.when(step > 0)
    def _():
        total_ref[...] += term

    @pl.when(step == pl.num_programs(0) - 1)
    def _():
        put_halves(out_refs, total_ref[...].T)


def hidden_grad_kernel(g_ref, wd_ref, da_ref):
    da_ref[...] = dot(g_ref[...], wd_ref[...])


def own_mlp_kernel(
    h2_ref, da_ref, wg_ref, wu_ref, dh_top_ref, dh_ref, act_ref, dgate_ref, dup_ref, total_ref
):
    wg, wu, h2 = wg_ref[...], wu_ref[...], h2_ref[...]
    act, dgate, dup = hidden_terms(dot(h2, wg), dot(h2, wu), da_ref[...])
    act_ref[...] = act
    dgate_ref[...] = dgate
    dup_ref[...] = dup
    accumulate(
        total_ref, (dh_top_ref, dh_ref), contract_last(wg, dgate) + contract_last(wu, dup)
    )


def down_kernel(act_ref, wd_ref, down_ref, total_ref):
    accumulate(total_ref, (down_ref,), contract_last(wd_ref[...], act_ref[...]))


def back_kernel(
    ids_ref, mid_ref, a_ref, b_ref, c_ref, d_ref, g_ref, gain_ref, w_ref, dx_ref, dy_ref, *refs
):
    half_ref, part_ref, do_refs = refs[0], refs[1], refs[2:]
    m = ids_ref[0] % QUAD
    stack_ref, do_refs = do_refs[-1], do_refs[:-1]
    mid = mid_ref[...]
    factor = row_factor(mid)
    dh2 = sum_halves((a_ref, b_ref, c_ref, d_ref))
    part_ref[...] = jnp.sum(dh2 * mid * factor, axis=0, keepdims=True)
    scaled = dh2 * row_of(gain_ref)
    inner = jnp.mean(mid * scaled, axis=-1, keepdims=True)
    dx = g_ref[...].astype(F32) + (factor * scaled - mid * (factor * factor * factor) * inner)
    dx_ref[...] = dx
    dy = dx.astype(BF16)
    dy_ref[...] = dy
    half = half_ref.shape[0]
    half_ref[...] = jnp.where(ids_ref[1] == 0, dy[:half], dy[half:])
    do = dot(dy, w_ref[...]).astype(BF16)
    columns = do.shape[1] // QUAD
    for k in range(QUAD):
        stack_ref[m ^ k] = do[:, k * columns : (k + 1) * columns]
    for j in range(QUAD):
        do_refs[j][...] = stack_ref[j]


def norm_rotate_back(grad, raw, gain, cos, sin, blocks):
    normed = grad * cos - partner(grad) * sin
    factor = lax.rsqrt(head_means(raw * raw, blocks) + EPSILON)
    scaled = normed * gain
    inner = head_means(raw * scaled, blocks)
    part = jnp.sum(normed * raw * factor, axis=0, keepdims=True)
    return factor * scaled - raw * (factor * factor * factor) * inner, part


def head_grad_kernel(ids_ref, dq_ref, raw_ref, h1_ref, *refs):
    attn_refs, dy_ref, mine, theirs, refs = refs[:4], refs[4], refs[5:8], refs[8:11], refs[11:]
    core = ids_ref[1]
    key_gain_ref, query_gain_ref, cos_ref, sin_ref, refs = *refs[:4], refs[4:]
    nz = (len(refs) - QUAD - 3) // 2
    dkv_refs, refs = refs[:nz], refs[nz:]
    part_ref, piece_refs, w_refs = refs[0], refs[1 : 1 + QUAD], refs[1 + QUAD : -2]
    total_ref, dy_all = refs[-2:]
    cos, sin, blocks = cos_ref[...], sin_ref[...], head_blocks()
    key_gain, query_gain = head_gain_rows(key_gain_ref, query_gain_ref)
    dkv = dkv_refs[0][...].astype(F32)
    for ref in dkv_refs[1:]:
        dkv = dkv + ref[...].astype(F32)
    scale = 64 ** (-0.5)
    low = []
    for c in range(3):
        lanes = slice(128 * c, 128 * (c + 1))
        given = dkv if c == 0 else dq_ref[:, 128 * (c - 1) : 128 * c] * scale
        gain = key_gain if c == 0 else query_gain
        grad, part = norm_rotate_back(given, raw_ref[:, lanes], gain, cos, sin, blocks)
        if c == 0:
            grad = jnp.where(lanes_of(grad) < 64, grad, dkv)
        part_ref[:, lanes] = part
        low.append(grad.astype(BF16))
    low = jnp.concatenate(low, axis=1)
    rows = low.shape[0]
    tokens = rows // (SEQS * QUAD)
    attn = []
    for seq in range(SEQS):
        for j in range(QUAD):
            begin = (seq * QUAD + j) * tokens
            piece_refs[j][seq * tokens : (seq + 1) * tokens] = low[begin : begin + tokens]
            if j == 0:
                dy_all[seq, j] = dy_ref[seq]
            attn.append(attn_refs[j][seq])
    for j in range(1, QUAD):
        dy_all[core, j] = mine[j - 1][...]
        dy_all[1 - core, j] = theirs[j - 1][...]
    columns = attn[0].shape[1]
    grad_wqkv = contract_first(h1_ref[...].reshape(rows, -1), low)
    grad_wo = contract_first(dy_all[...].reshape(rows, -1), jnp.concatenate(attn, axis=0))
    total_ref[...] = jnp.concatenate([grad_wqkv[:, : 128 + columns], grad_wo], axis=1)
    z = ids_ref[0] // QUAD
    owned = w_refs[0].shape[0]
    for step, ref in enumerate(w_refs):
        begin = pl.multiple_of(((z + nz - step) % nz) * owned, 8)
        ref[...] = total_ref[pl.ds(begin, owned), :].astype(BF16)


def spread_kernel(ids_ref, *refs):
    nz = len(refs) - QUAD - 1
    terms, (own_ref, *out_refs), total_ref = refs[:nz], refs[nz:-1], refs[-1]
    total = terms[0][...].astype(F32)
    for ref in terms[1:]:
        total = total + ref[...].astype(F32)
    total_ref[...] = total
    m = ids_ref[0] % QUAD
    rows = own_ref.shape[0]
    for j in range(QUAD):
        part = total_ref[pl.ds(pl.multiple_of((m ^ j) * rows, 8), rows), :]
        if j == 0:
            own_ref[...] = part
        else:
            out_refs[j - 1][...] = part.astype(BF16)


def assemble_kernel(ids_ref, own_ref, a_ref, b_ref, c_ref, wq_ref, wk_ref, wv_ref, wo_ref, stack_ref):
    m = ids_ref[0] % QUAD
    stack_ref[0] = own_ref[...]
    for j, ref in enumerate((a_ref, b_ref, c_ref)):
        stack_ref[j + 1] = ref[...].astype(F32)
    parts = [stack_ref[m ^ k] for k in range(QUAD)]
    columns = wq_ref.shape[1] // QUAD
    wk_ref[...] = jnp.concatenate([p[:, :64] for p in parts], axis=1)
    wv_ref[...] = jnp.concatenate([p[:, 64:128] for p in parts], axis=1)
    wq_ref[...] = jnp.concatenate([p[:, 128 : 128 + columns] for p in parts], axis=1)
    wo_ref[...] = jnp.concatenate([p[:, 128 + columns :] for p in parts], axis=1)


def input_grad_kernel(ids_ref, *refs):
    pieces, (x_ref, wq_ref, wk_ref, wv_ref, out_ref, part_ref, stack_ref) = refs[:QUAD], refs[QUAD:]
    m = ids_ref[0] % QUAD
    for j in range(QUAD):
        stack_ref[j] = pieces[j][...]
    parts = [stack_ref[m ^ k] for k in range(QUAD)]
    columns = wq_ref.shape[1] // QUAD
    dk = jnp.concatenate([p[:, :64] for p in parts], axis=1)
    dv = jnp.concatenate([p[:, 64:128] for p in parts], axis=1)
    dq = jnp.concatenate([p[:, 128 : 128 + columns] for p in parts], axis=1)
    total = (
        contract_last(dq, wq_ref[...])
        + contract_last(dk, wk_ref[...])
        + contract_last(dv, wv_ref[...])
    )
    out_ref[...] = total.astype(BF16)
    x = x_ref[...].astype(F32)
    part_ref[...] = jnp.sum(total * x * row_factor(x), axis=0, keepdims=True)


def tokens_kernel(x_ref, dx_ref, a_ref, b_ref, gain_ref, out_ref):
    x = x_ref[...].astype(F32)
    factor = row_factor(x)
    scaled = (a_ref[...].astype(F32) + b_ref[...].astype(F32)) * row_of(gain_ref)
    inner = jnp.mean(x * scaled, axis=-1, keepdims=True)
    back = factor * scaled - x * (factor * factor * factor) * inner
    out_ref[...] = (dx_ref[...] + back).astype(BF16)


def output_kernel(mid_ref, a_ref, b_ref, out_ref):
    out_ref[...] = (mid_ref[...] + (a_ref[...].astype(F32) + b_ref[...].astype(F32))).astype(BF16)


def bulk_mlp_kernel(ids_ref, *refs, pieces, row_tile, first):
    sides, refs = (refs[: pieces[0]], refs[pieces[0] : sum(pieces)]), refs[sum(pieces) :]
    act_ref, dgate_ref, dup_ref, wg_ref, wu_ref, wd_ref, refs = *refs[:6], refs[6:]
    if first:
        own_refs, other_ref, h2c_ref, gc_ref, h2_ref, g_ref, sems = refs[:3], *refs[3:]
    else:
        h2c_ref, gc_ref, own_refs, other_ref, h2_ref, g_ref, sems = *refs[:2], refs[2:5], *refs[5:]
    rows = act_ref.shape[0]
    tokens, width = h2_ref.shape
    own_rows = own_refs[0].shape[0]
    pair_rows = 2 * own_rows

    @pl.when(pl.program_id(0) == 0)
    def _():
        half = rows // 2
        places = pieces[1] // 2
        copies = []

        def copy_rows(source, skip, size, target, begin, sem):
            return pltpu.make_async_copy(
                source.at[pl.ds(skip, size)], target.at[pl.ds(begin, size)], sems.at[sem]
            )

        begin = 0
        for i, source in enumerate(sides[0]):
            skip = half if i in (0, 2) else 0
            copies.append(copy_rows(source, skip, source.shape[0] - skip, h2_ref, begin, i))
            begin += source.shape[0] - skip
        for copy in copies:
            copy.start()
        for core in range(2):

            @pl.when(ids_ref[1] == core)
            def _():
                own_y, other_y = sides[1][:places], sides[1][places : 2 * places]
                if core == 1:
                    own_y, other_y = other_y, own_y
                blocks = [*own_y[1:], *other_y]
                for i, source in enumerate(blocks):
                    for part in range(2):
                        to = (i + part * len(blocks)) * half
                        sem = len(sides[0]) + 2 * i + part
                        copy_rows(source, (core ^ part) * half, half, g_ref, to, sem).start()
                last = len(sides[0]) + 4 * places - 2
                copy_rows(sides[1][-1], 0, rows, g_ref, tokens - rows, last).start()

        for i in range(2 * (2 * places - 1)):
            copies.append(copy_rows(sides[1][0], 0, half, g_ref, 0, len(sides[0]) + i))
        last = len(sides[0]) + 4 * places - 2
        copies.append(copy_rows(sides[1][-1], 0, rows, g_ref, tokens - rows, last))
        if first:
            me = ids_ref[0]
            row = lax.broadcasted_iota(jnp.int32, (width, pair_rows), 0)
            col = lax.broadcasted_iota(jnp.int32, (width, pair_rows), 1)
            target = jnp.where(col < own_rows, me * own_rows + col, ((me ^ 1) - 1) * own_rows + col)
            chosen = jnp.where(row == target, 1.0, 0.0).astype(BF16)
        for copy in copies:
            copy.wait()
        if first:
            h2c_ref[...] = dot(h2_ref[...], chosen).T.astype(BF16)
            gc_ref[...] = dot(g_ref[...], chosen).T.astype(BF16)

    wg, wu, wd = wg_ref[...], wu_ref[...], wd_ref[...]
    last = slice(tokens - rows, tokens)
    totals = [
        dot(left[:, last], term[...])
        for left, term in ((h2c_ref, dgate_ref), (h2c_ref, dup_ref), (gc_ref, act_ref))
    ]
    for begin in range(0, tokens - rows, row_tile):
        part = slice(begin, min(begin + row_tile, tokens - rows))
        h2 = h2_ref[part]
        act, dgate, dup = hidden_terms(dot(h2, wg), dot(h2, wu), dot(g_ref[part], wd))
        h2c, gc = h2c_ref[:, part], gc_ref[:, part]
        terms = [dot(h2c, dgate), dot(h2c, dup), dot(gc, act)]
        totals = [a + b for a, b in zip(totals, terms)]
    for i, (own, total) in enumerate(zip(own_refs, totals)):
        own[...] = total[:own_rows]
        other_ref[i] = total[own_rows:].astype(BF16)


def bulk_mlp(ids, h2, g, own_terms, weights, chosen, own_rows, begin, end, tile, after):
    width = h2[0].shape[1]
    rows, hidden = own_terms[0].shape
    tokens = sum(piece.shape[0] for piece in h2) - rows
    out_hidden = min(end * tile, hidden) - begin * tile
    weight = pl.BlockSpec((width, tile), lambda i: (0, i + begin))
    term = pl.BlockSpec((rows, tile), lambda i: (0, i + begin))
    result = pl.BlockSpec((own_rows, tile), lambda i: (0, i))
    columns = pl.BlockSpec((2 * own_rows, tokens), lambda i: (0, 0))
    first = not chosen
    pieces = (len(h2), len(g))
    body = functools.partial(
        bulk_mlp_kernel, pieces=pieces, row_tile=min(tokens, 1024), first=first
    )
    return pl.pallas_call(
        ordered(body, len(after)),
        grid=(end - begin,),
        in_specs=[ANYWHERE] * len(after)
        + [SCALARS]
        + [ANYWHERE] * sum(pieces)
        + [term] * 3
        + [weight] * 3
        + [columns] * len(chosen),
        out_specs=[result] * 3
        + [pl.BlockSpec((3, own_rows, tile), lambda i: (0, 0, i))]
        + [columns] * (2 if first else 0),
        out_shape=[shape((own_rows, out_hidden), F32)] * 3
        + [shape((3, own_rows, out_hidden), BF16)]
        + [shape((2 * own_rows, tokens), BF16)] * (2 if first else 0),
        scratch_shapes=[pltpu.VMEM((tokens, width), BF16)] * 2 + [pltpu.SemaphoreType.DMA((len(h2) + 2 * len(g) - 3,))],
        compiler_params=pltpu.CompilerParams(vmem_limit_bytes=VMEM_LIMIT),
        cost_estimate=cost(
            6 * tokens * (width + 2 * own_rows) * out_hidden,
            6 * width * out_hidden + 4 * tokens * width,
            tokens * out_hidden,
            scale=1,
        ),
        name="bulk_mlp",
    )(*after, ids, *h2, *g, *own_terms, *weights, *chosen)


def finish_kernel(*refs):
    first, second, theirs, outs = refs[:3], refs[3:6], refs[6:8], refs[8:]
    cut = first[0].shape[1]
    for i in range(3):
        outs[i][:, :cut] = first[i][...] + theirs[0][i].astype(F32)
        outs[i][:, cut:] = second[i][...] + theirs[1][i].astype(F32)


def bulk_finish(first, second, theirs_first, theirs_second):
    rows, first_hidden = first[0].shape
    second_hidden = second[0].shape[1]
    hidden = first_hidden + second_hidden
    block = rows // 3 if rows % 48 == 0 else rows

    def spec(columns):
        return pl.BlockSpec((block, columns), lambda i: (i, 0))

    def theirs_spec(columns):
        return pl.BlockSpec((3, block, columns), lambda i: (0, i, 0))

    return pl.pallas_call(
        finish_kernel,
        grid=(rows // block,),
        in_specs=[spec(first_hidden)] * 3
        + [spec(second_hidden)] * 3
        + [theirs_spec(first_hidden), theirs_spec(second_hidden)],
        out_specs=[spec(hidden)] * 3,
        out_shape=[shape((rows, hidden), F32)] * 3,
        compiler_params=pltpu.CompilerParams(vmem_limit_bytes=VMEM_LIMIT),
        cost_estimate=cost(rows * hidden, 30 * rows * hidden),
        name="bulk_finish",
    )(*first, *second, theirs_first, theirs_second)


def gains_kernel(a_ref, b_ref, attn_ref, mlp_ref, query_ref, key_ref):
    total = a_ref[...] + b_ref[...]
    width = attn_ref.shape[0]
    attn_ref[...] = total[:width]
    mlp_ref[...] = total[width : 2 * width]
    heads = total[2 * width :]
    key_ref[...] = heads[:64]
    query_ref[...] = heads[128:192] + heads[192:256] + heads[256:320]


def shards(
    tokens,
    w_query,
    w_key,
    w_value,
    w_output,
    w_gate,
    w_up,
    w_down,
    attn_gain,
    mlp_gain,
    query_gain,
    key_gain,
    segments,
    positions,
    cotangent,
):
    count = lax.axis_size("ctx")
    me = lax.axis_index("ctx")
    core = lax.axis_index("tp")
    nz = count // QUAD
    m = me % QUAD
    head = query_gain.shape[0]
    rows, model = tokens.shape
    q_heads = w_query.shape[1] // head
    kv_heads = w_key.shape[1] // head
    group = q_heads // kv_heads
    pair = rows // SEQS
    quad_rows = QUAD * rows
    columns = group * head
    own_rows = model // count
    flips = [flip_pairs(count, j) for j in range(QUAD)]
    ids = jnp.stack([me, core]).astype(jnp.int32)

    def quad_exchange(pieces):
        return [pieces[0]] + [send(pieces[j], flips[j]) for j in range(1, QUAD)]

    own_tokens = tokens.reshape(SEQS, pair, model)
    half = lax.dynamic_index_in_dim(own_tokens, core, 0, keepdims=False)
    mine = [send(half, flips[j]) for j in range(1, QUAD)]
    theirs = [swap_cores(p) for p in mine]

    freqs = ROPE_BASE ** (-2.0 * np.arange(head // 2) / head)
    freqs = jnp.asarray(np.tile(freqs, 4)[None, :], F32)
    bias, angles = kernel_call(
        mask_kernel,
        "visible",
        (ids, freqs, segments.reshape(count, SEQS * pair)),
        [shape((SEQS, count * pair, QUAD * pair), F32), shape((quad_rows, 2 * head), F32)],
        scalars=True,
    )
    sign = jnp.asarray(np.tile(np.repeat([-1.0, 1.0], head // 2), 2)[None, :], F32)
    cos, sin = jnp.cos(angles), jnp.sin(angles) * sign
    w_head = jnp.concatenate(
        [
            lax.dynamic_slice_in_dim(w_key, m * head, head, 1),
            lax.dynamic_slice_in_dim(w_value, m * head, head, 1),
            lax.dynamic_slice_in_dim(w_query, m * columns, columns, 1),
            jnp.zeros((model, head), BF16),
        ],
        axis=1,
    )
    h1, raw, q, kv_own, g_copy = kernel_call(
        qkv_kernel,
        "query_key_value",
        (
            ids,
            own_tokens,
            *mine,
            *theirs,
            attn_gain,
            w_head,
            key_gain,
            query_gain,
            cos,
            sin,
            cotangent,
        ),
        [
            shape((SEQS, QUAD, pair, model), BF16),
            shape((quad_rows, 6 * head), F32),
            shape((quad_rows, 4 * head), BF16),
            shape((quad_rows, 2 * head), BF16),
            shape((rows, model), BF16),
        ],
        flops=2 * quad_rows * model * 6 * head,
        scalars=True,
    )
    kv = [kv_own] + [send(kv_own, shift_pairs(count, s)) for s in range(1, nz)]
    hidden = w_down.shape[1]
    (da,) = hidden_call(
        hidden_grad_kernel,
        "hidden_grad",
        (cotangent, w_down),
        [shape((rows, hidden), F32)],
        after=(kv_own,),
    )
    g_blocks = [lax.ppermute(g_copy, ("ctx", "tp"), core_pairs(count))]

    def next_cotangents(after):
        g_blocks[-1] = touch(g_blocks[-1], after)
        g_blocks.append(send(g_blocks[-1], shift_pairs(count, 1)))

    *attn, lse = attention_forward(q, bias, kv, group, (da,))
    next_cotangents((lse,))
    attn_pieces = quad_exchange([a.reshape(rows, columns) for a in attn])
    branch = kernel_call(
        branch_kernel,
        "branch",
        (ids, *attn_pieces, w_output),
        [shape((rows // 2, model), BF16)] * 2,
        flops=2 * rows * model * w_output.shape[1],
        scalars=True,
        scratch=[pltpu.VMEM((QUAD, rows, columns), BF16)],
    )
    middle, h2, h2_half = kernel_call(
        middle_kernel,
        "middle",
        (ids, tokens, *branch, *[swap_cores(b) for b in branch], mlp_gain),
        [shape((rows, model), F32), shape((rows, model), BF16), shape((rows // 2, model), BF16)],
        scalars=True,
    )
    h2_pieces = gather_column(h2_half, count)

    g_first = swap_cores(g_blocks[0])
    *dh2, act, dgate, dup = hidden_call(
        own_mlp_kernel,
        "own_mlp",
        (h2, da, w_gate, w_up),
        [shape((rows // 2, model), BF16)] * 2 + [shape((rows, hidden), BF16)] * 3,
        scratch=[pltpu.VMEM((model, rows), F32)],
        matmuls=4,
        after=(g_first,),
    )
    h2_packed = pack(h2_pieces, (act,))
    g_blocks[1] = touch(g_blocks[1], (h2,))
    g_second = swap_cores(g_blocks[1])
    for _ in range(2, nz - 1):
        next_cotangents((act,))
    grad_middle, dy, dy_half, mlp_gain_part, *do = kernel_call(
        back_kernel,
        "back",
        (ids, middle, *dh2, *[swap_cores(d) for d in dh2], cotangent, mlp_gain, w_output),
        [
            shape((rows, model), F32),
            shape((rows, model), BF16),
            shape((rows // 2, model), BF16),
            shape((1, model), F32),
            *[shape((rows, columns), BF16)] * QUAD,
        ],
        flops=2 * rows * model * w_output.shape[1],
        scalars=True,
        scratch=[pltpu.VMEM((QUAD, rows, columns), BF16)],
        after=(h2_packed, g_second),
    )
    do_pieces = [d.reshape(SEQS, pair, columns) for d in quad_exchange(do)]
    dy_half = touch(dy_half, do_pieces[1:])
    dy_mine = [send(dy_half, flips[j]) for j in range(1, QUAD)]
    dy_theirs = [swap_cores(p) for p in dy_mine]
    dy_pieces = (dy.reshape(SEQS, pair, model), *dy_mine, *dy_theirs)
    dq, *dkv = attention_backward(
        q, bias, lse, do_pieces, kv, (g_blocks[-1],)
    )
    next_cotangents((dq,))
    g_swapped = [g_first, g_second] + [swap_cores(g) for g in g_blocks[2:-1]]
    h2_column = touch(h2_packed, (dq, *dy_mine))
    h2_other = send(h2_column, flips[2])
    (down,) = hidden_call(
        down_kernel,
        "down",
        (act, w_down),
        [shape((rows, model), BF16)],
        scratch=[pltpu.VMEM((model, rows), F32)],
        after=(dq,),
    )
    dkv = [dkv[0]] + [send(dkv[s], shift_pairs(count, nz - s)) for s in range(1, nz)]


    z_rows = model // nz
    head_part, *rest = kernel_call(
        head_grad_kernel,
        "head_grad",
        (ids, dq, raw, h1, *attn, *dy_pieces, key_gain, query_gain, cos, sin, *dkv),
        [
            shape((1, 6 * head), F32),
            *[shape((rows, 6 * head), BF16)] * QUAD,
            *[shape((z_rows, 8 * head), BF16)] * nz,
        ],
        flops=2 * quad_rows * model * 9 * head,
        scalars=True,
        scratch=[
            pltpu.VMEM((model, 8 * head), F32),
            pltpu.VMEM((SEQS, QUAD, pair, model), BF16),
        ],
        after=(down,),
    )
    grad_pieces, w_parts = quad_exchange(rest[:QUAD]), rest[QUAD:]
    w_parts = [w_parts[0]] + [send(w_parts[s], shift_pairs(count, nz - s)) for s in range(1, nz)]
    h2_column = touch(h2_column, (h2_other, head_part))
    h2_other = touch(h2_other, (h2_column,))
    g_blocks[-1] = touch(g_blocks[-1], (h2_column,))
    h2_rows = (h2_column, h2_other, swap_cores(h2_column), swap_cores(h2_other), h2)
    g_rows = (*g_blocks, *g_swapped, swap_cores(g_blocks[-1]), cotangent)

    tile = 512
    tiles = pl.cdiv(hidden, tile)
    cut = (2 * tiles + 2) // 3

    def bulk_part(chosen, begin, end, after):
        result = bulk_mlp(
            ids,
            h2_rows,
            g_rows,
            (act, dgate, dup),
            (w_gate, w_up, w_down),
            chosen,
            own_rows,
            begin,
            end,
            tile,
            after,
        )
        return result[:3], result[3], result[4:]

    bulk_first = bulk_part((), 0, cut, (head_part,))
    theirs_first = send(touch(bulk_first[1], grad_pieces[1:]), flips[1])
    bulk_second = bulk_part(bulk_first[2], cut, tiles, ())
    theirs_second = send(bulk_second[1], flips[1])
    after_bulk = (bulk_second[0][0],)
    down = touch(down, after_bulk)
    (output,) = kernel_call(
        output_kernel, "output", (middle, down, swap_cores(down)), [shape((rows, model), BF16)]
    )
    dh1, attn_gain_part = kernel_call(
        input_grad_kernel,
        "input_grad",
        (ids, *grad_pieces, tokens, w_query, w_key, w_value),
        [shape((rows, model), BF16), shape((1, model), F32)],
        flops=2 * rows * model * (q_heads + 2 * kv_heads) * head,
        scalars=True,
        scratch=[pltpu.VMEM((QUAD, rows, 6 * head), BF16)],
        after=after_bulk,
    )
    (grad_tokens,) = kernel_call(
        tokens_kernel,
        "tokens_grad",
        (tokens, grad_middle, dh1, swap_cores(dh1), attn_gain),
        [shape((rows, model), BF16)],
    )
    spread = kernel_call(
        spread_kernel,
        "spread",
        (ids, *w_parts),
        [shape((own_rows, 8 * head), F32)] + [shape((own_rows, 8 * head), BF16)] * (QUAD - 1),
        scalars=True,
        scratch=[pltpu.VMEM((z_rows, 8 * head), F32)],
        after=after_bulk,
    )
    gains = jnp.concatenate([attn_gain_part, 0.5 * mlp_gain_part, head_part], axis=1)[0]
    gains = gains + swap_cores(gains)
    gains = gains + send(gains, flips[2])
    fillers = [spread[0], output]
    for i in range(2, count.bit_length() - 1):
        gains = touch(gains, (fillers[min(i, 3) - 2],))
        gains = gains + send(gains, flip_pairs(count, 1 << i))
    gains = touch(gains, (grad_tokens,))
    grad_attn_gain, grad_mlp_gain, grad_query_gain, grad_key_gain = kernel_call(
        gains_kernel,
        "gains",
        (gains, send(gains, flips[1])),
        [shape((model,), F32)] * 2 + [shape((head,), F32)] * 2,
    )
    spread = quad_exchange(spread)
    grad_wq, grad_wk, grad_wv, grad_wo = kernel_call(
        assemble_kernel,
        "assemble",
        (ids, *spread),
        [
            shape((own_rows, q_heads * head), F32),
            shape((own_rows, kv_heads * head), F32),
            shape((own_rows, kv_heads * head), F32),
            shape((own_rows, q_heads * head), F32),
        ],
        scalars=True,
        scratch=[pltpu.VMEM((QUAD, own_rows, 8 * head), F32)],
    )

    mlp_grads = bulk_finish(bulk_first[0], bulk_second[0], theirs_first, theirs_second)
    return (
        output,
        grad_tokens,
        grad_wq,
        grad_wk,
        grad_wv,
        grad_wo,
        mlp_grads[0],
        mlp_grads[1],
        mlp_grads[2],
        grad_attn_gain,
        grad_mlp_gain,
        grad_query_gain,
        grad_key_gain,
    )


def solution(mesh):
    rows = P("ctx", None)
    columns = P(None, "tp")
    both = P("ctx", "tp")
    in_specs = (rows,) + (columns,) * 7 + (P(),) * 5 + (P("ctx"), rows)
    out_specs = (rows, rows) + (both,) * 7 + (P(),) * 4
    return jax.shard_map(shards, mesh=mesh, in_specs=in_specs, out_specs=out_specs, check_vma=False)
```

```python
import functools

import jax
import jax.numpy as jnp
import numpy as np
from jax import lax
from jax.experimental import pallas as pl
from jax.experimental.pallas import tpu as pltpu
from jax.sharding import PartitionSpec as P

BLK = 32
SEQS = 2
QUAD = 4
EPSILON = 1e-05
ROPE_BASE = 1000000.0
MASKED = -1e30
F32 = jnp.float32
BF16 = jnp.bfloat16
MIB = 1024 * 1024
VMEM_LIMIT = 56 * MIB
ROOMY = ("pack", "back", "spread", "head_grad", "middle",)


def dot(left, right):
    return jnp.dot(left, right, preferred_element_type=F32)


def contract_last(left, right):
    return lax.dot_general(left, right, (((1,), (1,)), ((), ())), preferred_element_type=F32)


def contract_first(left, right):
    return lax.dot_general(left, right, (((0,), (0,)), ((), ())), preferred_element_type=F32)


def shift_pairs(count, step):
    nz = count // QUAD
    return [(i, ((i // QUAD + step) % nz) * QUAD + i % QUAD) for i in range(count)]


def flip_pairs(count, bits):
    return [(i, i ^ bits) for i in range(count)]


def send(value, pairs):
    return lax.ppermute(value, "ctx", pairs)


def swap_cores(value):
    return lax.ppermute(value, "tp", [(0, 1), (1, 0)])


def core_pairs(count):
    return [pair for i in range(count) for pair in ((2 * i, 2 * i), (2 * i + 1, 2 * (i ^ 2) + 1))]


def gather_column(half, count):
    return [half] + [send(half, shift_pairs(count, s)) for s in range(1, count // QUAD)]


COST_SCALE = 0.01


def cost(flops, bytes_accessed, transcendentals=0, scale=COST_SCALE):
    return pl.CostEstimate(
        flops=int(flops * scale),
        bytes_accessed=int(bytes_accessed * scale),
        transcendentals=int(transcendentals * scale),
    )


SCALARS = pl.BlockSpec(memory_space=pltpu.SMEM)


ANYWHERE = pl.BlockSpec(memory_space=pl.ANY)


def ordered(body, extra):
    return lambda *refs: body(*refs[extra:])


def kernel_call(
    body, name, args, out_shape, flops=0, scalars=False, scratch=(), after=(), scale=COST_SCALE
):
    vmem = pl.BlockSpec(memory_space=pltpu.VMEM)
    roomy = name in ROOMY
    bytes_accessed = sum(a.size * a.dtype.itemsize for a in (*args, *out_shape))
    return pl.pallas_call(
        ordered(body, len(after)),
        in_specs=[ANYWHERE] * len(after)
        + [SCALARS if scalars and i == 0 else vmem for i in range(len(args))],
        out_specs=[vmem] * len(out_shape),
        out_shape=list(out_shape),
        scratch_shapes=list(scratch),
        compiler_params=pltpu.CompilerParams(
            vmem_limit_bytes=VMEM_LIMIT if roomy else min(3 * bytes_accessed + 8 * MIB, VMEM_LIMIT)
        ),
        cost_estimate=cost(flops, bytes_accessed, scale=scale),
        name=name,
    )(*after, *args)


def shape(dims, dtype):
    return jax.ShapeDtypeStruct(dims, dtype)


def pack_kernel(*refs):
    pieces, out_ref = refs[:-1], refs[-1]
    rows = pieces[0].shape[0]
    for i, piece in enumerate(pieces):
        out_ref[i * rows : (i + 1) * rows] = piece[...]


def pack(pieces, after=()):
    rows, width = pieces[0].shape
    out = shape((len(pieces) * rows, width), pieces[0].dtype)
    return kernel_call(pack_kernel, "pack", pieces, [out], after=after)[0]


def touch(value, after):
    return pl.pallas_call(
        lambda *refs: None,
        in_specs=[ANYWHERE] * (1 + len(after)),
        out_specs=ANYWHERE,
        out_shape=shape(value.shape, value.dtype),
        input_output_aliases={0: 0},
        name="touch",
    )(value, *after)


def row_factor(x):
    return lax.rsqrt(jnp.mean(x * x, axis=-1, keepdims=True) + EPSILON)


def head_means(x, blocks):
    high = x.astype(BF16)
    low = (x - high.astype(F32)).astype(BF16)
    return dot(high, blocks) + dot(low, blocks)


def head_blocks():
    row = lax.broadcasted_iota(jnp.int32, (128, 128), 0)
    col = lax.broadcasted_iota(jnp.int32, (128, 128), 1)
    return jnp.where(row // 64 == col // 64, 1.0 / 64, 0.0).astype(BF16)


def row_of(ref):
    return ref[...].reshape(1, -1)


def head_gain_rows(key_ref, query_ref):
    key, query = row_of(key_ref), row_of(query_ref)
    return jnp.concatenate([key, key], axis=1), jnp.concatenate([query, query], axis=1)


def lanes_of(x):
    return lax.broadcasted_iota(jnp.int32, x.shape, 1)


def partner(x):
    return jnp.where(lanes_of(x) % 64 < 32, pltpu.roll(x, 96, 1), pltpu.roll(x, 32, 1))


def mask_kernel(ids_ref, freq_ref, seg_ref, bias_ref, angle_ref):
    me = ids_ref[0]
    count = seg_ref.shape[0]
    nz = count // QUAD
    tokens = seg_ref.shape[1] // SEQS
    z, m = me // QUAD, me % QUAD

    def place(chip, offset):
        return jnp.where(offset < BLK, chip * BLK, (2 * count - 2 - chip) * BLK) + offset

    chips = [((z + nz - step) % nz) * QUAD + (m ^ j) for step in range(nz) for j in range(QUAD)]
    seg_rows = [seg_ref[pl.ds(chip, 1), :].astype(F32) for chip in chips]
    fill = jnp.zeros((128 - count, SEQS * tokens), F32)
    seg_cols = jnp.concatenate([*seg_rows, fill], axis=0).T
    row_offset = lax.broadcasted_iota(jnp.int32, (1, tokens), 1)
    col_offset = lax.broadcasted_iota(jnp.int32, (tokens, 1), 0)
    place_q = jnp.concatenate([place(chip, row_offset) for chip in chips[:QUAD]], axis=1)
    far = 2 * count * BLK
    for seq in range(SEQS):
        of_seq = slice(seq * tokens, (seq + 1) * tokens)
        seg_q = jnp.concatenate([row[:, of_seq] for row in seg_rows[:QUAD]], axis=1)
        first = jnp.full((tokens, QUAD * tokens), far, jnp.int32)
        for i, chip in enumerate(chips):
            place_k = place(chip, col_offset)
            same = seg_cols[of_seq, i : i + 1] == seg_q
            bias_ref[seq, i * tokens : (i + 1) * tokens, :] = jnp.where(
                same & (place_k <= place_q), 0.0, MASKED
            )
            first = jnp.minimum(first, jnp.where(same, place_k, far))
        position = (place_q - jnp.min(first, axis=0, keepdims=True)).astype(F32)
        rows = position.shape[1]
        angle_ref[seq * rows : (seq + 1) * rows, :] = (
            jnp.broadcast_to(position, (128, rows)).T * freq_ref[...]
        )


def qkv_kernel(ids_ref, own_ref, *refs):
    mine, theirs = refs[:3], refs[3:6]
    gain_ref, w_ref, key_gain_ref, query_gain_ref, cos_ref, sin_ref, g_ref = refs[6:13]
    h1_ref, raw_ref, q_ref, kv_ref, copy_ref = refs[13:]
    core = ids_ref[1]
    gain = row_of(gain_ref)
    copy_ref[...] = g_ref[...]

    def put(seq, j, piece):
        x = piece.astype(F32)
        h1_ref[seq, j] = (x * row_factor(x) * gain).astype(BF16)

    put(0, 0, own_ref[0])
    put(1, 0, own_ref[1])
    for j in range(1, QUAD):
        put(core, j, mine[j - 1][...])
        put(1 - core, j, theirs[j - 1][...])
    rows = raw_ref.shape[0]
    raw = dot(h1_ref[...].reshape(rows, -1), w_ref[...])
    raw_ref[...] = raw
    cos, sin, blocks = cos_ref[...], sin_ref[...], head_blocks()
    key_gain, query_gain = head_gain_rows(key_gain_ref, query_gain_ref)
    out = []
    for c in range(3):
        x = raw[:, 128 * c : 128 * (c + 1)]
        gain = key_gain if c == 0 else query_gain * 64 ** (-0.5)
        n = x * lax.rsqrt(head_means(x * x, blocks) + EPSILON) * gain
        out.append(n * cos + partner(n) * sin)
    kv_ref[...] = jnp.where(lanes_of(out[0]) < 64, out[0], raw[:, :128]).astype(BF16)
    q_ref[...] = jnp.concatenate(out[1:], axis=1).astype(BF16)


def head_lanes(x, g, upper):
    part = x[:, 128 * (g // 2) : 128 * (g // 2) + 128]
    if (g % 2 == 1) != upper:
        part = pltpu.roll(part, 64, 1)
    keep = (lanes_of(part) >= 64) if upper else (lanes_of(part) < 64)
    return jnp.where(keep, part, 0.0).astype(BF16)


def attention_forward_kernel(q_ref, bias_ref, *refs):
    kv_refs, o_refs, lse_ref = refs[: -QUAD - 1], refs[-QUAD - 1 : -1], refs[-1]
    group = lse_ref.shape[1]
    kv = jnp.concatenate([r[...] for r in kv_refs], axis=0)
    v_t = kv.T[64:]
    q = q_ref[...].astype(F32)
    bias = bias_ref[0]
    out = []
    for g in range(group):
        s = contract_last(kv, head_lanes(q, g, False)) + bias
        top = jnp.max(s, axis=0, keepdims=True)
        p = jnp.exp(s - top)
        total = jnp.sum(p, axis=0, keepdims=True)
        out.append(dot(v_t, p.astype(BF16)) / total)
        lse_ref[0, g] = top + jnp.log(total)
    o = jnp.concatenate(out, axis=0).T.astype(BF16)
    rows = o.shape[0] // QUAD
    for j in range(QUAD):
        o_refs[j][0] = o[j * rows : (j + 1) * rows]


def attention_backward_kernel(q_ref, bias_ref, lse_ref, *refs):
    do_refs, kv_refs, dq_ref, dkv_refs = refs[:QUAD], None, None, None
    rest = refs[QUAD:]
    pieces = (len(rest) - 1) // 2
    kv_refs, dq_ref, dkv_refs = rest[:pieces], rest[pieces], rest[pieces + 1 :]
    group = lse_ref.shape[1]
    kv = jnp.concatenate([r[...] for r in kv_refs], axis=0)
    k_t = kv.T[:64]
    q = q_ref[...].astype(F32)
    do = jnp.concatenate([r[0].astype(F32) for r in do_refs], axis=0)
    do = jnp.concatenate([do, jnp.zeros((do.shape[0], 64), F32)], axis=1)
    rows = q.shape[0]
    bias = bias_ref[0]
    total = jnp.zeros(kv.shape, F32)
    dq = []
    for g in range(group):
        both = jnp.concatenate([head_lanes(q, g, False), head_lanes(do, g, True)], axis=0)
        products = contract_last(kv, both)
        p = jnp.exp(products[:, :rows] + (bias - lse_ref[0, g]))
        dp = products[:, rows:]
        delta = jnp.sum(p * dp, axis=0, keepdims=True)
        ds = (p * (dp - delta)).astype(BF16)
        total = total + dot(jnp.concatenate([ds, p.astype(BF16)], axis=1), both)
        dq.append(dot(k_t, ds))
    dq.append(jnp.zeros(dq[0].shape, F32))
    dq_ref[...] = jnp.concatenate(dq, axis=0).T
    for i, ref in enumerate(dkv_refs):
        ref[...] = total[i * rows : (i + 1) * rows].astype(BF16)


def attention_specs(rows, keys, pieces):
    q = pl.BlockSpec((rows, 256), lambda s: (s, 0))
    bias = pl.BlockSpec((1, keys, rows), lambda s: (s, 0, 0))
    kv = [pl.BlockSpec((rows, 128), lambda s: (s, 0))] * pieces
    return q, bias, kv


def attention_forward(q, bias, kv, group, after):
    seqs, keys, rows = bias.shape
    q_spec, bias_spec, kv_specs = attention_specs(rows, keys, len(kv))
    work = seqs * group * keys * rows
    return pl.pallas_call(
        ordered(attention_forward_kernel, len(after)),
        grid=(seqs,),
        in_specs=[*[ANYWHERE] * len(after), q_spec, bias_spec, *kv_specs],
        out_specs=[
            *[pl.BlockSpec((1, rows // QUAD, group * 64), lambda s: (s, 0, 0))] * QUAD,
            pl.BlockSpec((1, group, 1, rows), lambda s: (s, 0, 0, 0)),
        ],
        out_shape=[
            *[shape((seqs, rows // QUAD, group * 64), BF16)] * QUAD,
            shape((seqs, group, 1, rows), F32),
        ],
        compiler_params=pltpu.CompilerParams(vmem_limit_bytes=VMEM_LIMIT),
        cost_estimate=cost(6 * work * 128, 4 * bias.size, work),
        name="attention_forward",
    )(*after, q, bias, *kv)


def attention_backward(q, bias, lse, do, kv, after=()):
    seqs, keys, rows = bias.shape
    group = lse.shape[1]
    q_spec, bias_spec, kv_specs = attention_specs(rows, keys, len(kv))
    work = seqs * group * keys * rows
    return pl.pallas_call(
        ordered(attention_backward_kernel, len(after)),
        grid=(seqs,),
        in_specs=[
            *[ANYWHERE] * len(after),
            q_spec,
            bias_spec,
            pl.BlockSpec((1, group, 1, rows), lambda s: (s, 0, 0, 0)),
            *[pl.BlockSpec((1, rows // QUAD, group * 64), lambda s: (s, 0, 0))] * QUAD,
            *kv_specs,
        ],
        out_specs=[q_spec, *kv_specs],
        out_shape=[shape(q.shape, F32)] + [shape(k.shape, BF16) for k in kv],
        compiler_params=pltpu.CompilerParams(vmem_limit_bytes=VMEM_LIMIT),
        cost_estimate=cost(10 * work * 128, 4 * bias.size, work),
        name="attention_backward",
    )(*after, q, bias, lse, *do, *kv)


def put_halves(refs, value):
    rows = refs[0].shape[0]
    for i, ref in enumerate(refs):
        ref[...] = value[i * rows : (i + 1) * rows].astype(ref.dtype)


def sum_halves(refs):
    own = jnp.concatenate([refs[0][...], refs[1][...]], axis=0).astype(F32)
    return own + jnp.concatenate([refs[2][...], refs[3][...]], axis=0).astype(F32)


def branch_kernel(ids_ref, *refs):
    pieces, w_ref, out_refs, stack_ref = refs[:QUAD], refs[QUAD], refs[QUAD + 1 : -1], refs[-1]
    m = ids_ref[0] % QUAD
    for j in range(QUAD):
        stack_ref[j] = pieces[j][...]
    attn = jnp.concatenate([stack_ref[m ^ k] for k in range(QUAD)], axis=1)
    put_halves(out_refs, contract_last(attn, w_ref[...]))


def middle_kernel(ids_ref, x_ref, *refs):
    branch_refs, (gain_ref, mid_ref, h2_ref, half_ref) = refs[:4], refs[4:]
    mid = x_ref[...].astype(F32) + sum_halves(branch_refs)
    mid_ref[...] = mid
    h2 = (mid * row_factor(mid) * row_of(gain_ref)).astype(BF16)
    h2_ref[...] = h2
    rows = half_ref.shape[0]
    half_ref[...] = jnp.where(ids_ref[1] == 0, h2[:rows], h2[rows:])


def hidden_terms(gate, up, da):
    sg = jax.nn.sigmoid(gate)
    silu = gate * sg
    act = (silu * up).astype(BF16)
    dgate = (da * up * (sg + silu * (1.0 - sg))).astype(BF16)
    dup = (da * silu).astype(BF16)
    return act, dgate, dup


def hidden_tile(hidden):
    return next(t for t in (1152, 384, 128, hidden) if hidden % t == 0)


def hidden_call(body, name, args, out_shape, scratch=(), matmuls=1, after=()):
    hidden = max(a.shape[-1] for a in args)
    tile = hidden_tile(hidden)

    def spec(a):
        if a.shape[-1] == hidden:
            return pl.BlockSpec((a.shape[0], tile), lambda i: (0, i))
        return pl.BlockSpec(a.shape, lambda i: (0, 0))

    rows, width = args[0].shape[0], 1536
    return pl.pallas_call(
        ordered(body, len(after)),
        grid=(hidden // tile,),
        in_specs=[ANYWHERE] * len(after) + [spec(a) for a in args],
        out_specs=[spec(o) for o in out_shape],
        out_shape=list(out_shape),
        scratch_shapes=list(scratch),
        compiler_params=pltpu.CompilerParams(vmem_limit_bytes=VMEM_LIMIT),
        cost_estimate=cost(
            4 * matmuls * rows * width * hidden,
            sum(a.size * a.dtype.itemsize for a in (*args, *out_shape)),
        ),
        name=name,
    )(*after, *args)


def accumulate(total_ref, out_refs, term):
    step = pl.program_id(0)

    @pl.when(step == 0)
    def _():
        total_ref[...] = term

    @pl.when(step > 0)
    def _():
        total_ref[...] += term

    @pl.when(step == pl.num_programs(0) - 1)
    def _():
        put_halves(out_refs, total_ref[...].T)


def hidden_grad_kernel(g_ref, wd_ref, da_ref):
    da_ref[...] = dot(g_ref[...], wd_ref[...])


def own_mlp_kernel(
    h2_ref, da_ref, wg_ref, wu_ref, dh_top_ref, dh_ref, act_ref, dgate_ref, dup_ref, total_ref
):
    wg, wu, h2 = wg_ref[...], wu_ref[...], h2_ref[...]
    act, dgate, dup = hidden_terms(dot(h2, wg), dot(h2, wu), da_ref[...])
    act_ref[...] = act
    dgate_ref[...] = dgate
    dup_ref[...] = dup
    accumulate(
        total_ref, (dh_top_ref, dh_ref), contract_last(wg, dgate) + contract_last(wu, dup)
    )


def down_kernel(act_ref, wd_ref, down_ref, total_ref):
    accumulate(total_ref, (down_ref,), contract_last(wd_ref[...], act_ref[...]))


def back_kernel(
    ids_ref, mid_ref, a_ref, b_ref, c_ref, d_ref, g_ref, gain_ref, w_ref, dx_ref, dy_ref, *refs
):
    half_ref, part_ref, do_refs = refs[0], refs[1], refs[2:]
    m = ids_ref[0] % QUAD
    stack_ref, do_refs = do_refs[-1], do_refs[:-1]
    mid = mid_ref[...]
    factor = row_factor(mid)
    dh2 = sum_halves((a_ref, b_ref, c_ref, d_ref))
    part_ref[...] = jnp.sum(dh2 * mid * factor, axis=0, keepdims=True)
    scaled = dh2 * row_of(gain_ref)
    inner = jnp.mean(mid * scaled, axis=-1, keepdims=True)
    dx = g_ref[...].astype(F32) + (factor * scaled - mid * (factor * factor * factor) * inner)
    dx_ref[...] = dx
    dy = dx.astype(BF16)
    dy_ref[...] = dy
    half = half_ref.shape[0]
    half_ref[...] = jnp.where(ids_ref[1] == 0, dy[:half], dy[half:])
    do = dot(dy, w_ref[...]).astype(BF16)
    columns = do.shape[1] // QUAD
    for k in range(QUAD):
        stack_ref[m ^ k] = do[:, k * columns : (k + 1) * columns]
    for j in range(QUAD):
        do_refs[j][...] = stack_ref[j]


def norm_rotate_back(grad, raw, gain, cos, sin, blocks):
    normed = grad * cos - partner(grad) * sin
    factor = lax.rsqrt(head_means(raw * raw, blocks) + EPSILON)
    scaled = normed * gain
    inner = head_means(raw * scaled, blocks)
    part = jnp.sum(normed * raw * factor, axis=0, keepdims=True)
    return factor * scaled - raw * (factor * factor * factor) * inner, part


def head_grad_kernel(ids_ref, dq_ref, raw_ref, h1_ref, *refs):
    attn_refs, dy_ref, mine, theirs, refs = refs[:4], refs[4], refs[5:8], refs[8:11], refs[11:]
    core = ids_ref[1]
    key_gain_ref, query_gain_ref, cos_ref, sin_ref, refs = *refs[:4], refs[4:]
    nz = (len(refs) - QUAD - 3) // 2
    dkv_refs, refs = refs[:nz], refs[nz:]
    part_ref, piece_refs, w_refs = refs[0], refs[1 : 1 + QUAD], refs[1 + QUAD : -2]
    total_ref, dy_all = refs[-2:]
    cos, sin, blocks = cos_ref[...], sin_ref[...], head_blocks()
    key_gain, query_gain = head_gain_rows(key_gain_ref, query_gain_ref)
    dkv = dkv_refs[0][...].astype(F32)
    for ref in dkv_refs[1:]:
        dkv = dkv + ref[...].astype(F32)
    scale = 64 ** (-0.5)
    low = []
    for c in range(3):
        lanes = slice(128 * c, 128 * (c + 1))
        given = dkv if c == 0 else dq_ref[:, 128 * (c - 1) : 128 * c] * scale
        gain = key_gain if c == 0 else query_gain
        grad, part = norm_rotate_back(given, raw_ref[:, lanes], gain, cos, sin, blocks)
        if c == 0:
            grad = jnp.where(lanes_of(grad) < 64, grad, dkv)
        part_ref[:, lanes] = part
        low.append(grad.astype(BF16))
    low = jnp.concatenate(low, axis=1)
    rows = low.shape[0]
    tokens = rows // (SEQS * QUAD)
    attn = []
    for seq in range(SEQS):
        for j in range(QUAD):
            begin = (seq * QUAD + j) * tokens
            piece_refs[j][seq * tokens : (seq + 1) * tokens] = low[begin : begin + tokens]
            if j == 0:
                dy_all[seq, j] = dy_ref[seq]
            attn.append(attn_refs[j][seq])
    for j in range(1, QUAD):
        dy_all[core, j] = mine[j - 1][...]
        dy_all[1 - core, j] = theirs[j - 1][...]
    columns = attn[0].shape[1]
    grad_wqkv = contract_first(h1_ref[...].reshape(rows, -1), low)
    grad_wo = contract_first(dy_all[...].reshape(rows, -1), jnp.concatenate(attn, axis=0))
    total_ref[...] = jnp.concatenate([grad_wqkv[:, : 128 + columns], grad_wo], axis=1)
    z = ids_ref[0] // QUAD
    owned = w_refs[0].shape[0]
    for step, ref in enumerate(w_refs):
        begin = pl.multiple_of(((z + nz - step) % nz) * owned, 8)
        ref[...] = total_ref[pl.ds(begin, owned), :].astype(BF16)


def spread_kernel(ids_ref, *refs):
    nz = len(refs) - QUAD - 1
    terms, (own_ref, *out_refs), total_ref = refs[:nz], refs[nz:-1], refs[-1]
    total = terms[0][...].astype(F32)
    for ref in terms[1:]:
        total = total + ref[...].astype(F32)
    total_ref[...] = total
    m = ids_ref[0] % QUAD
    rows = own_ref.shape[0]
    for j in range(QUAD):
        part = total_ref[pl.ds(pl.multiple_of((m ^ j) * rows, 8), rows), :]
        if j == 0:
            own_ref[...] = part
        else:
            out_refs[j - 1][...] = part.astype(BF16)


def assemble_kernel(ids_ref, own_ref, a_ref, b_ref, c_ref, wq_ref, wk_ref, wv_ref, wo_ref, stack_ref):
    m = ids_ref[0] % QUAD
    stack_ref[0] = own_ref[...]
    for j, ref in enumerate((a_ref, b_ref, c_ref)):
        stack_ref[j + 1] = ref[...].astype(F32)
    parts = [stack_ref[m ^ k] for k in range(QUAD)]
    columns = wq_ref.shape[1] // QUAD
    wk_ref[...] = jnp.concatenate([p[:, :64] for p in parts], axis=1)
    wv_ref[...] = jnp.concatenate([p[:, 64:128] for p in parts], axis=1)
    wq_ref[...] = jnp.concatenate([p[:, 128 : 128 + columns] for p in parts], axis=1)
    wo_ref[...] = jnp.concatenate([p[:, 128 + columns :] for p in parts], axis=1)


def input_grad_kernel(ids_ref, *refs):
    pieces, (x_ref, wq_ref, wk_ref, wv_ref, out_ref, part_ref, stack_ref) = refs[:QUAD], refs[QUAD:]
    m = ids_ref[0] % QUAD
    for j in range(QUAD):
        stack_ref[j] = pieces[j][...]
    parts = [stack_ref[m ^ k] for k in range(QUAD)]
    columns = wq_ref.shape[1] // QUAD
    dk = jnp.concatenate([p[:, :64] for p in parts], axis=1)
    dv = jnp.concatenate([p[:, 64:128] for p in parts], axis=1)
    dq = jnp.concatenate([p[:, 128 : 128 + columns] for p in parts], axis=1)
    total = (
        contract_last(dq, wq_ref[...])
        + contract_last(dk, wk_ref[...])
        + contract_last(dv, wv_ref[...])
    )
    out_ref[...] = total.astype(BF16)
    x = x_ref[...].astype(F32)
    part_ref[...] = jnp.sum(total * x * row_factor(x), axis=0, keepdims=True)


def tokens_kernel(x_ref, dx_ref, a_ref, b_ref, gain_ref, out_ref):
    x = x_ref[...].astype(F32)
    factor = row_factor(x)
    scaled = (a_ref[...].astype(F32) + b_ref[...].astype(F32)) * row_of(gain_ref)
    inner = jnp.mean(x * scaled, axis=-1, keepdims=True)
    back = factor * scaled - x * (factor * factor * factor) * inner
    out_ref[...] = (dx_ref[...] + back).astype(BF16)


def output_kernel(mid_ref, a_ref, b_ref, out_ref):
    out_ref[...] = (mid_ref[...] + (a_ref[...].astype(F32) + b_ref[...].astype(F32))).astype(BF16)


def bulk_mlp_kernel(ids_ref, *refs, pieces, row_tile, first):
    sides, refs = (refs[: pieces[0]], refs[pieces[0] : sum(pieces)]), refs[sum(pieces) :]
    act_ref, dgate_ref, dup_ref, wg_ref, wu_ref, wd_ref, refs = *refs[:6], refs[6:]
    if first:
        own_refs, other_ref, h2c_ref, gc_ref, h2_ref, g_ref, sems = refs[:3], *refs[3:]
    else:
        h2c_ref, gc_ref, own_refs, other_ref, h2_ref, g_ref, sems = *refs[:2], refs[2:5], *refs[5:]
    rows = act_ref.shape[0]
    tokens, width = h2_ref.shape
    own_rows = own_refs[0].shape[0]
    pair_rows = 2 * own_rows

    @pl.when(pl.program_id(0) == 0)
    def _():
        half = rows // 2
        places = pieces[1] // 2
        copies = []

        def copy_rows(source, skip, size, target, begin, sem):
            return pltpu.make_async_copy(
                source.at[pl.ds(skip, size)], target.at[pl.ds(begin, size)], sems.at[sem]
            )

        begin = 0
        for i, source in enumerate(sides[0]):
            skip = half if i in (0, 2) else 0
            copies.append(copy_rows(source, skip, source.shape[0] - skip, h2_ref, begin, i))
            begin += source.shape[0] - skip
        for copy in copies:
            copy.start()
        for core in range(2):

            @pl.when(ids_ref[1] == core)
            def _():
                own_y, other_y = sides[1][:places], sides[1][places : 2 * places]
                if core == 1:
                    own_y, other_y = other_y, own_y
                blocks = [*own_y[1:], *other_y]
                for i, source in enumerate(blocks):
                    for part in range(2):
                        to = (i + part * len(blocks)) * half
                        sem = len(sides[0]) + 2 * i + part
                        copy_rows(source, (core ^ part) * half, half, g_ref, to, sem).start()
                last = len(sides[0]) + 4 * places - 2
                copy_rows(sides[1][-1], 0, rows, g_ref, tokens - rows, last).start()

        for i in range(2 * (2 * places - 1)):
            copies.append(copy_rows(sides[1][0], 0, half, g_ref, 0, len(sides[0]) + i))
        last = len(sides[0]) + 4 * places - 2
        copies.append(copy_rows(sides[1][-1], 0, rows, g_ref, tokens - rows, last))
        if first:
            me = ids_ref[0]
            row = lax.broadcasted_iota(jnp.int32, (width, pair_rows), 0)
            col = lax.broadcasted_iota(jnp.int32, (width, pair_rows), 1)
            target = jnp.where(col < own_rows, me * own_rows + col, ((me ^ 1) - 1) * own_rows + col)
            chosen = jnp.where(row == target, 1.0, 0.0).astype(BF16)
        for copy in copies:
            copy.wait()
        if first:
            h2c_ref[...] = dot(h2_ref[...], chosen).T.astype(BF16)
            gc_ref[...] = dot(g_ref[...], chosen).T.astype(BF16)

    wg, wu, wd = wg_ref[...], wu_ref[...], wd_ref[...]
    last = slice(tokens - rows, tokens)
    totals = [
        dot(left[:, last], term[...])
        for left, term in ((h2c_ref, dgate_ref), (h2c_ref, dup_ref), (gc_ref, act_ref))
    ]
    for begin in range(0, tokens - rows, row_tile):
        part = slice(begin, min(begin + row_tile, tokens - rows))
        h2 = h2_ref[part]
        act, dgate, dup = hidden_terms(dot(h2, wg), dot(h2, wu), dot(g_ref[part], wd))
        h2c, gc = h2c_ref[:, part], gc_ref[:, part]
        terms = [dot(h2c, dgate), dot(h2c, dup), dot(gc, act)]
        totals = [a + b for a, b in zip(totals, terms)]
    for i, (own, total) in enumerate(zip(own_refs, totals)):
        own[...] = total[:own_rows]
        other_ref[i] = total[own_rows:].astype(BF16)


def bulk_mlp(ids, h2, g, own_terms, weights, chosen, own_rows, begin, end, tile, after):
    width = h2[0].shape[1]
    rows, hidden = own_terms[0].shape
    tokens = sum(piece.shape[0] for piece in h2) - rows
    out_hidden = min(end * tile, hidden) - begin * tile
    weight = pl.BlockSpec((width, tile), lambda i: (0, i + begin))
    term = pl.BlockSpec((rows, tile), lambda i: (0, i + begin))
    result = pl.BlockSpec((own_rows, tile), lambda i: (0, i))
    columns = pl.BlockSpec((2 * own_rows, tokens), lambda i: (0, 0))
    first = not chosen
    pieces = (len(h2), len(g))
    body = functools.partial(
        bulk_mlp_kernel, pieces=pieces, row_tile=min(tokens, 1024), first=first
    )
    return pl.pallas_call(
        ordered(body, len(after)),
        grid=(end - begin,),
        in_specs=[ANYWHERE] * len(after)
        + [SCALARS]
        + [ANYWHERE] * sum(pieces)
        + [term] * 3
        + [weight] * 3
        + [columns] * len(chosen),
        out_specs=[result] * 3
        + [pl.BlockSpec((3, own_rows, tile), lambda i: (0, 0, i))]
        + [columns] * (2 if first else 0),
        out_shape=[shape((own_rows, out_hidden), F32)] * 3
        + [shape((3, own_rows, out_hidden), BF16)]
        + [shape((2 * own_rows, tokens), BF16)] * (2 if first else 0),
        scratch_shapes=[pltpu.VMEM((tokens, width), BF16)] * 2 + [pltpu.SemaphoreType.DMA((len(h2) + 2 * len(g) - 3,))],
        compiler_params=pltpu.CompilerParams(vmem_limit_bytes=VMEM_LIMIT),
        cost_estimate=cost(
            6 * tokens * (width + 2 * own_rows) * out_hidden,
            6 * width * out_hidden + 4 * tokens * width,
            tokens * out_hidden,
            scale=1,
        ),
        name="bulk_mlp",
    )(*after, ids, *h2, *g, *own_terms, *weights, *chosen)


def finish_kernel(*refs):
    first, second, theirs, outs = refs[:3], refs[3:6], refs[6:8], refs[8:]
    cut = first[0].shape[1]
    for i in range(3):
        outs[i][:, :cut] = first[i][...] + theirs[0][i].astype(F32)
        outs[i][:, cut:] = second[i][...] + theirs[1][i].astype(F32)


def bulk_finish(first, second, theirs_first, theirs_second):
    rows, first_hidden = first[0].shape
    second_hidden = second[0].shape[1]
    hidden = first_hidden + second_hidden
    block = rows // 3 if rows % 48 == 0 else rows

    def spec(columns):
        return pl.BlockSpec((block, columns), lambda i: (i, 0))

    def theirs_spec(columns):
        return pl.BlockSpec((3, block, columns), lambda i: (0, i, 0))

    return pl.pallas_call(
        finish_kernel,
        grid=(rows // block,),
        in_specs=[spec(first_hidden)] * 3
        + [spec(second_hidden)] * 3
        + [theirs_spec(first_hidden), theirs_spec(second_hidden)],
        out_specs=[spec(hidden)] * 3,
        out_shape=[shape((rows, hidden), F32)] * 3,
        compiler_params=pltpu.CompilerParams(vmem_limit_bytes=VMEM_LIMIT),
        cost_estimate=cost(rows * hidden, 30 * rows * hidden),
        name="bulk_finish",
    )(*first, *second, theirs_first, theirs_second)


def gains_kernel(a_ref, b_ref, attn_ref, mlp_ref, query_ref, key_ref):
    total = a_ref[...] + b_ref[...]
    width = attn_ref.shape[0]
    attn_ref[...] = total[:width]
    mlp_ref[...] = total[width : 2 * width]
    heads = total[2 * width :]
    key_ref[...] = heads[:64]
    query_ref[...] = heads[128:192] + heads[192:256] + heads[256:320]


def shards(
    tokens,
    w_query,
    w_key,
    w_value,
    w_output,
    w_gate,
    w_up,
    w_down,
    attn_gain,
    mlp_gain,
    query_gain,
    key_gain,
    segments,
    positions,
    cotangent,
):
    count = lax.axis_size("ctx")
    me = lax.axis_index("ctx")
    core = lax.axis_index("tp")
    nz = count // QUAD
    m = me % QUAD
    head = query_gain.shape[0]
    rows, model = tokens.shape
    q_heads = w_query.shape[1] // head
    kv_heads = w_key.shape[1] // head
    group = q_heads // kv_heads
    pair = rows // SEQS
    quad_rows = QUAD * rows
    columns = group * head
    own_rows = model // count
    flips = [flip_pairs(count, j) for j in range(QUAD)]
    ids = jnp.stack([me, core]).astype(jnp.int32)

    def quad_exchange(pieces):
        return [pieces[0]] + [send(pieces[j], flips[j]) for j in range(1, QUAD)]

    own_tokens = tokens.reshape(SEQS, pair, model)
    half = lax.dynamic_index_in_dim(own_tokens, core, 0, keepdims=False)
    mine = [send(half, flips[j]) for j in range(1, QUAD)]
    theirs = [swap_cores(p) for p in mine]

    freqs = ROPE_BASE ** (-2.0 * np.arange(head // 2) / head)
    freqs = jnp.asarray(np.tile(freqs, 4)[None, :], F32)
    bias, angles = kernel_call(
        mask_kernel,
        "visible",
        (ids, freqs, segments.reshape(count, SEQS * pair)),
        [shape((SEQS, count * pair, QUAD * pair), F32), shape((quad_rows, 2 * head), F32)],
        scalars=True,
    )
    sign = jnp.asarray(np.tile(np.repeat([-1.0, 1.0], head // 2), 2)[None, :], F32)
    cos, sin = jnp.cos(angles), jnp.sin(angles) * sign
    w_head = jnp.concatenate(
        [
            lax.dynamic_slice_in_dim(w_key, m * head, head, 1),
            lax.dynamic_slice_in_dim(w_value, m * head, head, 1),
            lax.dynamic_slice_in_dim(w_query, m * columns, columns, 1),
            jnp.zeros((model, head), BF16),
        ],
        axis=1,
    )
    h1, raw, q, kv_own, g_copy = kernel_call(
        qkv_kernel,
        "query_key_value",
        (
            ids,
            own_tokens,
            *mine,
            *theirs,
            attn_gain,
            w_head,
            key_gain,
            query_gain,
            cos,
            sin,
            cotangent,
        ),
        [
            shape((SEQS, QUAD, pair, model), BF16),
            shape((quad_rows, 6 * head), F32),
            shape((quad_rows, 4 * head), BF16),
            shape((quad_rows, 2 * head), BF16),
            shape((rows, model), BF16),
        ],
        flops=2 * quad_rows * model * 6 * head,
        scalars=True,
    )
    kv = [kv_own] + [send(kv_own, shift_pairs(count, s)) for s in range(1, nz)]
    hidden = w_down.shape[1]
    (da,) = hidden_call(
        hidden_grad_kernel,
        "hidden_grad",
        (cotangent, w_down),
        [shape((rows, hidden), F32)],
        after=(kv_own,),
    )
    g_blocks = [lax.ppermute(g_copy, ("ctx", "tp"), core_pairs(count))]

    def next_cotangents(after):
        g_blocks[-1] = touch(g_blocks[-1], after)
        g_blocks.append(send(g_blocks[-1], shift_pairs(count, 1)))

    *attn, lse = attention_forward(q, bias, kv, group, (da,))
    next_cotangents((lse,))
    attn_pieces = quad_exchange([a.reshape(rows, columns) for a in attn])
    branch = kernel_call(
        branch_kernel,
        "branch",
        (ids, *attn_pieces, w_output),
        [shape((rows // 2, model), BF16)] * 2,
        flops=2 * rows * model * w_output.shape[1],
        scalars=True,
        scratch=[pltpu.VMEM((QUAD, rows, columns), BF16)],
    )
    middle, h2, h2_half = kernel_call(
        middle_kernel,
        "middle",
        (ids, tokens, *branch, *[swap_cores(b) for b in branch], mlp_gain),
        [shape((rows, model), F32), shape((rows, model), BF16), shape((rows // 2, model), BF16)],
        scalars=True,
    )
    h2_pieces = gather_column(h2_half, count)

    g_first = swap_cores(g_blocks[0])
    *dh2, act, dgate, dup = hidden_call(
        own_mlp_kernel,
        "own_mlp",
        (h2, da, w_gate, w_up),
        [shape((rows // 2, model), BF16)] * 2 + [shape((rows, hidden), BF16)] * 3,
        scratch=[pltpu.VMEM((model, rows), F32)],
        matmuls=4,
        after=(g_first,),
    )
    h2_packed = pack(h2_pieces, (act,))
    g_blocks[1] = touch(g_blocks[1], (h2,))
    g_second = swap_cores(g_blocks[1])
    for _ in range(2, nz - 1):
        next_cotangents((act,))
    grad_middle, dy, dy_half, mlp_gain_part, *do = kernel_call(
        back_kernel,
        "back",
        (ids, middle, *dh2, *[swap_cores(d) for d in dh2], cotangent, mlp_gain, w_output),
        [
            shape((rows, model), F32),
            shape((rows, model), BF16),
            shape((rows // 2, model), BF16),
            shape((1, model), F32),
            *[shape((rows, columns), BF16)] * QUAD,
        ],
        flops=2 * rows * model * w_output.shape[1],
        scalars=True,
        scratch=[pltpu.VMEM((QUAD, rows, columns), BF16)],
        after=(h2_packed, g_second),
    )
    do_pieces = [d.reshape(SEQS, pair, columns) for d in quad_exchange(do)]
    dy_half = touch(dy_half, do_pieces[1:])
    dy_mine = [send(dy_half, flips[j]) for j in range(1, QUAD)]
    dy_theirs = [swap_cores(p) for p in dy_mine]
    dy_pieces = (dy.reshape(SEQS, pair, model), *dy_mine, *dy_theirs)
    dq, *dkv = attention_backward(
        q, bias, lse, do_pieces, kv, (g_blocks[-1],)
    )
    next_cotangents((dq,))
    g_swapped = [g_first, g_second] + [swap_cores(g) for g in g_blocks[2:-1]]
    h2_column = touch(h2_packed, (dq, *dy_mine))
    h2_other = send(h2_column, flips[2])
    (down,) = hidden_call(
        down_kernel,
        "down",
        (act, w_down),
        [shape((rows, model), BF16)],
        scratch=[pltpu.VMEM((model, rows), F32)],
        after=(dq,),
    )
    dkv = [dkv[0]] + [send(dkv[s], shift_pairs(count, nz - s)) for s in range(1, nz)]


    z_rows = model // nz
    head_part, *rest = kernel_call(
        head_grad_kernel,
        "head_grad",
        (ids, dq, raw, h1, *attn, *dy_pieces, key_gain, query_gain, cos, sin, *dkv),
        [
            shape((1, 6 * head), F32),
            *[shape((rows, 6 * head), BF16)] * QUAD,
            *[shape((z_rows, 8 * head), BF16)] * nz,
        ],
        flops=2 * quad_rows * model * 9 * head,
        scalars=True,
        scratch=[
            pltpu.VMEM((model, 8 * head), F32),
            pltpu.VMEM((SEQS, QUAD, pair, model), BF16),
        ],
        after=(down,),
    )
    grad_pieces, w_parts = quad_exchange(rest[:QUAD]), rest[QUAD:]
    w_parts = [w_parts[0]] + [send(w_parts[s], shift_pairs(count, nz - s)) for s in range(1, nz)]
    h2_column = touch(h2_column, (h2_other, head_part))
    h2_other = touch(h2_other, (h2_column,))
    h2_rows = (h2_column, h2_other, swap_cores(h2_column), swap_cores(h2_other), h2)
    g_rows = (*g_blocks, *g_swapped, swap_cores(g_blocks[-1]), cotangent)

    tile = 512
    tiles = pl.cdiv(hidden, tile)
    cut = (tiles + 1) // 2

    def bulk_part(chosen, begin, end, after):
        result = bulk_mlp(
            ids,
            h2_rows,
            g_rows,
            (act, dgate, dup),
            (w_gate, w_up, w_down),
            chosen,
            own_rows,
            begin,
            end,
            tile,
            after,
        )
        return result[:3], result[3], result[4:]

    bulk_first = bulk_part((), 0, cut, (head_part,))
    theirs_first = send(touch(bulk_first[1], grad_pieces[1:]), flips[1])
    bulk_second = bulk_part(bulk_first[2], cut, tiles, ())
    theirs_second = send(bulk_second[1], flips[1])
    after_bulk = (bulk_second[0][0],)
    down = touch(down, after_bulk)
    (output,) = kernel_call(
        output_kernel, "output", (middle, down, swap_cores(down)), [shape((rows, model), BF16)]
    )
    dh1, attn_gain_part = kernel_call(
        input_grad_kernel,
        "input_grad",
        (ids, *grad_pieces, tokens, w_query, w_key, w_value),
        [shape((rows, model), BF16), shape((1, model), F32)],
        flops=2 * rows * model * (q_heads + 2 * kv_heads) * head,
        scalars=True,
        scratch=[pltpu.VMEM((QUAD, rows, 6 * head), BF16)],
        after=after_bulk,
    )
    (grad_tokens,) = kernel_call(
        tokens_kernel,
        "tokens_grad",
        (tokens, grad_middle, dh1, swap_cores(dh1), attn_gain),
        [shape((rows, model), BF16)],
    )
    spread = kernel_call(
        spread_kernel,
        "spread",
        (ids, *w_parts),
        [shape((own_rows, 8 * head), F32)] + [shape((own_rows, 8 * head), BF16)] * (QUAD - 1),
        scalars=True,
        scratch=[pltpu.VMEM((z_rows, 8 * head), F32)],
        after=after_bulk,
    )
    gains = jnp.concatenate([attn_gain_part, 0.5 * mlp_gain_part, head_part], axis=1)[0]
    gains = gains + swap_cores(gains)
    gains = gains + send(gains, flips[2])
    fillers = [spread[0], output]
    for i in range(2, count.bit_length() - 1):
        gains = touch(gains, (fillers[min(i, 3) - 2],))
        gains = gains + send(gains, flip_pairs(count, 1 << i))
    gains = touch(gains, (grad_tokens,))
    grad_attn_gain, grad_mlp_gain, grad_query_gain, grad_key_gain = kernel_call(
        gains_kernel,
        "gains",
        (gains, send(gains, flips[1])),
        [shape((model,), F32)] * 2 + [shape((head,), F32)] * 2,
    )
    spread = quad_exchange(spread)
    grad_wq, grad_wk, grad_wv, grad_wo = kernel_call(
        assemble_kernel,
        "assemble",
        (ids, *spread),
        [
            shape((own_rows, q_heads * head), F32),
            shape((own_rows, kv_heads * head), F32),
            shape((own_rows, kv_heads * head), F32),
            shape((own_rows, q_heads * head), F32),
        ],
        scalars=True,
        scratch=[pltpu.VMEM((QUAD, own_rows, 8 * head), F32)],
    )

    mlp_grads = bulk_finish(bulk_first[0], bulk_second[0], theirs_first, theirs_second)
    return (
        output,
        grad_tokens,
        grad_wq,
        grad_wk,
        grad_wv,
        grad_wo,
        mlp_grads[0],
        mlp_grads[1],
        mlp_grads[2],
        grad_attn_gain,
        grad_mlp_gain,
        grad_query_gain,
        grad_key_gain,
    )


def solution(mesh):
    rows = P("ctx", None)
    columns = P(None, "tp")
    both = P("ctx", "tp")
    in_specs = (rows,) + (columns,) * 7 + (P(),) * 5 + (P("ctx"), rows)
    out_specs = (rows, rows) + (both,) * 7 + (P(),) * 4
    return jax.shard_map(shards, mesh=mesh, in_specs=in_specs, out_specs=out_specs, check_vma=False)
```

```python
import functools

import jax
import jax.numpy as jnp
import numpy as np
from jax import lax
from jax.experimental import pallas as pl
from jax.experimental.pallas import tpu as pltpu
from jax.sharding import PartitionSpec as P

BLK = 32
SEQS = 2
QUAD = 4
EPSILON = 1e-05
ROPE_BASE = 1000000.0
MASKED = -1e30
F32 = jnp.float32
BF16 = jnp.bfloat16
MIB = 1024 * 1024
VMEM_LIMIT = 56 * MIB
ROOMY = ("pack", "back", "spread", "head_grad", "middle",)


def dot(left, right):
    return jnp.dot(left, right, preferred_element_type=F32)


def contract_last(left, right):
    return lax.dot_general(left, right, (((1,), (1,)), ((), ())), preferred_element_type=F32)


def contract_first(left, right):
    return lax.dot_general(left, right, (((0,), (0,)), ((), ())), preferred_element_type=F32)


def shift_pairs(count, step):
    nz = count // QUAD
    return [(i, ((i // QUAD + step) % nz) * QUAD + i % QUAD) for i in range(count)]


def flip_pairs(count, bits):
    return [(i, i ^ bits) for i in range(count)]


def send(value, pairs):
    return lax.ppermute(value, "ctx", pairs)


def swap_cores(value):
    return lax.ppermute(value, "tp", [(0, 1), (1, 0)])


def core_pairs(count):
    return [pair for i in range(count) for pair in ((2 * i, 2 * i), (2 * i + 1, 2 * (i ^ 2) + 1))]


def gather_column(half, count):
    return [half] + [send(half, shift_pairs(count, s)) for s in range(1, count // QUAD)]


COST_SCALE = 0.01


def cost(flops, bytes_accessed, transcendentals=0, scale=COST_SCALE):
    return pl.CostEstimate(
        flops=int(flops * scale),
        bytes_accessed=int(bytes_accessed * scale),
        transcendentals=int(transcendentals * scale),
    )


SCALARS = pl.BlockSpec(memory_space=pltpu.SMEM)


ANYWHERE = pl.BlockSpec(memory_space=pl.ANY)


def ordered(body, extra):
    return lambda *refs: body(*refs[extra:])


def kernel_call(
    body, name, args, out_shape, flops=0, scalars=False, scratch=(), after=(), scale=COST_SCALE
):
    vmem = pl.BlockSpec(memory_space=pltpu.VMEM)
    roomy = name in ROOMY
    bytes_accessed = sum(a.size * a.dtype.itemsize for a in (*args, *out_shape))
    return pl.pallas_call(
        ordered(body, len(after)),
        in_specs=[ANYWHERE] * len(after)
        + [SCALARS if scalars and i == 0 else vmem for i in range(len(args))],
        out_specs=[vmem] * len(out_shape),
        out_shape=list(out_shape),
        scratch_shapes=list(scratch),
        compiler_params=pltpu.CompilerParams(
            vmem_limit_bytes=VMEM_LIMIT if roomy else min(3 * bytes_accessed + 8 * MIB, VMEM_LIMIT)
        ),
        cost_estimate=cost(flops, bytes_accessed, scale=scale),
        name=name,
    )(*after, *args)


def shape(dims, dtype):
    return jax.ShapeDtypeStruct(dims, dtype)


def pack_kernel(*refs):
    pieces, out_ref = refs[:-1], refs[-1]
    rows = pieces[0].shape[0]
    for i, piece in enumerate(pieces):
        out_ref[i * rows : (i + 1) * rows] = piece[...]


def pack(pieces, after=()):
    rows, width = pieces[0].shape
    out = shape((len(pieces) * rows, width), pieces[0].dtype)
    return kernel_call(pack_kernel, "pack", pieces, [out], after=after)[0]


def touch(value, after):
    return pl.pallas_call(
        lambda *refs: None,
        in_specs=[ANYWHERE] * (1 + len(after)),
        out_specs=ANYWHERE,
        out_shape=shape(value.shape, value.dtype),
        input_output_aliases={0: 0},
        name="touch",
    )(value, *after)


def row_factor(x):
    return lax.rsqrt(jnp.mean(x * x, axis=-1, keepdims=True) + EPSILON)


def head_means(x, blocks):
    high = x.astype(BF16)
    low = (x - high.astype(F32)).astype(BF16)
    return dot(high, blocks) + dot(low, blocks)


def head_blocks():
    row = lax.broadcasted_iota(jnp.int32, (128, 128), 0)
    col = lax.broadcasted_iota(jnp.int32, (128, 128), 1)
    return jnp.where(row // 64 == col // 64, 1.0 / 64, 0.0).astype(BF16)


def row_of(ref):
    return ref[...].reshape(1, -1)


def head_gain_rows(key_ref, query_ref):
    key, query = row_of(key_ref), row_of(query_ref)
    return jnp.concatenate([key, key], axis=1), jnp.concatenate([query, query], axis=1)


def lanes_of(x):
    return lax.broadcasted_iota(jnp.int32, x.shape, 1)


def partner(x):
    return jnp.where(lanes_of(x) % 64 < 32, pltpu.roll(x, 96, 1), pltpu.roll(x, 32, 1))


def mask_kernel(ids_ref, freq_ref, seg_ref, bias_ref, angle_ref):
    me = ids_ref[0]
    count = seg_ref.shape[0]
    nz = count // QUAD
    tokens = seg_ref.shape[1] // SEQS
    z, m = me // QUAD, me % QUAD

    def place(chip, offset):
        return jnp.where(offset < BLK, chip * BLK, (2 * count - 2 - chip) * BLK) + offset

    chips = [((z + nz - step) % nz) * QUAD + (m ^ j) for step in range(nz) for j in range(QUAD)]
    seg_rows = [seg_ref[pl.ds(chip, 1), :].astype(F32) for chip in chips]
    fill = jnp.zeros((128 - count, SEQS * tokens), F32)
    seg_cols = jnp.concatenate([*seg_rows, fill], axis=0).T
    row_offset = lax.broadcasted_iota(jnp.int32, (1, tokens), 1)
    col_offset = lax.broadcasted_iota(jnp.int32, (tokens, 1), 0)
    place_q = jnp.concatenate([place(chip, row_offset) for chip in chips[:QUAD]], axis=1)
    far = 2 * count * BLK
    for seq in range(SEQS):
        of_seq = slice(seq * tokens, (seq + 1) * tokens)
        seg_q = jnp.concatenate([row[:, of_seq] for row in seg_rows[:QUAD]], axis=1)
        first = jnp.full((tokens, QUAD * tokens), far, jnp.int32)
        for i, chip in enumerate(chips):
            place_k = place(chip, col_offset)
            same = seg_cols[of_seq, i : i + 1] == seg_q
            bias_ref[seq, i * tokens : (i + 1) * tokens, :] = jnp.where(
                same & (place_k <= place_q), 0.0, MASKED
            )
            first = jnp.minimum(first, jnp.where(same, place_k, far))
        position = (place_q - jnp.min(first, axis=0, keepdims=True)).astype(F32)
        rows = position.shape[1]
        angle_ref[seq * rows : (seq + 1) * rows, :] = (
            jnp.broadcast_to(position, (128, rows)).T * freq_ref[...]
        )


def qkv_kernel(ids_ref, own_ref, *refs):
    mine, theirs = refs[:3], refs[3:6]
    gain_ref, w_ref, key_gain_ref, query_gain_ref, cos_ref, sin_ref, g_ref = refs[6:13]
    h1_ref, raw_ref, q_ref, kv_ref, copy_ref = refs[13:]
    core = ids_ref[1]
    gain = row_of(gain_ref)
    copy_ref[...] = g_ref[...]

    def put(seq, j, piece):
        x = piece.astype(F32)
        h1_ref[seq, j] = (x * row_factor(x) * gain).astype(BF16)

    put(0, 0, own_ref[0])
    put(1, 0, own_ref[1])
    for j in range(1, QUAD):
        put(core, j, mine[j - 1][...])
        put(1 - core, j, theirs[j - 1][...])
    rows = raw_ref.shape[0]
    raw = dot(h1_ref[...].reshape(rows, -1), w_ref[...])
    raw_ref[...] = raw
    cos, sin, blocks = cos_ref[...], sin_ref[...], head_blocks()
    key_gain, query_gain = head_gain_rows(key_gain_ref, query_gain_ref)
    out = []
    for c in range(3):
        x = raw[:, 128 * c : 128 * (c + 1)]
        gain = key_gain if c == 0 else query_gain * 64 ** (-0.5)
        n = x * lax.rsqrt(head_means(x * x, blocks) + EPSILON) * gain
        out.append(n * cos + partner(n) * sin)
    kv_ref[...] = jnp.where(lanes_of(out[0]) < 64, out[0], raw[:, :128]).astype(BF16)
    q_ref[...] = jnp.concatenate(out[1:], axis=1).astype(BF16)


def head_lanes(x, g, upper):
    part = x[:, 128 * (g // 2) : 128 * (g // 2) + 128]
    if (g % 2 == 1) != upper:
        part = pltpu.roll(part, 64, 1)
    keep = (lanes_of(part) >= 64) if upper else (lanes_of(part) < 64)
    return jnp.where(keep, part, 0.0).astype(BF16)


def attention_forward_kernel(q_ref, bias_ref, *refs):
    kv_refs, o_refs, lse_ref = refs[: -QUAD - 1], refs[-QUAD - 1 : -1], refs[-1]
    group = lse_ref.shape[1]
    kv = jnp.concatenate([r[...] for r in kv_refs], axis=0)
    v_t = kv.T[64:]
    q = q_ref[...].astype(F32)
    bias = bias_ref[0]
    out = []
    for g in range(group):
        s = contract_last(kv, head_lanes(q, g, False)) + bias
        top = jnp.max(s, axis=0, keepdims=True)
        p = jnp.exp(s - top)
        total = jnp.sum(p, axis=0, keepdims=True)
        out.append(dot(v_t, p.astype(BF16)) / total)
        lse_ref[0, g] = top + jnp.log(total)
    o = jnp.concatenate(out, axis=0).T.astype(BF16)
    rows = o.shape[0] // QUAD
    for j in range(QUAD):
        o_refs[j][0] = o[j * rows : (j + 1) * rows]


def attention_backward_kernel(q_ref, bias_ref, lse_ref, *refs):
    do_refs, kv_refs, dq_ref, dkv_refs = refs[:QUAD], None, None, None
    rest = refs[QUAD:]
    pieces = (len(rest) - 1) // 2
    kv_refs, dq_ref, dkv_refs = rest[:pieces], rest[pieces], rest[pieces + 1 :]
    group = lse_ref.shape[1]
    kv = jnp.concatenate([r[...] for r in kv_refs], axis=0)
    k_t = kv.T[:64]
    q = q_ref[...].astype(F32)
    do = jnp.concatenate([r[0].astype(F32) for r in do_refs], axis=0)
    do = jnp.concatenate([do, jnp.zeros((do.shape[0], 64), F32)], axis=1)
    rows = q.shape[0]
    bias = bias_ref[0]
    total = jnp.zeros(kv.shape, F32)
    dq = []
    for g in range(group):
        both = jnp.concatenate([head_lanes(q, g, False), head_lanes(do, g, True)], axis=0)
        products = contract_last(kv, both)
        p = jnp.exp(products[:, :rows] + (bias - lse_ref[0, g]))
        dp = products[:, rows:]
        delta = jnp.sum(p * dp, axis=0, keepdims=True)
        ds = (p * (dp - delta)).astype(BF16)
        total = total + dot(jnp.concatenate([ds, p.astype(BF16)], axis=1), both)
        dq.append(dot(k_t, ds))
    dq.append(jnp.zeros(dq[0].shape, F32))
    dq_ref[...] = jnp.concatenate(dq, axis=0).T
    for i, ref in enumerate(dkv_refs):
        ref[...] = total[i * rows : (i + 1) * rows].astype(BF16)


def attention_specs(rows, keys, pieces):
    q = pl.BlockSpec((rows, 256), lambda s: (s, 0))
    bias = pl.BlockSpec((1, keys, rows), lambda s: (s, 0, 0))
    kv = [pl.BlockSpec((rows, 128), lambda s: (s, 0))] * pieces
    return q, bias, kv


def attention_forward(q, bias, kv, group, after):
    seqs, keys, rows = bias.shape
    q_spec, bias_spec, kv_specs = attention_specs(rows, keys, len(kv))
    work = seqs * group * keys * rows
    return pl.pallas_call(
        ordered(attention_forward_kernel, len(after)),
        grid=(seqs,),
        in_specs=[*[ANYWHERE] * len(after), q_spec, bias_spec, *kv_specs],
        out_specs=[
            *[pl.BlockSpec((1, rows // QUAD, group * 64), lambda s: (s, 0, 0))] * QUAD,
            pl.BlockSpec((1, group, 1, rows), lambda s: (s, 0, 0, 0)),
        ],
        out_shape=[
            *[shape((seqs, rows // QUAD, group * 64), BF16)] * QUAD,
            shape((seqs, group, 1, rows), F32),
        ],
        compiler_params=pltpu.CompilerParams(vmem_limit_bytes=VMEM_LIMIT),
        cost_estimate=cost(6 * work * 128, 4 * bias.size, work),
        name="attention_forward",
    )(*after, q, bias, *kv)


def attention_backward(q, bias, lse, do, kv, after=()):
    seqs, keys, rows = bias.shape
    group = lse.shape[1]
    q_spec, bias_spec, kv_specs = attention_specs(rows, keys, len(kv))
    work = seqs * group * keys * rows
    return pl.pallas_call(
        ordered(attention_backward_kernel, len(after)),
        grid=(seqs,),
        in_specs=[
            *[ANYWHERE] * len(after),
            q_spec,
            bias_spec,
            pl.BlockSpec((1, group, 1, rows), lambda s: (s, 0, 0, 0)),
            *[pl.BlockSpec((1, rows // QUAD, group * 64), lambda s: (s, 0, 0))] * QUAD,
            *kv_specs,
        ],
        out_specs=[q_spec, *kv_specs],
        out_shape=[shape(q.shape, F32)] + [shape(k.shape, BF16) for k in kv],
        compiler_params=pltpu.CompilerParams(vmem_limit_bytes=VMEM_LIMIT),
        cost_estimate=cost(10 * work * 128, 4 * bias.size, work),
        name="attention_backward",
    )(*after, q, bias, lse, *do, *kv)


def put_halves(refs, value):
    rows = refs[0].shape[0]
    for i, ref in enumerate(refs):
        ref[...] = value[i * rows : (i + 1) * rows].astype(ref.dtype)


def sum_halves(refs):
    own = jnp.concatenate([refs[0][...], refs[1][...]], axis=0).astype(F32)
    return own + jnp.concatenate([refs[2][...], refs[3][...]], axis=0).astype(F32)


def branch_kernel(ids_ref, *refs):
    pieces, w_ref, out_refs, stack_ref = refs[:QUAD], refs[QUAD], refs[QUAD + 1 : -1], refs[-1]
    m = ids_ref[0] % QUAD
    for j in range(QUAD):
        stack_ref[j] = pieces[j][...]
    attn = jnp.concatenate([stack_ref[m ^ k] for k in range(QUAD)], axis=1)
    put_halves(out_refs, contract_last(attn, w_ref[...]))


def middle_kernel(ids_ref, x_ref, *refs):
    branch_refs, (gain_ref, mid_ref, h2_ref, half_ref) = refs[:4], refs[4:]
    mid = x_ref[...].astype(F32) + sum_halves(branch_refs)
    mid_ref[...] = mid
    h2 = (mid * row_factor(mid) * row_of(gain_ref)).astype(BF16)
    h2_ref[...] = h2
    rows = half_ref.shape[0]
    half_ref[...] = jnp.where(ids_ref[1] == 0, h2[:rows], h2[rows:])


def hidden_terms(gate, up, da):
    sg = jax.nn.sigmoid(gate)
    silu = gate * sg
    act = (silu * up).astype(BF16)
    dgate = (da * up * (sg + silu * (1.0 - sg))).astype(BF16)
    dup = (da * silu).astype(BF16)
    return act, dgate, dup


def hidden_tile(hidden):
    return next(t for t in (1152, 384, 128, hidden) if hidden % t == 0)


def hidden_call(body, name, args, out_shape, scratch=(), matmuls=1, after=()):
    hidden = max(a.shape[-1] for a in args)
    tile = hidden_tile(hidden)

    def spec(a):
        if a.shape[-1] == hidden:
            return pl.BlockSpec((a.shape[0], tile), lambda i: (0, i))
        return pl.BlockSpec(a.shape, lambda i: (0, 0))

    rows, width = args[0].shape[0], 1536
    return pl.pallas_call(
        ordered(body, len(after)),
        grid=(hidden // tile,),
        in_specs=[ANYWHERE] * len(after) + [spec(a) for a in args],
        out_specs=[spec(o) for o in out_shape],
        out_shape=list(out_shape),
        scratch_shapes=list(scratch),
        compiler_params=pltpu.CompilerParams(vmem_limit_bytes=VMEM_LIMIT),
        cost_estimate=cost(
            4 * matmuls * rows * width * hidden,
            sum(a.size * a.dtype.itemsize for a in (*args, *out_shape)),
        ),
        name=name,
    )(*after, *args)


def accumulate(total_ref, out_refs, term):
    step = pl.program_id(0)

    @pl.when(step == 0)
    def _():
        total_ref[...] = term

    @pl.when(step > 0)
    def _():
        total_ref[...] += term

    @pl.when(step == pl.num_programs(0) - 1)
    def _():
        put_halves(out_refs, total_ref[...].T)


def hidden_grad_kernel(g_ref, wd_ref, da_ref):
    da_ref[...] = dot(g_ref[...], wd_ref[...])


def own_mlp_kernel(
    h2_ref, da_ref, wg_ref, wu_ref, dh_top_ref, dh_ref, act_ref, dgate_ref, dup_ref, total_ref
):
    wg, wu, h2 = wg_ref[...], wu_ref[...], h2_ref[...]
    act, dgate, dup = hidden_terms(dot(h2, wg), dot(h2, wu), da_ref[...])
    act_ref[...] = act
    dgate_ref[...] = dgate
    dup_ref[...] = dup
    accumulate(
        total_ref, (dh_top_ref, dh_ref), contract_last(wg, dgate) + contract_last(wu, dup)
    )


def down_kernel(act_ref, wd_ref, down_ref, total_ref):
    accumulate(total_ref, (down_ref,), contract_last(wd_ref[...], act_ref[...]))


def back_kernel(
    ids_ref, mid_ref, a_ref, b_ref, c_ref, d_ref, g_ref, gain_ref, w_ref, dx_ref, dy_ref, *refs
):
    half_ref, part_ref, do_refs = refs[0], refs[1], refs[2:]
    m = ids_ref[0] % QUAD
    stack_ref, do_refs = do_refs[-1], do_refs[:-1]
    mid = mid_ref[...]
    factor = row_factor(mid)
    dh2 = sum_halves((a_ref, b_ref, c_ref, d_ref))
    part_ref[...] = jnp.sum(dh2 * mid * factor, axis=0, keepdims=True)
    scaled = dh2 * row_of(gain_ref)
    inner = jnp.mean(mid * scaled, axis=-1, keepdims=True)
    dx = g_ref[...].astype(F32) + (factor * scaled - mid * (factor * factor * factor) * inner)
    dx_ref[...] = dx
    dy = dx.astype(BF16)
    dy_ref[...] = dy
    half = half_ref.shape[0]
    half_ref[...] = jnp.where(ids_ref[1] == 0, dy[:half], dy[half:])
    do = dot(dy, w_ref[...]).astype(BF16)
    columns = do.shape[1] // QUAD
    for k in range(QUAD):
        stack_ref[m ^ k] = do[:, k * columns : (k + 1) * columns]
    for j in range(QUAD):
        do_refs[j][...] = stack_ref[j]


def norm_rotate_back(grad, raw, gain, cos, sin, blocks):
    normed = grad * cos - partner(grad) * sin
    factor = lax.rsqrt(head_means(raw * raw, blocks) + EPSILON)
    scaled = normed * gain
    inner = head_means(raw * scaled, blocks)
    part = jnp.sum(normed * raw * factor, axis=0, keepdims=True)
    return factor * scaled - raw * (factor * factor * factor) * inner, part


def head_grad_kernel(ids_ref, dq_ref, raw_ref, h1_ref, *refs):
    attn_refs, dy_ref, mine, theirs, refs = refs[:4], refs[4], refs[5:8], refs[8:11], refs[11:]
    core = ids_ref[1]
    key_gain_ref, query_gain_ref, cos_ref, sin_ref, refs = *refs[:4], refs[4:]
    nz = (len(refs) - QUAD - 3) // 2
    dkv_refs, refs = refs[:nz], refs[nz:]
    part_ref, piece_refs, w_refs = refs[0], refs[1 : 1 + QUAD], refs[1 + QUAD : -2]
    total_ref, dy_all = refs[-2:]
    cos, sin, blocks = cos_ref[...], sin_ref[...], head_blocks()
    key_gain, query_gain = head_gain_rows(key_gain_ref, query_gain_ref)
    dkv = dkv_refs[0][...].astype(F32)
    for ref in dkv_refs[1:]:
        dkv = dkv + ref[...].astype(F32)
    scale = 64 ** (-0.5)
    low = []
    for c in range(3):
        lanes = slice(128 * c, 128 * (c + 1))
        given = dkv if c == 0 else dq_ref[:, 128 * (c - 1) : 128 * c] * scale
        gain = key_gain if c == 0 else query_gain
        grad, part = norm_rotate_back(given, raw_ref[:, lanes], gain, cos, sin, blocks)
        if c == 0:
            grad = jnp.where(lanes_of(grad) < 64, grad, dkv)
        part_ref[:, lanes] = part
        low.append(grad.astype(BF16))
    low = jnp.concatenate(low, axis=1)
    rows = low.shape[0]
    tokens = rows // (SEQS * QUAD)
    attn = []
    for seq in range(SEQS):
        for j in range(QUAD):
            begin = (seq * QUAD + j) * tokens
            piece_refs[j][seq * tokens : (seq + 1) * tokens] = low[begin : begin + tokens]
            if j == 0:
                dy_all[seq, j] = dy_ref[seq]
            attn.append(attn_refs[j][seq])
    for j in range(1, QUAD):
        dy_all[core, j] = mine[j - 1][...]
        dy_all[1 - core, j] = theirs[j - 1][...]
    columns = attn[0].shape[1]
    grad_wqkv = contract_first(h1_ref[...].reshape(rows, -1), low)
    grad_wo = contract_first(dy_all[...].reshape(rows, -1), jnp.concatenate(attn, axis=0))
    total_ref[...] = jnp.concatenate([grad_wqkv[:, : 128 + columns], grad_wo], axis=1)
    z = ids_ref[0] // QUAD
    owned = w_refs[0].shape[0]
    for step, ref in enumerate(w_refs):
        begin = pl.multiple_of(((z + nz - step) % nz) * owned, 8)
        ref[...] = total_ref[pl.ds(begin, owned), :].astype(BF16)


def spread_kernel(ids_ref, *refs):
    nz = len(refs) - QUAD - 1
    terms, (own_ref, *out_refs), total_ref = refs[:nz], refs[nz:-1], refs[-1]
    total = terms[0][...].astype(F32)
    for ref in terms[1:]:
        total = total + ref[...].astype(F32)
    total_ref[...] = total
    m = ids_ref[0] % QUAD
    rows = own_ref.shape[0]
    for j in range(QUAD):
        part = total_ref[pl.ds(pl.multiple_of((m ^ j) * rows, 8), rows), :]
        if j == 0:
            own_ref[...] = part
        else:
            out_refs[j - 1][...] = part.astype(BF16)


def assemble_kernel(ids_ref, own_ref, a_ref, b_ref, c_ref, wq_ref, wk_ref, wv_ref, wo_ref, stack_ref):
    m = ids_ref[0] % QUAD
    stack_ref[0] = own_ref[...]
    for j, ref in enumerate((a_ref, b_ref, c_ref)):
        stack_ref[j + 1] = ref[...].astype(F32)
    parts = [stack_ref[m ^ k] for k in range(QUAD)]
    columns = wq_ref.shape[1] // QUAD
    wk_ref[...] = jnp.concatenate([p[:, :64] for p in parts], axis=1)
    wv_ref[...] = jnp.concatenate([p[:, 64:128] for p in parts], axis=1)
    wq_ref[...] = jnp.concatenate([p[:, 128 : 128 + columns] for p in parts], axis=1)
    wo_ref[...] = jnp.concatenate([p[:, 128 + columns :] for p in parts], axis=1)


def input_grad_kernel(ids_ref, *refs):
    pieces, (x_ref, wq_ref, wk_ref, wv_ref, out_ref, part_ref, stack_ref) = refs[:QUAD], refs[QUAD:]
    m = ids_ref[0] % QUAD
    for j in range(QUAD):
        stack_ref[j] = pieces[j][...]
    parts = [stack_ref[m ^ k] for k in range(QUAD)]
    columns = wq_ref.shape[1] // QUAD
    dk = jnp.concatenate([p[:, :64] for p in parts], axis=1)
    dv = jnp.concatenate([p[:, 64:128] for p in parts], axis=1)
    dq = jnp.concatenate([p[:, 128 : 128 + columns] for p in parts], axis=1)
    total = (
        contract_last(dq, wq_ref[...])
        + contract_last(dk, wk_ref[...])
        + contract_last(dv, wv_ref[...])
    )
    out_ref[...] = total.astype(BF16)
    x = x_ref[...].astype(F32)
    part_ref[...] = jnp.sum(total * x * row_factor(x), axis=0, keepdims=True)


def tokens_kernel(x_ref, dx_ref, a_ref, b_ref, gain_ref, out_ref):
    x = x_ref[...].astype(F32)
    factor = row_factor(x)
    scaled = (a_ref[...].astype(F32) + b_ref[...].astype(F32)) * row_of(gain_ref)
    inner = jnp.mean(x * scaled, axis=-1, keepdims=True)
    back = factor * scaled - x * (factor * factor * factor) * inner
    out_ref[...] = (dx_ref[...] + back).astype(BF16)


def output_kernel(mid_ref, a_ref, b_ref, out_ref):
    out_ref[...] = (mid_ref[...] + (a_ref[...].astype(F32) + b_ref[...].astype(F32))).astype(BF16)


def bulk_mlp_kernel(ids_ref, *refs, pieces, row_tile, first):
    sides, refs = (refs[: pieces[0]], refs[pieces[0] : sum(pieces)]), refs[sum(pieces) :]
    act_ref, dgate_ref, dup_ref, wg_ref, wu_ref, wd_ref, refs = *refs[:6], refs[6:]
    if first:
        own_refs, other_ref, h2c_ref, gc_ref, h2_ref, g_ref, sems = refs[:3], *refs[3:]
    else:
        h2c_ref, gc_ref, own_refs, other_ref, h2_ref, g_ref, sems = *refs[:2], refs[2:5], *refs[5:]
    rows = act_ref.shape[0]
    tokens, width = h2_ref.shape
    own_rows = own_refs[0].shape[0]
    pair_rows = 2 * own_rows

    @pl.when(pl.program_id(0) == 0)
    def _():
        half = rows // 2
        places = pieces[1] // 2
        copies = []

        def copy_rows(source, skip, size, target, begin, sem):
            return pltpu.make_async_copy(
                source.at[pl.ds(skip, size)], target.at[pl.ds(begin, size)], sems.at[sem]
            )

        begin = 0
        for i, source in enumerate(sides[0]):
            skip = half if i in (0, 2) else 0
            copies.append(copy_rows(source, skip, source.shape[0] - skip, h2_ref, begin, i))
            begin += source.shape[0] - skip
        for copy in copies:
            copy.start()
        for core in range(2):

            @pl.when(ids_ref[1] == core)
            def _():
                own_y, other_y = sides[1][:places], sides[1][places : 2 * places]
                if core == 1:
                    own_y, other_y = other_y, own_y
                blocks = [*own_y[1:], *other_y]
                for i, source in enumerate(blocks):
                    for part in range(2):
                        to = (i + part * len(blocks)) * half
                        sem = len(sides[0]) + 2 * i + part
                        copy_rows(source, (core ^ part) * half, half, g_ref, to, sem).start()
                last = len(sides[0]) + 4 * places - 2
                copy_rows(sides[1][-1], 0, rows, g_ref, tokens - rows, last).start()

        for i in range(2 * (2 * places - 1)):
            copies.append(copy_rows(sides[1][0], 0, half, g_ref, 0, len(sides[0]) + i))
        last = len(sides[0]) + 4 * places - 2
        copies.append(copy_rows(sides[1][-1], 0, rows, g_ref, tokens - rows, last))
        if first:
            me = ids_ref[0]
            row = lax.broadcasted_iota(jnp.int32, (width, pair_rows), 0)
            col = lax.broadcasted_iota(jnp.int32, (width, pair_rows), 1)
            target = jnp.where(col < own_rows, me * own_rows + col, ((me ^ 1) - 1) * own_rows + col)
            chosen = jnp.where(row == target, 1.0, 0.0).astype(BF16)
        for copy in copies:
            copy.wait()
        if first:
            h2c_ref[...] = dot(h2_ref[...], chosen).T.astype(BF16)
            gc_ref[...] = dot(g_ref[...], chosen).T.astype(BF16)

    wg, wu, wd = wg_ref[...], wu_ref[...], wd_ref[...]
    last = slice(tokens - rows, tokens)
    totals = [
        dot(left[:, last], term[...])
        for left, term in ((h2c_ref, dgate_ref), (h2c_ref, dup_ref), (gc_ref, act_ref))
    ]
    for begin in range(0, tokens - rows, row_tile):
        part = slice(begin, min(begin + row_tile, tokens - rows))
        h2 = h2_ref[part]
        act, dgate, dup = hidden_terms(dot(h2, wg), dot(h2, wu), dot(g_ref[part], wd))
        h2c, gc = h2c_ref[:, part], gc_ref[:, part]
        terms = [dot(h2c, dgate), dot(h2c, dup), dot(gc, act)]
        totals = [a + b for a, b in zip(totals, terms)]
    for i, (own, total) in enumerate(zip(own_refs, totals)):
        own[...] = total[:own_rows]
        other_ref[i] = total[own_rows:].astype(BF16)


def bulk_mlp(ids, h2, g, own_terms, weights, chosen, own_rows, begin, end, tile, after):
    width = h2[0].shape[1]
    rows, hidden = own_terms[0].shape
    tokens = sum(piece.shape[0] for piece in h2) - rows
    out_hidden = min(end * tile, hidden) - begin * tile
    weight = pl.BlockSpec((width, tile), lambda i: (0, i + begin))
    term = pl.BlockSpec((rows, tile), lambda i: (0, i + begin))
    result = pl.BlockSpec((own_rows, tile), lambda i: (0, i))
    columns = pl.BlockSpec((2 * own_rows, tokens), lambda i: (0, 0))
    first = not chosen
    pieces = (len(h2), len(g))
    body = functools.partial(
        bulk_mlp_kernel, pieces=pieces, row_tile=min(tokens, 1024), first=first
    )
    return pl.pallas_call(
        ordered(body, len(after)),
        grid=(end - begin,),
        in_specs=[ANYWHERE] * len(after)
        + [SCALARS]
        + [ANYWHERE] * sum(pieces)
        + [term] * 3
        + [weight] * 3
        + [columns] * len(chosen),
        out_specs=[result] * 3
        + [pl.BlockSpec((3, own_rows, tile), lambda i: (0, 0, i))]
        + [columns] * (2 if first else 0),
        out_shape=[shape((own_rows, out_hidden), F32)] * 3
        + [shape((3, own_rows, out_hidden), BF16)]
        + [shape((2 * own_rows, tokens), BF16)] * (2 if first else 0),
        scratch_shapes=[pltpu.VMEM((tokens, width), BF16)] * 2 + [pltpu.SemaphoreType.DMA((len(h2) + 2 * len(g) - 3,))],
        compiler_params=pltpu.CompilerParams(vmem_limit_bytes=VMEM_LIMIT),
        cost_estimate=cost(
            6 * tokens * (width + 2 * own_rows) * out_hidden,
            6 * width * out_hidden + 4 * tokens * width,
            tokens * out_hidden,
            scale=1,
        ),
        name="bulk_mlp",
    )(*after, ids, *h2, *g, *own_terms, *weights, *chosen)


def finish_kernel(*refs):
    first, second, theirs, outs = refs[:3], refs[3:6], refs[6:8], refs[8:]
    cut = first[0].shape[1]
    for i in range(3):
        outs[i][:, :cut] = first[i][...] + theirs[0][i].astype(F32)
        outs[i][:, cut:] = second[i][...] + theirs[1][i].astype(F32)


def bulk_finish(first, second, theirs_first, theirs_second):
    rows, first_hidden = first[0].shape
    second_hidden = second[0].shape[1]
    hidden = first_hidden + second_hidden
    block = rows // 6 if rows % 96 == 0 else rows

    def spec(columns):
        return pl.BlockSpec((block, columns), lambda i: (i, 0))

    def theirs_spec(columns):
        return pl.BlockSpec((3, block, columns), lambda i: (0, i, 0))

    return pl.pallas_call(
        finish_kernel,
        grid=(rows // block,),
        in_specs=[spec(first_hidden)] * 3
        + [spec(second_hidden)] * 3
        + [theirs_spec(first_hidden), theirs_spec(second_hidden)],
        out_specs=[spec(hidden)] * 3,
        out_shape=[shape((rows, hidden), F32)] * 3,
        compiler_params=pltpu.CompilerParams(vmem_limit_bytes=VMEM_LIMIT),
        cost_estimate=cost(rows * hidden, 30 * rows * hidden),
        name="bulk_finish",
    )(*first, *second, theirs_first, theirs_second)


def gains_kernel(a_ref, b_ref, attn_ref, mlp_ref, query_ref, key_ref):
    total = a_ref[...] + b_ref[...]
    width = attn_ref.shape[0]
    attn_ref[...] = total[:width]
    mlp_ref[...] = total[width : 2 * width]
    heads = total[2 * width :]
    key_ref[...] = heads[:64]
    query_ref[...] = heads[128:192] + heads[192:256] + heads[256:320]


def shards(
    tokens,
    w_query,
    w_key,
    w_value,
    w_output,
    w_gate,
    w_up,
    w_down,
    attn_gain,
    mlp_gain,
    query_gain,
    key_gain,
    segments,
    positions,
    cotangent,
):
    count = lax.axis_size("ctx")
    me = lax.axis_index("ctx")
    core = lax.axis_index("tp")
    nz = count // QUAD
    m = me % QUAD
    head = query_gain.shape[0]
    rows, model = tokens.shape
    q_heads = w_query.shape[1] // head
    kv_heads = w_key.shape[1] // head
    group = q_heads // kv_heads
    pair = rows // SEQS
    quad_rows = QUAD * rows
    columns = group * head
    own_rows = model // count
    flips = [flip_pairs(count, j) for j in range(QUAD)]
    ids = jnp.stack([me, core]).astype(jnp.int32)

    def quad_exchange(pieces):
        return [pieces[0]] + [send(pieces[j], flips[j]) for j in range(1, QUAD)]

    own_tokens = tokens.reshape(SEQS, pair, model)
    half = lax.dynamic_index_in_dim(own_tokens, core, 0, keepdims=False)
    mine = [send(half, flips[j]) for j in range(1, QUAD)]
    theirs = [swap_cores(p) for p in mine]

    freqs = ROPE_BASE ** (-2.0 * np.arange(head // 2) / head)
    freqs = jnp.asarray(np.tile(freqs, 4)[None, :], F32)
    bias, angles = kernel_call(
        mask_kernel,
        "visible",
        (ids, freqs, segments.reshape(count, SEQS * pair)),
        [shape((SEQS, count * pair, QUAD * pair), F32), shape((quad_rows, 2 * head), F32)],
        scalars=True,
    )
    sign = jnp.asarray(np.tile(np.repeat([-1.0, 1.0], head // 2), 2)[None, :], F32)
    cos, sin = jnp.cos(angles), jnp.sin(angles) * sign
    w_head = jnp.concatenate(
        [
            lax.dynamic_slice_in_dim(w_key, m * head, head, 1),
            lax.dynamic_slice_in_dim(w_value, m * head, head, 1),
            lax.dynamic_slice_in_dim(w_query, m * columns, columns, 1),
            jnp.zeros((model, head), BF16),
        ],
        axis=1,
    )
    h1, raw, q, kv_own, g_copy = kernel_call(
        qkv_kernel,
        "query_key_value",
        (
            ids,
            own_tokens,
            *mine,
            *theirs,
            attn_gain,
            w_head,
            key_gain,
            query_gain,
            cos,
            sin,
            cotangent,
        ),
        [
            shape((SEQS, QUAD, pair, model), BF16),
            shape((quad_rows, 6 * head), F32),
            shape((quad_rows, 4 * head), BF16),
            shape((quad_rows, 2 * head), BF16),
            shape((rows, model), BF16),
        ],
        flops=2 * quad_rows * model * 6 * head,
        scalars=True,
    )
    kv = [kv_own] + [send(kv_own, shift_pairs(count, s)) for s in range(1, nz)]
    hidden = w_down.shape[1]
    (da,) = hidden_call(
        hidden_grad_kernel,
        "hidden_grad",
        (cotangent, w_down),
        [shape((rows, hidden), F32)],
        after=(kv_own,),
    )
    g_blocks = [lax.ppermute(g_copy, ("ctx", "tp"), core_pairs(count))]

    def next_cotangents(after):
        g_blocks[-1] = touch(g_blocks[-1], after)
        g_blocks.append(send(g_blocks[-1], shift_pairs(count, 1)))

    *attn, lse = attention_forward(q, bias, kv, group, (da,))
    next_cotangents((lse,))
    attn_pieces = quad_exchange([a.reshape(rows, columns) for a in attn])
    branch = kernel_call(
        branch_kernel,
        "branch",
        (ids, *attn_pieces, w_output),
        [shape((rows // 2, model), BF16)] * 2,
        flops=2 * rows * model * w_output.shape[1],
        scalars=True,
        scratch=[pltpu.VMEM((QUAD, rows, columns), BF16)],
    )
    middle, h2, h2_half = kernel_call(
        middle_kernel,
        "middle",
        (ids, tokens, *branch, *[swap_cores(b) for b in branch], mlp_gain),
        [shape((rows, model), F32), shape((rows, model), BF16), shape((rows // 2, model), BF16)],
        scalars=True,
    )
    h2_pieces = gather_column(h2_half, count)

    g_first = swap_cores(g_blocks[0])
    *dh2, act, dgate, dup = hidden_call(
        own_mlp_kernel,
        "own_mlp",
        (h2, da, w_gate, w_up),
        [shape((rows // 2, model), BF16)] * 2 + [shape((rows, hidden), BF16)] * 3,
        scratch=[pltpu.VMEM((model, rows), F32)],
        matmuls=4,
        after=(g_first,),
    )
    h2_packed = pack(h2_pieces, (act,))
    g_blocks[1] = touch(g_blocks[1], (h2,))
    g_second = swap_cores(g_blocks[1])
    for _ in range(2, nz - 1):
        next_cotangents((act,))
    grad_middle, dy, dy_half, mlp_gain_part, *do = kernel_call(
        back_kernel,
        "back",
        (ids, middle, *dh2, *[swap_cores(d) for d in dh2], cotangent, mlp_gain, w_output),
        [
            shape((rows, model), F32),
            shape((rows, model), BF16),
            shape((rows // 2, model), BF16),
            shape((1, model), F32),
            *[shape((rows, columns), BF16)] * QUAD,
        ],
        flops=2 * rows * model * w_output.shape[1],
        scalars=True,
        scratch=[pltpu.VMEM((QUAD, rows, columns), BF16)],
        after=(h2_packed, g_second),
    )
    do_pieces = [d.reshape(SEQS, pair, columns) for d in quad_exchange(do)]
    dy_half = touch(dy_half, do_pieces[1:])
    dy_mine = [send(dy_half, flips[j]) for j in range(1, QUAD)]
    dy_theirs = [swap_cores(p) for p in dy_mine]
    dy_pieces = (dy.reshape(SEQS, pair, model), *dy_mine, *dy_theirs)
    dq, *dkv = attention_backward(
        q, bias, lse, do_pieces, kv, (g_blocks[-1],)
    )
    next_cotangents((dq,))
    g_swapped = [g_first, g_second] + [swap_cores(g) for g in g_blocks[2:-1]]
    h2_column = touch(h2_packed, (dq, *dy_mine))
    h2_other = send(h2_column, flips[2])
    (down,) = hidden_call(
        down_kernel,
        "down",
        (act, w_down),
        [shape((rows, model), BF16)],
        scratch=[pltpu.VMEM((model, rows), F32)],
        after=(dq,),
    )
    dkv = [dkv[0]] + [send(dkv[s], shift_pairs(count, nz - s)) for s in range(1, nz)]


    z_rows = model // nz
    head_part, *rest = kernel_call(
        head_grad_kernel,
        "head_grad",
        (ids, dq, raw, h1, *attn, *dy_pieces, key_gain, query_gain, cos, sin, *dkv),
        [
            shape((1, 6 * head), F32),
            *[shape((rows, 6 * head), BF16)] * QUAD,
            *[shape((z_rows, 8 * head), BF16)] * nz,
        ],
        flops=2 * quad_rows * model * 9 * head,
        scalars=True,
        scratch=[
            pltpu.VMEM((model, 8 * head), F32),
            pltpu.VMEM((SEQS, QUAD, pair, model), BF16),
        ],
        after=(down,),
    )
    grad_pieces, w_parts = quad_exchange(rest[:QUAD]), rest[QUAD:]
    w_parts = [w_parts[0]] + [send(w_parts[s], shift_pairs(count, nz - s)) for s in range(1, nz)]
    h2_column = touch(h2_column, (h2_other, head_part))
    h2_other = touch(h2_other, (h2_column,))
    h2_rows = (h2_column, h2_other, swap_cores(h2_column), swap_cores(h2_other), h2)
    g_rows = (*g_blocks, *g_swapped, swap_cores(g_blocks[-1]), cotangent)

    tile = 512
    tiles = pl.cdiv(hidden, tile)
    cut = (tiles + 1) // 2

    def bulk_part(chosen, begin, end, after):
        result = bulk_mlp(
            ids,
            h2_rows,
            g_rows,
            (act, dgate, dup),
            (w_gate, w_up, w_down),
            chosen,
            own_rows,
            begin,
            end,
            tile,
            after,
        )
        return result[:3], result[3], result[4:]

    bulk_first = bulk_part((), 0, cut, (head_part,))
    theirs_first = send(touch(bulk_first[1], grad_pieces[1:]), flips[1])
    bulk_second = bulk_part(bulk_first[2], cut, tiles, ())
    theirs_second = send(bulk_second[1], flips[1])
    after_bulk = (bulk_second[0][0],)
    down = touch(down, after_bulk)
    (output,) = kernel_call(
        output_kernel, "output", (middle, down, swap_cores(down)), [shape((rows, model), BF16)]
    )
    dh1, attn_gain_part = kernel_call(
        input_grad_kernel,
        "input_grad",
        (ids, *grad_pieces, tokens, w_query, w_key, w_value),
        [shape((rows, model), BF16), shape((1, model), F32)],
        flops=2 * rows * model * (q_heads + 2 * kv_heads) * head,
        scalars=True,
        scratch=[pltpu.VMEM((QUAD, rows, 6 * head), BF16)],
        after=after_bulk,
    )
    (grad_tokens,) = kernel_call(
        tokens_kernel,
        "tokens_grad",
        (tokens, grad_middle, dh1, swap_cores(dh1), attn_gain),
        [shape((rows, model), BF16)],
    )
    spread = kernel_call(
        spread_kernel,
        "spread",
        (ids, *w_parts),
        [shape((own_rows, 8 * head), F32)] + [shape((own_rows, 8 * head), BF16)] * (QUAD - 1),
        scalars=True,
        scratch=[pltpu.VMEM((z_rows, 8 * head), F32)],
        after=after_bulk,
    )
    gains = jnp.concatenate([attn_gain_part, 0.5 * mlp_gain_part, head_part], axis=1)[0]
    gains = gains + swap_cores(gains)
    gains = gains + send(gains, flips[2])
    fillers = [spread[0], output]
    for i in range(2, count.bit_length() - 1):
        gains = touch(gains, (fillers[min(i, 3) - 2],))
        gains = gains + send(gains, flip_pairs(count, 1 << i))
    gains = touch(gains, (grad_tokens,))
    grad_attn_gain, grad_mlp_gain, grad_query_gain, grad_key_gain = kernel_call(
        gains_kernel,
        "gains",
        (gains, send(gains, flips[1])),
        [shape((model,), F32)] * 2 + [shape((head,), F32)] * 2,
    )
    spread = quad_exchange(spread)
    grad_wq, grad_wk, grad_wv, grad_wo = kernel_call(
        assemble_kernel,
        "assemble",
        (ids, *spread),
        [
            shape((own_rows, q_heads * head), F32),
            shape((own_rows, kv_heads * head), F32),
            shape((own_rows, kv_heads * head), F32),
            shape((own_rows, q_heads * head), F32),
        ],
        scalars=True,
        scratch=[pltpu.VMEM((QUAD, own_rows, 8 * head), F32)],
    )

    mlp_grads = bulk_finish(bulk_first[0], bulk_second[0], theirs_first, theirs_second)
    return (
        output,
        grad_tokens,
        grad_wq,
        grad_wk,
        grad_wv,
        grad_wo,
        mlp_grads[0],
        mlp_grads[1],
        mlp_grads[2],
        grad_attn_gain,
        grad_mlp_gain,
        grad_query_gain,
        grad_key_gain,
    )


def solution(mesh):
    rows = P("ctx", None)
    columns = P(None, "tp")
    both = P("ctx", "tp")
    in_specs = (rows,) + (columns,) * 7 + (P(),) * 5 + (P("ctx"), rows)
    out_specs = (rows, rows) + (both,) * 7 + (P(),) * 4
    return jax.shard_map(shards, mesh=mesh, in_specs=in_specs, out_specs=out_specs, check_vma=False)
```
